256 devices in a mesh: leaf: 64 (over z, y, core), front: 4 (over x).
Axes of the slice: x: 4, y: 4, z: 8, core: 2. Of those that a mesh axis runs over, the one named last changes fastest.
Arguments:
- front: bfloat16 [64, 2, 4, 256, 2048], P('leaf', None, 'front')
- pivot_tiles: int32 [64], P('leaf'), may hold values from 1 to 2, as said below
- send_table: int32 [64, 4, 3, 64], P('leaf', 'front'), may hold values from -1 to 15, as said below
Outputs:
- factor: float32 [64, 2, 4, 256, 512], P('leaf', None, 'front')
- ancestor: float32 [64, 4, 16, 256, 256], P('leaf', 'front')
The draws below stay inside these ranges and needn't reach their ends.
Inputs may be any that keep to these rules, and one draw needn't show every extreme that they name: Front s eliminates its first pivot_tiles[s] tile columns; some front has 2 and some has 1. `send_table`: slot p of device (s, g) goes to leaf p. A slot is either unused (all three entries -1) or names a local tile row r and tile column j whose global tile row r * 4 + g and column j are both at least pivot_tiles[s], with an ancestor slot; every such tile of the device is named by exactly one slot. The 1 slots to leaf 0 are used on every device.
All inputs are finite; a program needn't handle non-finite values.
Results may differ from the reference program's by a relative error of at most 0.0003.
Values sent between devices are 32-bit elements; how exact they have to be, the bound alone decides.
No kernel may reach another device: no remote copies, remote signals or barrier semaphores. Data moves between devices by JAX's collectives and lax.ppermute only.
A program may use at most 128 MiB of HBM per device.

```python
import math
import jax
import jax.numpy as jnp
from jax import lax

TILE = 256
RT = 2
PT = 2
ASLOT = 16
LEAVES = 64
GRID = 4
NT = 8
NF = 2048
CAP = 1
SLOTS = 64


def pivot_counts(key):
    key = jax.random.fold_in(key, 11)
    draws = jax.random.randint(key, (LEAVES,), 0, 8)
    counts = jnp.where(draws < 5, 1, jnp.where(draws < 7, 2, PT))
    picks = jax.random.permutation(jax.random.fold_in(key, 1), LEAVES)
    counts = counts.at[picks[0]].set(PT).at[picks[1]].set(1)
    return counts.astype(jnp.int32)


def draw_pivot_tiles(key, part):
    return pivot_counts(key)


def draw_send_table(key, part):
    pivots = pivot_counts(key)
    key = jax.random.fold_in(key, 23)
    local = RT * NT
    row_tile = jnp.arange(local, dtype=jnp.int32) // NT
    col_tile = jnp.arange(local, dtype=jnp.int32) % NT

    def one_device(leaf, place):
        inner = jax.random.fold_in(jax.random.fold_in(key, leaf), place)
        needed = pivots[leaf]
        live = (row_tile * GRID + place >= needed) & (col_tile >= needed)
        shuffle = jax.random.permutation(jax.random.fold_in(inner, 1), local)
        score = jnp.where(live, 0, local) + shuffle
        order = jnp.argsort(score)
        count = jnp.sum(live.astype(jnp.int32))
        others = jax.random.permutation(jax.random.fold_in(inner, 2), SLOTS - CAP) + CAP
        rank = jnp.concatenate([jnp.arange(CAP, dtype=jnp.int32), others.astype(jnp.int32)])
        used = rank < count
        chosen = order[jnp.clip(rank, 0, local - 1)]
        rows = jnp.where(used, row_tile[chosen], -1)
        cols = jnp.where(used, col_tile[chosen], -1)
        targets = jnp.where(used, jax.random.randint(jax.random.fold_in(inner, 3), (SLOTS,), 0, ASLOT), -1)
        return jnp.stack([rows, cols, targets]).astype(jnp.int32)

    def one_leaf(leaf):
        return jax.vmap(lambda place: one_device(leaf, place))(jnp.arange(GRID, dtype=jnp.int32))
    return jax.vmap(one_leaf)(jnp.arange(LEAVES, dtype=jnp.int32))


def draw_front(key, part):
    key = jax.random.fold_in(key, 5)
    reach = (60.0 / (8.0 * math.pi * NF)) ** (1.0 / 3.0)

    def one_front(number):
        inner = jax.random.fold_in(key, number)
        spots = jax.random.uniform(inner, (3, NF), jnp.float32)
        squared = jnp.zeros((NF, NF), jnp.float32)
        for axis_number in range(3):
            apart = spots[axis_number][:, None] - spots[axis_number][None, :]
            squared = squared + apart * apart
        coupling = 0.5 * jnp.exp(-jnp.sqrt(squared) / reach)
        nugget = jax.random.uniform(jax.random.fold_in(inner, 1), (NF,), jnp.float32, 0.3, 0.6)
        matrix = coupling + jnp.diag(nugget)
        return matrix.reshape(RT, GRID, TILE, NF).astype(jnp.bfloat16)
    return lax.map(one_front, jnp.arange(LEAVES, dtype=jnp.int32))


def setup_inputs(seed: int = 0) -> dict:
    key_of = jax.random.split(jax.random.key(seed), 4)
    front = draw_front(jax.random.fold_in(key_of[3], 71), 0)
    pivot_tiles = draw_pivot_tiles(jax.random.fold_in(key_of[3], 71), 0)
    send_table = draw_send_table(jax.random.fold_in(key_of[3], 71), 0)
    return dict(front=front, pivot_tiles=pivot_tiles, send_table=send_table)


def front_factor(matrix, pivots):
    work = matrix.astype(jnp.float32)
    tile_of_row = jnp.arange(NF, dtype=jnp.int32) // TILE
    columns = []
    for panel in range(PT):
        left = panel * TILE
        panel_rows = work[:, left:left + TILE]
        factor_tile = jnp.linalg.cholesky(panel_rows[left:left + TILE])
        solved = lax.linalg.triangular_solve(factor_tile, panel_rows, left_side=False, lower=True, transpose_a=True)
        keep = (tile_of_row >= panel) & (panel < pivots)
        solved = jnp.where(keep[:, None], solved, 0.0)
        work = work - jnp.dot(solved, solved.T, precision=lax.Precision.HIGHEST)
        columns.append(solved)
    return (jnp.concatenate(columns, axis=1), work)

def reference(front, pivot_tiles, send_table):
    fronts = front.reshape(LEAVES, NF, NF)
    places = jnp.arange(GRID, dtype=jnp.int32)
    owners = jnp.arange(SLOTS, dtype=jnp.int32) // CAP

    def visit(ancestor, item):
        matrix, pivots, table = item
        factor, work = front_factor(matrix, pivots)
        tiles = work.reshape(NT, TILE, NT, TILE).transpose(0, 2, 1, 3)
        live = table[:, 0] >= 0
        rows = jnp.clip(table[:, 0], 0, RT - 1) * GRID + places[:, None]
        cols = jnp.clip(table[:, 1], 0, NT - 1)
        picked = tiles[rows, cols]
        picked = jnp.where(live[:, :, None, None], picked, 0.0)
        targets = jnp.where(live, table[:, 2], ASLOT)
        ancestor = ancestor.at[owners[None, :], places[:, None], targets].add(picked, mode='drop')
        return (ancestor, factor.reshape(RT, GRID, TILE, PT * TILE))
    start = jnp.zeros((LEAVES, GRID, ASLOT, TILE, TILE), jnp.float32)
    ancestor, factor = lax.scan(visit, start, (fronts, pivot_tiles, send_table))
    return (factor, ancestor)
```

```python
import functools

import jax
import jax.numpy as jnp
from jax import lax
from jax.experimental import pallas as pl
from jax.experimental.pallas import tpu as pltpu
from jax.sharding import PartitionSpec as P

PT = 2
ASLOT = 16
B = 64
T = 256
F32 = jnp.float32
BF16 = jnp.bfloat16
HIGHEST = lax.Precision.HIGHEST
VMEM = pl.BlockSpec(memory_space=pltpu.VMEM)
SMEM = pl.BlockSpec(memory_space=pltpu.SMEM)
ANY = pl.BlockSpec(memory_space=pl.ANY)
NN = (((1,), (0,)), ((), ()))
NT = (((1,), (1,)), ((), ()))
TN = (((0,), (0,)), ((), ()))


def dot(a, b, dims):
    return lax.dot_general(a, b, dims, precision=HIGHEST, preferred_element_type=F32)


def dot1(a, b, dims):
    return lax.dot_general(a, b, dims, preferred_element_type=F32)


def split(x):
    high = x.astype(BF16)
    return high, (x - high.astype(F32)).astype(BF16)


def split3(x):
    high = x.astype(BF16)
    rest = x - high.astype(F32)
    mid = rest.astype(BF16)
    return high, mid, (rest - mid.astype(F32)).astype(BF16)


def dot3(a, b, dims):
    ah, al = a
    bh, bl = b
    return dot1(ah, bh, dims) + (dot1(ah, bl, dims) + dot1(al, bh, dims))


def factor64(groups, f_ref):
    sub = lax.broadcasted_iota(jnp.int32, (8, 128), 0)

    def body(it, gs):
        cols = [[jnp.broadcast_to(g[:, t:t + 1], (8, 128)) for t in range(8)] for g in gs]
        rows = [jnp.broadcast_to(gs[0][t:t + 1, :], (8, 128)) for t in range(8)]
        s = [[jnp.broadcast_to(cols[0][t][u:u + 1, :], (8, 128)) if u >= t else None for t in range(8)] for u in range(8)]
        inv = [None] * 8
        for t in range(8):
            inv[t] = 1.0 / s[t][t]
            for u in range(t + 1, 8):
                low = s[u][t] * inv[t]
                for v in range(u, 8):
                    s[v][u] = s[v][u] - low * s[v][t]
                rows[u] = rows[u] - low * rows[t]
                for g in range(1, 8):
                    cols[g][u] = cols[g][u] - low * cols[g][t]
        done = jnp.zeros((8, 128), F32)
        for t in range(8):
            done = jnp.where(sub == t, rows[t] * lax.rsqrt(s[t][t]), done)
        f_ref[pl.ds(pl.multiple_of(it * 8, 8), 8), :] = pltpu.roll(done, it * 8, 1)
        scaled = [rows[t] * inv[t] for t in range(8)]
        left = []
        for g in range(1, 8):
            piece = gs[g]
            for t in range(8):
                piece = piece - cols[g][t] * scaled[t]
            left.append(pltpu.roll(piece, 120, 1))
        left.append(gs[0])
        return tuple(left)

    lax.fori_loop(0, 8, body, tuple(groups))


def factor256(x_ref, f_ref):
    lane = lax.broadcasted_iota(jnp.int32, (B, 128), 1)
    row = lax.broadcasted_iota(jnp.int32, (B, 128), 0)
    ident = (lane - B == row).astype(F32)
    col = lax.broadcasted_iota(jnp.int32, (B, T), 1)
    wide_row = lax.broadcasted_iota(jnp.int32, (B, T), 0)
    for k in range(T // B):
        lo = k * B
        strip = x_ref[lo:lo + B, :]
        block = strip[:, (k // 2) * 128:(k // 2) * 128 + 128]
        if k % 2:
            block = pltpu.roll(block, B, 1)
        both = jnp.where(lane < B, block, ident)
        factor64([both[8 * g:8 * g + 8, :] for g in range(8)], f_ref)
        block_inv = f_ref[...][:, B:]
        inside = (col >= lo) & (col < lo + B)
        strip = jnp.where(inside, (col - lo == wide_row).astype(F32), strip)
        out = dot(block_inv, strip, NN)
        x_ref[lo:lo + B, :] = jnp.where(col < lo + B, out, 0.0)
        if lo + B < T:
            rest = T - lo - B
            rest_col = lax.broadcasted_iota(jnp.int32, (rest, T), 1)
            old = x_ref[lo + B:, :]
            old = jnp.where((rest_col >= lo) & (rest_col < lo + B), 0.0, old)
            x_ref[lo + B:, :] = old - dot(out[:, lo + B:], out, TN)


def first_kernel(w00_ref, inv0_ref, f_ref):
    inv0_ref[...] = w00_ref[...]
    factor256(inv0_ref, f_ref)


def second_kernel(piv_ref, inv0_ref, w10_ref, w11_ref, l10_ref, inv1_ref, f_ref):
    l10 = dot(w10_ref[...], inv0_ref[...], NT)
    l10_ref[...] = l10
    inv1_ref[...] = jnp.zeros((T, T), F32)

    @pl.when(piv_ref[0] >= 2)
    def _():
        inv1_ref[...] = w11_ref[...] - dot(l10, l10, NT)
        factor256(inv1_ref, f_ref)


def panel_kernel(place_ref, slot_ref, inv0_ref, l10_ref, inv1_ref, front_ref, *refs):
    pieces = refs[:12]
    factor_ref, out_ref, yh_ref, yl_ref, tile_ref, sem = refs[12:]
    place = place_ref[0]
    a0 = split3(inv0_ref[...])
    low = split(l10_ref[...])
    inv1 = inv1_ref[...]
    for q in range(4):
        for r in range(2):
            if q == 0:
                p0 = front_ref[0, r, 0, :, 0:T]
                p1 = front_ref[0, r, 0, :, T:2 * T].astype(F32)
            else:
                p0 = pieces[(q - 1) * 4 + r * 2][...].astype(BF16)
                p1 = pieces[(q - 1) * 4 + r * 2 + 1][...]
            y0 = dot1(p0, a0[0], NT) + (dot1(p0, a0[1], NT) + dot1(p0, a0[2], NT))
            y0h, y0l = split(y0)
            p1 = p1 - dot3((y0h, y0l), low, NT)
            y1 = dot(p1, inv1, NT)
            if r == 0:
                owner = lax.rem(place + q, 4)
                y1 = jnp.where(owner > 0, y1, 0.0)
            y1h, y1l = split(y1)
            n = q * 2 + r
            yh_ref[n, :, 0:T] = y0h
            yl_ref[n, :, 0:T] = y0l
            yh_ref[n, :, T:2 * T] = y1h
            yl_ref[n, :, T:2 * T] = y1l
            if q == 0:
                factor_ref[0, r, 0, :, 0:T] = y0
                factor_ref[0, r, 0, :, T:2 * T] = y1
    copies = []
    for r in range(2):
        for n in range(8):
            column = lax.rem(place + n // 2, 4) + 4 * (n % 2)
            start = pl.multiple_of(column * T, T)
            tile = front_ref[0, r, 0, :, pl.ds(start, T)].astype(F32)
            own = (yh_ref[r], yl_ref[r])
            other = (yh_ref[n], yl_ref[n])
            tile_ref[r * 8 + n] = tile - dot3(own, other, NT)
            slot = slot_ref[r * 8 + column]
            copy = pltpu.make_async_copy(tile_ref.at[r * 8 + n], out_ref.at[jnp.maximum(slot, 0)], sem.at[r * 8 + n])

            @pl.when(slot >= 0)
            def _():
                copy.start()
            copies.append((slot, copy))
    for slot, copy in copies:
        @pl.when(slot >= 0)
        def _():
            copy.wait()


def add_kernel(target_ref, arrived_ref, out_ref):
    step = pl.program_id(0)

    @pl.when(step == 0)
    def _():
        out_ref[...] = jnp.zeros_like(out_ref)

    for i in range(4):
        target = target_ref[step * 4 + i]

        @pl.when(target >= 0)
        def _():
            out_ref[target] += arrived_ref[i]


def local(front, pivot_tiles, send_table):
    place = lax.axis_index("front").astype(jnp.int32)
    up = [(i, (i + 1) % 4) for i in range(4)]
    down = [(i, (i - 1) % 4) for i in range(4)]
    own = [[front[0, r, 0, :, k * T:k * T + T].astype(F32) for k in range(2)] for r in range(2)]
    from_left = [[None, None], [None, None]]
    from_right = [[None, None], [None, None]]
    from_far = [[None, None], [None, None]]
    for r in range(2):
        for k in range(2):
            from_left[r][k] = lax.ppermute(own[r][k], "front", up)
            from_right[r][k] = lax.ppermute(own[r][k], "front", down)
            if k == 0:
                from_far[r][k] = lax.ppermute(from_left[r][k], "front", up)
            else:
                from_far[r][k] = lax.ppermute(from_right[r][k], "front", down)
    by_q = [own, from_right, from_far, from_left]

    def of_owner(owner, r, k):
        q = lax.rem(owner - place + 4, 4)
        out = by_q[0][r][k]
        for i in range(1, 4):
            out = jnp.where(q == i, by_q[i][r][k], out)
        return out

    inv0 = pl.pallas_call(
        first_kernel,
        out_shape=jax.ShapeDtypeStruct((T, T), F32),
        in_specs=[VMEM],
        out_specs=VMEM,
        scratch_shapes=[pltpu.VMEM((B, 128), F32)],
        compiler_params=pltpu.CompilerParams(vmem_limit_bytes=16 << 20),
        name="first",
    )(of_owner(0, 0, 0))
    l10, inv1 = pl.pallas_call(
        second_kernel,
        out_shape=(jax.ShapeDtypeStruct((T, T), F32),) * 2,
        in_specs=[SMEM, VMEM, VMEM, VMEM],
        out_specs=(VMEM, VMEM),
        scratch_shapes=[pltpu.VMEM((B, 128), F32)],
        compiler_params=pltpu.CompilerParams(vmem_limit_bytes=16 << 20),
        name="second",
    )(pivot_tiles, inv0, of_owner(1, 0, 0), of_owner(1, 0, 1))

    table = send_table[0, 0]
    where = jnp.where(table[0] >= 0, table[0] * 8 + table[1], -1)
    ids = jnp.arange(64, dtype=jnp.int32)
    slots = jnp.max(jnp.where(where[None, :] == jnp.arange(16, dtype=jnp.int32)[:, None], ids[None, :], -1), axis=1)
    received = [by_q[q][r][k] for q in range(1, 4) for r in range(2) for k in range(2)]
    factor, outgoing = pl.pallas_call(
        panel_kernel,
        out_shape=(jax.ShapeDtypeStruct((1, 2, 1, T, 2 * T), F32), jax.ShapeDtypeStruct((64, T, T), F32)),
        in_specs=[SMEM, SMEM] + [VMEM] * 16,
        out_specs=(VMEM, ANY),
        scratch_shapes=[
            pltpu.VMEM((8, T, 2 * T), BF16),
            pltpu.VMEM((8, T, 2 * T), BF16),
            pltpu.VMEM((16, T, T), F32),
            pltpu.SemaphoreType.DMA((16,)),
        ],
        compiler_params=pltpu.CompilerParams(vmem_limit_bytes=40 << 20),
        name="panel",
    )(place.reshape(1), slots, inv0, l10, inv1, front, *received)
    arrived = lax.all_to_all(outgoing, "leaf", split_axis=0, concat_axis=0, tiled=True)
    targets = lax.all_to_all(table[2], "leaf", split_axis=0, concat_axis=0, tiled=True)
    ancestor = pl.pallas_call(
        add_kernel,
        out_shape=jax.ShapeDtypeStruct((ASLOT, T, T), F32),
        grid=(16,),
        in_specs=[SMEM, pl.BlockSpec((4, T, T), lambda i: (i, 0, 0))],
        out_specs=pl.BlockSpec((ASLOT, T, T), lambda i: (0, 0, 0)),
        compiler_params=pltpu.CompilerParams(vmem_limit_bytes=32 << 20),
        name="add",
    )(targets, arrived)
    return (factor, ancestor.reshape(1, 1, ASLOT, T, T))


def solution(mesh):
    in_specs = (P("leaf", None, "front", None, None), P("leaf"), P("leaf", "front", None, None))
    out_specs = (P("leaf", None, "front", None, None), P("leaf", "front", None, None, None))
    return jax.shard_map(local, mesh=mesh, in_specs=in_specs, out_specs=out_specs, check_vma=False)
```

```python
import functools

import jax
import jax.numpy as jnp
from jax import lax
from jax.experimental import pallas as pl
from jax.experimental.pallas import tpu as pltpu
from jax.sharding import PartitionSpec as P

PT = 2
ASLOT = 16
TILES = 14
CZ = (18, 14, 11, 8)
CY = ((6, 5), (8, 5))
NEAR = 1
B = 64
T = 256
F32 = jnp.float32
BF16 = jnp.bfloat16
HIGHEST = lax.Precision.HIGHEST
VMEM = pl.BlockSpec(memory_space=pltpu.VMEM)
SMEM = pl.BlockSpec(memory_space=pltpu.SMEM)
ANY = pl.BlockSpec(memory_space=pl.ANY)
NN = (((1,), (0,)), ((), ()))
NT = (((1,), (1,)), ((), ()))
TN = (((0,), (0,)), ((), ()))


def dot(a, b, dims):
    return lax.dot_general(a, b, dims, precision=HIGHEST, preferred_element_type=F32)


def dot1(a, b, dims):
    return lax.dot_general(a, b, dims, preferred_element_type=F32)


def split(x):
    high = x.astype(BF16)
    return high, (x - high.astype(F32)).astype(BF16)


def split3(x):
    high = x.astype(BF16)
    rest = x - high.astype(F32)
    mid = rest.astype(BF16)
    return high, mid, (rest - mid.astype(F32)).astype(BF16)


def dot3(a, b, dims):
    ah, al = a
    bh, bl = b
    return dot1(ah, bh, dims) + (dot1(ah, bl, dims) + dot1(al, bh, dims))


def factor64(groups, f_ref):
    sub = lax.broadcasted_iota(jnp.int32, (8, 128), 0)

    def body(it, gs):
        cols = [[jnp.broadcast_to(g[:, t:t + 1], (8, 128)) for t in range(8)] for g in gs]
        rows = [jnp.broadcast_to(gs[0][t:t + 1, :], (8, 128)) for t in range(8)]
        s = [[jnp.broadcast_to(cols[0][t][u:u + 1, :], (8, 128)) if u >= t else None for t in range(8)] for u in range(8)]
        inv = [None] * 8
        for t in range(8):
            inv[t] = 1.0 / s[t][t]
            for u in range(t + 1, 8):
                low = s[u][t] * inv[t]
                for v in range(u, 8):
                    s[v][u] = s[v][u] - low * s[v][t]
                rows[u] = rows[u] - low * rows[t]
                for g in range(1, 8):
                    cols[g][u] = cols[g][u] - low * cols[g][t]
        done = jnp.zeros((8, 128), F32)
        for t in range(8):
            done = jnp.where(sub == t, rows[t] * lax.rsqrt(s[t][t]), done)
        f_ref[pl.ds(pl.multiple_of(it * 8, 8), 8), :] = pltpu.roll(done, it * 8, 1)
        scaled = [rows[t] * inv[t] for t in range(8)]
        left = []
        for g in range(1, 8):
            piece = gs[g]
            for t in range(8):
                piece = piece - cols[g][t] * scaled[t]
            left.append(pltpu.roll(piece, 120, 1))
        left.append(gs[0])
        return tuple(left)

    lax.fori_loop(0, 8, body, tuple(groups))


def factor256(x_ref, f_ref):
    lane = lax.broadcasted_iota(jnp.int32, (B, 128), 1)
    row = lax.broadcasted_iota(jnp.int32, (B, 128), 0)
    ident = (lane - B == row).astype(F32)
    col = lax.broadcasted_iota(jnp.int32, (B, T), 1)
    wide_row = lax.broadcasted_iota(jnp.int32, (B, T), 0)
    for k in range(T // B):
        lo = k * B
        strip = x_ref[lo:lo + B, :]
        block = strip[:, (k // 2) * 128:(k // 2) * 128 + 128]
        if k % 2:
            block = pltpu.roll(block, B, 1)
        both = jnp.where(lane < B, block, ident)
        factor64([both[8 * g:8 * g + 8, :] for g in range(8)], f_ref)
        block_inv = f_ref[...][:, B:]
        inside = (col >= lo) & (col < lo + B)
        strip = jnp.where(inside, (col - lo == wide_row).astype(F32), strip)
        out = dot(block_inv, strip, NN)
        x_ref[lo:lo + B, :] = jnp.where(col < lo + B, out, 0.0)
        if lo + B < T:
            rest = T - lo - B
            rest_col = lax.broadcasted_iota(jnp.int32, (rest, T), 1)
            old = x_ref[lo + B:, :]
            old = jnp.where((rest_col >= lo) & (rest_col < lo + B), 0.0, old)
            x_ref[lo + B:, :] = old - dot(out[:, lo + B:], out, TN)


def first_kernel(w00_ref, inv0_ref, f_ref):
    inv0_ref[...] = w00_ref[...]
    factor256(inv0_ref, f_ref)


def second_kernel(piv_ref, inv0_ref, w10_ref, w11_ref, l10_ref, inv1_ref, f_ref):
    l10 = dot(w10_ref[...], inv0_ref[...], NT)
    l10_ref[...] = l10
    inv1_ref[...] = jnp.zeros((T, T), F32)

    @pl.when(piv_ref[0] >= 2)
    def _():
        inv1_ref[...] = w11_ref[...] - dot(l10, l10, NT)
        factor256(inv1_ref, f_ref)


def iota(shape, dim):
    return lax.broadcasted_iota(jnp.int32, shape, dim)


def fdot(a, b):
    return lax.dot_general(a, b, (((1,), (0,)), ((), ())), preferred_element_type=F32)


def route(codes, z, y, c):
    shape = (32, 128)
    row, lane = iota(shape, 0), iota(shape, 1)
    zs, ys = row // 4, row % 4
    cs, zd, yd, cd = lane // 64, (lane // 8) % 8, (lane // 2) % 4, lane % 2
    live = (codes >= 0) & (lane % 64 > 0)
    sq = (128, 128)
    before = (iota(sq, 0) < iota(sq, 1)).astype(F32)
    ones = jnp.ones(sq, F32)
    dz = (zd - zs + 8) % 8
    masks = [(live & (dz == d)).astype(F32) for d in range(8)]
    rank = [None] + [fdot(masks[d], before) for d in range(1, 8)]
    total = [None] + [fdot(masks[d], ones) for d in range(1, 8)]
    ahead = total[1] + total[2] + total[3]
    behind = total[5] + total[6] + total[7]
    plus4 = jnp.clip(jnp.floor((total[4] + behind - ahead + 1.0) * 0.5), 0.0, total[4])
    minus4 = total[4] - plus4
    base = {3: plus4, 2: plus4 + total[3], 1: plus4 + total[3] + total[2], 5: minus4, 6: minus4 + total[5], 7: minus4 + total[5] + total[6]}
    position = jnp.where(rank[4] < plus4, rank[4], rank[4] - plus4) * masks[4]
    for d, start in base.items():
        position = position + masks[d] * (start + rank[d])
    up = plus4 + ahead, base[1], base[2], base[3]
    down = minus4 + behind, base[7], base[6], base[5]
    over = jnp.zeros(shape, F32)
    for k in range(4):
        over = jnp.maximum(over, jnp.maximum(up[k], down[k]) - CZ[k])
    negative = (dz > 4) | ((dz == 4) & (rank[4] >= plus4))
    core = jnp.where(dz == 0, cs, negative.astype(jnp.int32))
    tile = jnp.where(live, codes // 16, 0)
    slot = jnp.where(live, codes % 16, 0)
    mine = (row == z * 4 + y) & live & (dz > 0) & (core == c)
    send = jnp.where(mine, (position.astype(jnp.int32) * 2 + (cs != c)) * 16 + tile + 1, 0)
    table_a = jnp.sum(send, axis=0, keepdims=True) - 1
    from_lane, to_lane = iota(sq, 0), iota(sq, 1)
    pick = ((from_lane // 64 == to_lane // 8) & ((from_lane // 8) % 8 == z) & (from_lane % 8 == to_lane % 8) & (to_lane < 16)).astype(F32)
    here = fdot(live.astype(F32), pick) > 0.5
    core = fdot(core.astype(F32), pick).astype(jnp.int32)
    position = fdot(position, pick).astype(jnp.int32)
    tile = fdot(tile.astype(F32), pick).astype(jnp.int32)
    slot = fdot(slot.astype(F32), pick).astype(jnp.int32)
    cs, yd, cd = lane // 8, (lane // 2) % 4, lane % 2
    dz = (z - zs + 8) % 8
    hops = jnp.minimum(dz, 8 - dz)
    dy = (yd - ys + 4) % 4
    late = (hops > NEAR).astype(jnp.int32)
    rows = (32, 32)
    a, b = iota(rows, 0), iota(rows, 1)
    same = (a % 4 == b % 4).astype(F32)
    earlier = ((a % 4 == b % 4) & (b // 4 < a // 4)).astype(F32)
    yminus = jnp.zeros(shape, jnp.int32)
    yfar = (dy == 2).astype(jnp.int32)
    ypos = jnp.zeros(shape, F32)
    for r in range(2):
        for k in range(2):
            group = here & (late == r) & (core == k)
            m = [None] + [(group & (dy == d)).astype(F32) for d in range(1, 4)]
            sums = [None] + [fdot(m[d], ones) for d in range(1, 4)]
            n = [None] + [fdot(same, sums[d]) for d in range(1, 4)]
            order = [None] + [fdot(m[d], before) + fdot(earlier, sums[d]) for d in range(1, 4)]
            plus2 = jnp.clip(jnp.floor((n[2] + n[3] - n[1] + 1.0) * 0.5), 0.0, n[2])
            minus2 = n[2] - plus2
            goes_up = order[2] < plus2
            ypos = ypos + m[1] * (plus2 + order[1]) + m[3] * (minus2 + order[3])
            ypos = ypos + m[2] * jnp.where(goes_up, order[2], order[2] - plus2)
            yminus = yminus + (m[3] + m[2] * jnp.where(goes_up, 0.0, 1.0)).astype(jnp.int32)
            over = jnp.maximum(over, jnp.maximum(plus2 + n[1], minus2 + n[3]) - CY[r][0])
            over = jnp.maximum(over, jnp.maximum(plus2, minus2) - CY[r][1])
    ypos = ypos.astype(jnp.int32)
    held = jnp.where(hops == 0, tile, position)
    table_b = jnp.where(here & (core == c) & (ys == y) & (dy > 0), ((hops * 32 + held) * 2 + yminus) * 32 + ypos, -1)
    source = jnp.where(dy == 0, hops, 5 + 4 * late + 2 * yminus + yfar)
    held = jnp.where(dy == 0, held, ypos)
    table_c = jnp.where(here & (core == c) & (yd == y), ((source * 32 + held) * 2 + (cd != c)) * 16 + slot, -1)
    return table_a, table_b, table_c, jnp.max(over, keepdims=True)


def plan_kernel(where_ref, codes_ref, a_ref, b_ref, c_ref, over_ref):
    a, b, c, over = route(codes_ref[...], where_ref[0], where_ref[1], where_ref[2])
    a_ref[...] = a
    b_ref[...] = b
    c_ref[...] = c
    over_ref[...] = over


def panel_kernel(place_ref, first_ref, inv0_ref, l10_ref, inv1_ref, front_ref, *refs):
    pieces = refs[:12]
    factor_ref, out_ref, zero_ref, yh_ref, yl_ref = refs[12:]
    place = place_ref[0]
    a0 = split3(inv0_ref[...])
    low = split(l10_ref[...])
    inv1 = inv1_ref[...]
    for q in range(4):
        for r in range(2):
            if q == 0:
                p0 = front_ref[0, r, 0, :, 0:T]
                p1 = front_ref[0, r, 0, :, T:2 * T].astype(F32)
            else:
                p0 = pieces[(q - 1) * 4 + r * 2][...].astype(BF16)
                p1 = pieces[(q - 1) * 4 + r * 2 + 1][...]
            y0 = dot1(p0, a0[0], NT) + (dot1(p0, a0[1], NT) + dot1(p0, a0[2], NT))
            y0h, y0l = split(y0)
            p1 = p1 - dot3((y0h, y0l), low, NT)
            y1 = dot(p1, inv1, NT)
            if r == 0:
                owner = lax.rem(place + q, 4)
                y1 = jnp.where(owner > 0, y1, 0.0)
            y1h, y1l = split(y1)
            n = q * 2 + r
            yh_ref[n, :, 0:T] = y0h
            yl_ref[n, :, 0:T] = y0l
            yh_ref[n, :, T:2 * T] = y1h
            yl_ref[n, :, T:2 * T] = y1l
            if q == 0:
                factor_ref[0, r, 0, :, 0:T] = y0
                factor_ref[0, r, 0, :, T:2 * T] = y1
    for r in range(2):
        for n in range(8):
            column = lax.rem(place + n // 2, 4) + 4 * (n % 2)

            @pl.when(column > 0)
            def _():
                start = pl.multiple_of(column * T, T)
                tile = front_ref[0, r, 0, :, pl.ds(start, T)].astype(F32)
                own = (yh_ref[r], yl_ref[r])
                other = (yh_ref[n], yl_ref[n])
                tile = tile - dot3(own, other, NT)
                index = r * 7 + column - 1
                out_ref[index] = tile

                @pl.when(index == first_ref[0])
                def _():
                    zero_ref[...] = tile


def chunk_copy(sources, source, held, dest_refs, dest, pos, sem):
    for sid, lo, hi, ref in sources:
        for did, dlo, dhi, dref in dest_refs:
            @pl.when((source == sid) & (held >= lo) & (held < hi) & (dest == did) & (pos >= dlo) & (pos < dhi))
            def _():
                pltpu.make_async_copy(ref.at[held - lo], dref.at[pos - dlo], sem).start()


def queue_kernel(table_ref, own_ref, sib_ref, a_ref, b_ref, c_ref, d_ref, sem):
    outs = [None] * 4
    outs[0] = (0, 0, CZ[3], a_ref)
    outs[1] = (0, CZ[3], CZ[2], b_ref)
    outs[2] = (0, CZ[2], CZ[1], c_ref)
    outs[3] = (0, CZ[1], CZ[0], d_ref)
    sources = [(0, 0, TILES, own_ref), (1, 0, TILES, sib_ref)]

    def start(e, _):
        code = table_ref[0, e]

        @pl.when(code >= 0)
        def _():
            pos = code // 32
            chunk_copy(sources, (code // 16) % 2, code % 16, outs, 0, pos, sem.at[pos])
        return 0

    def wait(e, _):
        code = table_ref[0, e]

        @pl.when(code >= 0)
        def _():
            pltpu.make_async_copy(own_ref.at[0], a_ref.at[0], sem.at[code // 32]).wait()
        return 0

    lax.fori_loop(0, 128, start, 0)
    lax.fori_loop(0, 128, wait, 0)


def turn_kernel(late, where_ref, table_ref, *refs):
    z, y = where_ref[0], where_ref[1]
    near, far = CY[late]
    if late:
        spans = [(2, 0, CZ[3]), (2, CZ[3], CZ[2]), (2, CZ[2], CZ[1]), (3, 0, CZ[3]), (3, CZ[3], CZ[2]), (4, 0, CZ[3])]
        offsets = [2, 3, 4, 5, 6]
    else:
        spans = [(0, 0, TILES), (1, 0, CZ[3]), (1, CZ[3], CZ[2]), (1, CZ[2], CZ[1]), (1, CZ[1], CZ[0])]
        offsets = [7, 0, 1]
    count = len(spans)
    sources = [span + (ref,) for span, ref in zip(spans, refs[:count])]
    up_far, up_near, down_far, down_near, sem = refs[count:]
    outs = [(0, 0, far, up_far), (0, far, near, up_near), (1, 0, far, down_far), (1, far, near, down_near)]

    def each(act):
        for offset in offsets:
            row = lax.rem(z + offset, 8) * 4 + y

            def body(e, _):
                code = table_ref[row, e]

                @pl.when(code >= 0)
                def _():
                    pos, minus, held, hops = code % 32, (code // 32) % 2, (code // 64) % 32, code // 2048
                    act(pos, minus, held, hops)
                return 0

            lax.fori_loop(0, 16, body, 0)

    def start(pos, minus, held, hops):
        chunk_copy(sources, hops, held, outs, minus, pos, sem.at[minus * near + pos])

    def wait(pos, minus, held, hops):
        pltpu.make_async_copy(refs[0].at[0], up_far.at[0], sem.at[minus * near + pos]).wait()

    each(start)
    each(wait)


DEPTH = 8


def sum_kernel(where_ref, table_ref, codes_ref, *refs):
    z, y, c = where_ref[0], where_ref[1], where_ref[2]
    spans = [(0, 0, TILES), (1, 0, CZ[3]), (1, CZ[3], CZ[2]), (1, CZ[2], CZ[1]), (1, CZ[1], CZ[0]),
             (2, 0, CZ[3]), (2, CZ[3], CZ[2]), (2, CZ[2], CZ[1]), (3, 0, CZ[3]), (3, CZ[3], CZ[2]), (4, 0, CZ[3])]
    for late in range(2):
        near, far = CY[late]
        for minus in range(2):
            base = 5 + 4 * late + 2 * minus
            spans += [(base, 0, far), (base, far, near), (base + 1, 0, far)]
    spans += [(13 + i, 0, 8) for i in range(4)]
    count = len(spans)
    sources = [span + (ref,) for span, ref in zip(spans, refs[:count])]
    own_ref, sib_ref, list_ref, buf_ref, sem = refs[count:]
    own_ref[...] = jnp.zeros_like(own_ref)
    sib_ref[...] = jnp.zeros_like(sib_ref)

    def collect(row, n):
        for cs in range(2):
            for cd in range(2):
                code = table_ref[row, (cs * 4 + y) * 2 + cd]

                @pl.when(code >= 0)
                def _():
                    list_ref[n] = code
                n = n + (code >= 0).astype(jnp.int32)
        return n

    n = lax.fori_loop(0, 32, collect, jnp.int32(0))
    root = (z == 0) & (y == 0)

    def collect_root(row, n):
        code = codes_ref[row, c * 64]
        list_ref[n] = (((13 + row % 4) * 32 + row // 4) * 2 + c) * 16 + code % 16
        return n + 1

    n = lax.fori_loop(0, jnp.where(root, 32, 0), collect_root, n)

    def start(i):
        code = list_ref[i]
        source, held = code // 1024, (code // 32) % 32
        slot = lax.rem(i, DEPTH)
        for sid, lo, hi, ref in sources:
            @pl.when((source == sid) & (held >= lo) & (held < hi))
            def _():
                pltpu.make_async_copy(ref.at[held - lo], buf_ref.at[slot], sem.at[slot]).start()

    def prime(i, _):
        start(i)
        return 0

    def step(i, _):
        slot = lax.rem(i, DEPTH)
        pltpu.make_async_copy(refs[0].at[0], buf_ref.at[slot], sem.at[slot]).wait()
        code = list_ref[i]
        target = code % 16
        other = (code // 16) % 2

        @pl.when(other == 0)
        def _():
            own_ref[target] += buf_ref[slot]

        @pl.when(other == 1)
        def _():
            sib_ref[target] += buf_ref[slot]

        @pl.when(i + DEPTH < n)
        def _():
            start(i + DEPTH)
        return 0

    lax.fori_loop(0, jnp.minimum(n, DEPTH), prime, 0)
    lax.fori_loop(0, n, step, 0)


def slots_kernel(tile_ref, own_ref, out_ref, sem):
    def start(p, _):
        tile = tile_ref[p]

        @pl.when(tile >= 0)
        def _():
            pltpu.make_async_copy(own_ref.at[tile], out_ref.at[p], sem.at[p]).start()
        return 0

    def wait(p, _):
        @pl.when(tile_ref[p] >= 0)
        def _():
            pltpu.make_async_copy(own_ref.at[0], out_ref.at[p], sem.at[p]).wait()
        return 0

    lax.fori_loop(0, 64, start, 0)
    lax.fori_loop(0, 64, wait, 0)


def add_kernel(target_ref, arrived_ref, out_ref):
    step = pl.program_id(0)

    @pl.when(step == 0)
    def _():
        out_ref[...] = jnp.zeros_like(out_ref)

    for i in range(4):
        target = target_ref[step * 4 + i]

        @pl.when(target >= 0)
        def _():
            out_ref[target] += arrived_ref[i]


def tiles(*counts):
    return tuple(jax.ShapeDtypeStruct((n, T, T), F32) for n in counts)


def leaf_id(z, y, c):
    return ((z % 8) * 4 + y % 4) * 2 + c


PLACES = [(z, y, c) for z in range(8) for y in range(4) for c in range(2)]


def send(x, pairs):
    return lax.ppermute(x, "leaf", [(leaf_id(*a), leaf_id(*b)) for a, b in pairs])


def dense(work, zero, tile, slot, codes, where, a, b, c):
    outgoing = pl.pallas_call(
        slots_kernel,
        out_shape=tiles(64)[0],
        in_specs=[SMEM, ANY],
        out_specs=ANY,
        scratch_shapes=[pltpu.SemaphoreType.DMA((64,))],
        name="slots",
    )(tile, work)
    arrived = lax.all_to_all(outgoing, "leaf", split_axis=0, concat_axis=0, tiled=True)
    targets = lax.all_to_all(slot, "leaf", split_axis=0, concat_axis=0, tiled=True)
    return pl.pallas_call(
        add_kernel,
        out_shape=tiles(ASLOT)[0],
        grid=(16,),
        in_specs=[SMEM, pl.BlockSpec((4, T, T), lambda i: (i, 0, 0))],
        out_specs=pl.BlockSpec((ASLOT, T, T), lambda i: (0, 0, 0)),
        compiler_params=pltpu.CompilerParams(vmem_limit_bytes=32 << 20),
        name="add",
    )(targets, arrived)


def sparse(work, zero, tile, slot, codes, where, a, b, c):
    swap = [((z, y, c), (z, y, 1 - c)) for z, y, c in PLACES]
    ring = [((z, y, c), (z + 1 - 2 * c, y, c)) for z, y, c in PLACES]
    column = [zero]
    for z in range(1, 8):
        column.append(send(zero, [((z, y, c), (0, y, c)) for y in range(4) for c in range(2)]))
    column = jnp.stack(column)
    pass_on = send(column, [((0, 2, 0), (0, 1, 0)), ((0, 2, 1), (0, 3, 1))])
    row1 = send(column, [((0, 1, c), (0, 0, c)) for c in range(2)])
    row3 = send(column, [((0, 3, c), (0, 0, c)) for c in range(2)])
    row2 = send(pass_on, [((0, 1, 0), (0, 0, 0)), ((0, 3, 1), (0, 0, 1))])
    other = send(work, swap)
    cur = list(pl.pallas_call(
        queue_kernel,
        out_shape=tiles(CZ[3], CZ[2] - CZ[3], CZ[1] - CZ[2], CZ[0] - CZ[1]),
        in_specs=[SMEM, ANY, ANY],
        out_specs=(ANY,) * 4,
        scratch_shapes=[pltpu.SemaphoreType.DMA((CZ[0],))],
        name="queue",
    )(a, work, other))
    after = [None]
    for k in range(4):
        cur = [send(x, ring) for x in cur[:4 - k]]
        after.append(cur)
    turned = []
    for late in range(2):
        near, far = CY[late]
        held = after[2] + after[3] + after[4] if late else [work] + after[1]
        lists = pl.pallas_call(
            lambda *refs, late=late: turn_kernel(late, *refs),
            out_shape=tiles(far, near - far, far, near - far),
            in_specs=[SMEM, SMEM] + [ANY] * len(held),
            out_specs=(ANY,) * 4,
            scratch_shapes=[pltpu.SemaphoreType.DMA((2 * near,))],
            name="turn",
        )(where, b, *held)
        for minus in range(2):
            hop = [((z, y, c), (z, y + 1 - 2 * minus, c)) for z, y, c in PLACES]
            first = send(lists[2 * minus], hop)
            near_one = send(lists[2 * minus + 1], hop)
            turned += [first, near_one, send(first, hop)]
    held = [work] + after[1] + after[2] + after[3] + after[4] + turned + [column, row1, row2, row3]
    own, theirs = pl.pallas_call(
        sum_kernel,
        out_shape=tiles(ASLOT, ASLOT),
        in_specs=[SMEM, SMEM, SMEM] + [ANY] * len(held),
        out_specs=(VMEM, VMEM),
        scratch_shapes=[pltpu.SMEM((256,), jnp.int32), pltpu.VMEM((DEPTH, T, T), F32), pltpu.SemaphoreType.DMA((DEPTH,))],
        compiler_params=pltpu.CompilerParams(vmem_limit_bytes=32 << 20),
        name="sum",
    )(where, c, codes, *held)
    return own + send(theirs, swap)


def local(front, pivot_tiles, send_table):
    place = lax.axis_index("front").astype(jnp.int32)
    leaf = lax.axis_index("leaf").astype(jnp.int32)
    where = jnp.stack([leaf // 8, (leaf // 2) % 4, leaf % 2])
    table = send_table[0, 0]
    used = table[0] >= 0
    tile = jnp.where(used, table[0] * 7 + table[1] - 1, -1)
    code = jnp.where(used, tile * 16 + table[2], -1)
    codes = lax.all_gather(code, "leaf", tiled=True).reshape(32, 128)
    a, b, c, over = pl.pallas_call(
        plan_kernel,
        out_shape=(
            jax.ShapeDtypeStruct((1, 128), jnp.int32),
            jax.ShapeDtypeStruct((32, 128), jnp.int32),
            jax.ShapeDtypeStruct((32, 128), jnp.int32),
            jax.ShapeDtypeStruct((1, 1), F32),
        ),
        in_specs=[SMEM, VMEM],
        out_specs=(VMEM,) * 4,
        name="plan",
    )(where, codes)
    over = lax.pmax(over[0, 0], ("leaf", "front"))

    up = [(i, (i + 1) % 4) for i in range(4)]
    down = [(i, (i - 1) % 4) for i in range(4)]
    own = [[front[0, r, 0, :, k * T:k * T + T].astype(F32) for k in range(2)] for r in range(2)]
    from_left = [[None, None], [None, None]]
    from_right = [[None, None], [None, None]]
    from_far = [[None, None], [None, None]]
    for r in range(2):
        for k in range(2):
            from_left[r][k] = lax.ppermute(own[r][k], "front", up)
            from_right[r][k] = lax.ppermute(own[r][k], "front", down)
            if k == 0:
                from_far[r][k] = lax.ppermute(from_left[r][k], "front", up)
            else:
                from_far[r][k] = lax.ppermute(from_right[r][k], "front", down)
    by_q = [own, from_right, from_far, from_left]

    def of_owner(owner, r, k):
        q = lax.rem(owner - place + 4, 4)
        out = by_q[0][r][k]
        for i in range(1, 4):
            out = jnp.where(q == i, by_q[i][r][k], out)
        return out

    inv0 = pl.pallas_call(
        first_kernel,
        out_shape=jax.ShapeDtypeStruct((T, T), F32),
        in_specs=[VMEM],
        out_specs=VMEM,
        scratch_shapes=[pltpu.VMEM((B, 128), F32)],
        compiler_params=pltpu.CompilerParams(vmem_limit_bytes=16 << 20),
        name="first",
    )(of_owner(0, 0, 0))
    l10, inv1 = pl.pallas_call(
        second_kernel,
        out_shape=(jax.ShapeDtypeStruct((T, T), F32),) * 2,
        in_specs=[SMEM, VMEM, VMEM, VMEM],
        out_specs=(VMEM, VMEM),
        scratch_shapes=[pltpu.VMEM((B, 128), F32)],
        compiler_params=pltpu.CompilerParams(vmem_limit_bytes=16 << 20),
        name="second",
    )(pivot_tiles, inv0, of_owner(1, 0, 0), of_owner(1, 0, 1))

    received = [by_q[q][r][k] for q in range(1, 4) for r in range(2) for k in range(2)]
    factor, work, zero = pl.pallas_call(
        panel_kernel,
        out_shape=(jax.ShapeDtypeStruct((1, 2, 1, T, 2 * T), F32),) + tiles(TILES) + (jax.ShapeDtypeStruct((T, T), F32),),
        in_specs=[SMEM, SMEM] + [VMEM] * 16,
        out_specs=(VMEM, VMEM, VMEM),
        scratch_shapes=[pltpu.VMEM((8, T, 2 * T), BF16), pltpu.VMEM((8, T, 2 * T), BF16)],
        compiler_params=pltpu.CompilerParams(vmem_limit_bytes=40 << 20),
        name="panel",
    )(place.reshape(1), tile[0:1], inv0, l10, inv1, front, *received)
    ancestor = lax.cond(over > 0.0, dense, sparse, work, zero, tile, table[2], codes, where, a, b, c)
    return (factor, ancestor.reshape(1, 1, ASLOT, T, T))


def solution(mesh):
    in_specs = (P("leaf", None, "front", None, None), P("leaf"), P("leaf", "front", None, None))
    out_specs = (P("leaf", None, "front", None, None), P("leaf", "front", None, None, None))
    return jax.shard_map(local, mesh=mesh, in_specs=in_specs, out_specs=out_specs, check_vma=False)
```

```python
import functools

import jax
import jax.numpy as jnp
from jax import lax
from jax.experimental import pallas as pl
from jax.experimental.pallas import tpu as pltpu
from jax.sharding import PartitionSpec as P

PT = 2
ASLOT = 16
TILES = 14
CZ = (18, 14, 11, 8)
CY = ((6, 5), (8, 5))
NEAR = 1
LEAD = 6
B = 64
T = 256
F32 = jnp.float32
BF16 = jnp.bfloat16
HIGHEST = lax.Precision.HIGHEST
VMEM = pl.BlockSpec(memory_space=pltpu.VMEM)
SMEM = pl.BlockSpec(memory_space=pltpu.SMEM)
ANY = pl.BlockSpec(memory_space=pl.ANY)
NN = (((1,), (0,)), ((), ()))
NT = (((1,), (1,)), ((), ()))
TN = (((0,), (0,)), ((), ()))


def dot(a, b, dims):
    return lax.dot_general(a, b, dims, precision=HIGHEST, preferred_element_type=F32)


def dot1(a, b, dims):
    return lax.dot_general(a, b, dims, preferred_element_type=F32)


def split(x):
    high = x.astype(BF16)
    return high, (x - high.astype(F32)).astype(BF16)


def split3(x):
    high = x.astype(BF16)
    rest = x - high.astype(F32)
    mid = rest.astype(BF16)
    return high, mid, (rest - mid.astype(F32)).astype(BF16)


def dot3(a, b, dims):
    ah, al = a
    bh, bl = b
    return dot1(ah, bh, dims) + (dot1(ah, bl, dims) + dot1(al, bh, dims))


def factor64(groups, f_ref):
    sub = lax.broadcasted_iota(jnp.int32, (8, 128), 0)

    def body(it, gs):
        cols = [[jnp.broadcast_to(g[:, t:t + 1], (8, 128)) for t in range(8)] for g in gs]
        rows = [jnp.broadcast_to(gs[0][t:t + 1, :], (8, 128)) for t in range(8)]
        s = [[jnp.broadcast_to(cols[0][t][u:u + 1, :], (8, 128)) if u >= t else None for t in range(8)] for u in range(8)]
        inv = [None] * 8
        for t in range(8):
            inv[t] = 1.0 / s[t][t]
            for u in range(t + 1, 8):
                low = s[u][t] * inv[t]
                for v in range(u, 8):
                    s[v][u] = s[v][u] - low * s[v][t]
                rows[u] = rows[u] - low * rows[t]
                for g in range(1, 8):
                    cols[g][u] = cols[g][u] - low * cols[g][t]
        done = jnp.zeros((8, 128), F32)
        for t in range(8):
            done = jnp.where(sub == t, rows[t] * lax.rsqrt(s[t][t]), done)
        f_ref[pl.ds(pl.multiple_of(it * 8, 8), 8), :] = pltpu.roll(done, it * 8, 1)
        scaled = [rows[t] * inv[t] for t in range(8)]
        left = []
        for g in range(1, 8):
            piece = gs[g]
            for t in range(8):
                piece = piece - cols[g][t] * scaled[t]
            left.append(pltpu.roll(piece, 120, 1))
        left.append(gs[0])
        return tuple(left)

    lax.fori_loop(0, 8, body, tuple(groups))


def factor256(x_ref, f_ref):
    lane = lax.broadcasted_iota(jnp.int32, (B, 128), 1)
    row = lax.broadcasted_iota(jnp.int32, (B, 128), 0)
    ident = (lane - B == row).astype(F32)
    col = lax.broadcasted_iota(jnp.int32, (B, T), 1)
    wide_row = lax.broadcasted_iota(jnp.int32, (B, T), 0)
    for k in range(T // B):
        lo = k * B
        strip = x_ref[lo:lo + B, :]
        block = strip[:, (k // 2) * 128:(k // 2) * 128 + 128]
        if k % 2:
            block = pltpu.roll(block, B, 1)
        both = jnp.where(lane < B, block, ident)
        factor64([both[8 * g:8 * g + 8, :] for g in range(8)], f_ref)
        block_inv = f_ref[...][:, B:]
        inside = (col >= lo) & (col < lo + B)
        strip = jnp.where(inside, (col - lo == wide_row).astype(F32), strip)
        out = dot(block_inv, strip, NN)
        x_ref[lo:lo + B, :] = jnp.where(col < lo + B, out, 0.0)
        if lo + B < T:
            rest = T - lo - B
            rest_col = lax.broadcasted_iota(jnp.int32, (rest, T), 1)
            old = x_ref[lo + B:, :]
            old = jnp.where((rest_col >= lo) & (rest_col < lo + B), 0.0, old)
            x_ref[lo + B:, :] = old - dot(out[:, lo + B:], out, TN)


def first_kernel(w00_ref, inv0_ref, f_ref):
    inv0_ref[...] = w00_ref[...]
    factor256(inv0_ref, f_ref)


def second_kernel(piv_ref, inv0_ref, w10_ref, w11_ref, l10_ref, inv1_ref, f_ref):
    l10 = dot(w10_ref[...], inv0_ref[...], NT)
    l10_ref[...] = l10
    inv1_ref[...] = jnp.zeros((T, T), F32)

    @pl.when(piv_ref[0] >= 2)
    def _():
        inv1_ref[...] = w11_ref[...] - dot(l10, l10, NT)
        factor256(inv1_ref, f_ref)


def iota(shape, dim):
    return lax.broadcasted_iota(jnp.int32, shape, dim)


def fdot(a, b):
    return lax.dot_general(a, b, (((1,), (0,)), ((), ())), preferred_element_type=F32)


def route(codes, z, y, c):
    shape = (32, 128)
    row, lane = iota(shape, 0), iota(shape, 1)
    zs, ys = row // 4, row % 4
    cs, zd, yd, cd = lane // 64, (lane // 8) % 8, (lane // 2) % 4, lane % 2
    live = (codes >= 0) & (lane % 64 > 0)
    sq = (128, 128)
    before = (iota(sq, 0) < iota(sq, 1)).astype(F32)
    ones = jnp.ones(sq, F32)
    dz = (zd - zs + 8) % 8
    masks = [(live & (dz == d)).astype(F32) for d in range(8)]
    rank = [None] + [fdot(masks[d], before) for d in range(1, 8)]
    total = [None] + [fdot(masks[d], ones) for d in range(1, 8)]
    ahead = total[1] + total[2] + total[3]
    behind = total[5] + total[6] + total[7]
    plus4 = jnp.clip(jnp.floor((total[4] + behind - ahead + 1.0) * 0.5), 0.0, total[4])
    minus4 = total[4] - plus4
    base = {3: plus4, 2: plus4 + total[3], 1: plus4 + total[3] + total[2], 5: minus4, 6: minus4 + total[5], 7: minus4 + total[5] + total[6]}
    position = jnp.where(rank[4] < plus4, rank[4], rank[4] - plus4) * masks[4]
    for d, start in base.items():
        position = position + masks[d] * (start + rank[d])
    up = plus4 + ahead, base[1], base[2], base[3]
    down = minus4 + behind, base[7], base[6], base[5]
    over = jnp.zeros(shape, F32)
    for k in range(4):
        over = jnp.maximum(over, jnp.maximum(up[k], down[k]) - CZ[k])
    negative = (dz > 4) | ((dz == 4) & (rank[4] >= plus4))
    core = jnp.where(dz == 0, cs, negative.astype(jnp.int32))
    tile = jnp.where(live, codes // 16, 0)
    slot = jnp.where(live, codes % 16, 0)
    mine = (row == z * 4 + y) & live & (dz > 0) & (core == c)
    send = jnp.where(mine, (position.astype(jnp.int32) * 2 + (cs != c)) * 16 + tile + 1, 0)
    table_a = jnp.sum(send, axis=0, keepdims=True) - 1
    here = live
    hops = jnp.minimum(dz, 8 - dz)
    dy = (yd - ys + 4) % 4
    late = (hops > NEAR).astype(jnp.int32)
    together = ((iota(sq, 0) // 8) % 8 == (iota(sq, 1) // 8) % 8).astype(F32)
    before = before * together
    position = position.astype(jnp.int32)
    rows = (32, 32)
    a, b = iota(rows, 0), iota(rows, 1)
    same = (a % 4 == b % 4).astype(F32)
    earlier = ((a % 4 == b % 4) & (b // 4 < a // 4)).astype(F32)
    yminus = jnp.zeros(shape, jnp.int32)
    yfar = (dy == 2).astype(jnp.int32)
    ypos = jnp.zeros(shape, F32)
    for r in range(2):
        for k in range(2):
            group = here & (late == r) & (core == k)
            m = [None] + [(group & (dy == d)).astype(F32) for d in range(1, 4)]
            sums = [None] + [fdot(m[d], together) for d in range(1, 4)]
            n = [None] + [fdot(same, sums[d]) for d in range(1, 4)]
            order = [None] + [fdot(m[d], before) + fdot(earlier, sums[d]) for d in range(1, 4)]
            plus2 = jnp.clip(jnp.floor((n[2] + n[3] - n[1] + 1.0) * 0.5), 0.0, n[2])
            minus2 = n[2] - plus2
            goes_up = order[2] < plus2
            ypos = ypos + m[1] * (plus2 + order[1]) + m[3] * (minus2 + order[3])
            ypos = ypos + m[2] * jnp.where(goes_up, order[2], order[2] - plus2)
            yminus = yminus + (m[3] + m[2] * jnp.where(goes_up, 0.0, 1.0)).astype(jnp.int32)
            over = jnp.maximum(over, jnp.maximum(plus2 + n[1], minus2 + n[3]) - CY[r][0])
            over = jnp.maximum(over, jnp.maximum(plus2, minus2) - CY[r][1])
    ypos = ypos.astype(jnp.int32)
    held = jnp.where(hops == 0, tile, position)
    table_b = jnp.where(here & (zd == z) & (core == c) & (ys == y) & (dy > 0), ((hops * 32 + held) * 2 + yminus) * 32 + ypos, -1)
    source = jnp.where(dy == 0, hops, 5 + 4 * late + 2 * yminus + yfar)
    held = jnp.where(dy == 0, held, ypos)
    table_c = jnp.where(here & (zd == z) & (core == c) & (yd == y), ((source * 32 + held) * 2 + (cd != c)) * 16 + slot, -1)
    return table_a, table_b, table_c, jnp.max(over, keepdims=True)


def plan_kernel(where_ref, codes_ref, a_ref, b_ref, c_ref, over_ref):
    a, b, c, over = route(codes_ref[...], where_ref[0], where_ref[1], where_ref[2])
    a_ref[...] = a
    b_ref[...] = b
    c_ref[...] = c
    over_ref[...] = over


def panel_kernel(place_ref, first_ref, inv0_ref, l10_ref, inv1_ref, front_ref, *refs):
    pieces = refs[:12]
    factor_ref, out_ref, zero_ref, yh_ref, yl_ref = refs[12:]
    place = place_ref[0]
    a0 = split3(inv0_ref[...])
    low = split(l10_ref[...])
    inv1 = inv1_ref[...]
    for q in range(4):
        for r in range(2):
            if q == 0:
                p0 = front_ref[0, r, 0, :, 0:T]
                p1 = front_ref[0, r, 0, :, T:2 * T].astype(F32)
            else:
                p0 = pieces[(q - 1) * 4 + r * 2][...].astype(BF16)
                p1 = pieces[(q - 1) * 4 + r * 2 + 1][...]
            y0 = dot1(p0, a0[0], NT) + (dot1(p0, a0[1], NT) + dot1(p0, a0[2], NT))
            y0h, y0l = split(y0)
            p1 = p1 - dot3((y0h, y0l), low, NT)
            y1 = dot(p1, inv1, NT)
            if r == 0:
                owner = lax.rem(place + q, 4)
                y1 = jnp.where(owner > 0, y1, 0.0)
            y1h, y1l = split(y1)
            n = q * 2 + r
            yh_ref[n, :, 0:T] = y0h
            yl_ref[n, :, 0:T] = y0l
            yh_ref[n, :, T:2 * T] = y1h
            yl_ref[n, :, T:2 * T] = y1l
            if q == 0:
                factor_ref[0, r, 0, :, 0:T] = y0
                factor_ref[0, r, 0, :, T:2 * T] = y1
    for r in range(2):
        for n in range(8):
            column = lax.rem(place + n // 2, 4) + 4 * (n % 2)

            @pl.when(column > 0)
            def _():
                start = pl.multiple_of(column * T, T)
                tile = front_ref[0, r, 0, :, pl.ds(start, T)].astype(F32)
                own = (yh_ref[r], yl_ref[r])
                other = (yh_ref[n], yl_ref[n])
                tile = tile - dot3(own, other, NT)
                index = r * 7 + column - 1
                out_ref[index] = tile

                @pl.when(index == first_ref[0])
                def _():
                    zero_ref[...] = tile


def chunk_copy(sources, source, held, dest_refs, dest, pos, sem):
    for sid, lo, hi, ref in sources:
        for did, dlo, dhi, dref in dest_refs:
            @pl.when((source == sid) & (held >= lo) & (held < hi) & (dest == did) & (pos >= dlo) & (pos < dhi))
            def _():
                pltpu.make_async_copy(ref.at[held - lo], dref.at[pos - dlo], sem).start()


def queue_kernel(table_ref, own_ref, sib_ref, a_ref, b_ref, sem):
    outs = [(0, 0, LEAD, a_ref), (0, LEAD, CZ[0], b_ref)]
    sources = [(0, 0, TILES, own_ref), (1, 0, TILES, sib_ref)]

    def start(e, _):
        code = table_ref[0, e]

        @pl.when(code >= 0)
        def _():
            pos = code // 32
            chunk_copy(sources, (code // 16) % 2, code % 16, outs, 0, pos, sem.at[pos])
        return 0

    def wait(e, _):
        code = table_ref[0, e]

        @pl.when(code >= 0)
        def _():
            pltpu.make_async_copy(own_ref.at[0], a_ref.at[0], sem.at[code // 32]).wait()
        return 0

    lax.fori_loop(0, 128, start, 0)
    lax.fori_loop(0, 128, wait, 0)


def turn_kernel(late, where_ref, table_ref, *refs):
    z, y = where_ref[0], where_ref[1]
    near, far = CY[late]
    if late:
        spans = [(k, lo, hi) for k in range(2, 5) for lo, hi in ((0, LEAD), (LEAD, CZ[k - 1]))]
        offsets = [2, 3, 4, 5, 6]
    else:
        spans = [(0, 0, TILES), (1, 0, LEAD), (1, LEAD, CZ[0])]
        offsets = [7, 0, 1]
    count = len(spans)
    sources = [span + (ref,) for span, ref in zip(spans, refs[:count])]
    up_far, up_near, down_far, down_near, sem = refs[count:]
    outs = [(0, 0, far, up_far), (0, far, near, up_near), (1, 0, far, down_far), (1, far, near, down_near)]

    def each(act):
        for offset in offsets:
            row = lax.rem(z + offset, 8) * 4 + y

            def body(e, _):
                code = table_ref[row, (e // 8) * 64 + z * 8 + e % 8]

                @pl.when(code >= 0)
                def _():
                    pos, minus, held, hops = code % 32, (code // 32) % 2, (code // 64) % 32, code // 2048
                    act(pos, minus, held, hops)
                return 0

            lax.fori_loop(0, 16, body, 0)

    def start(pos, minus, held, hops):
        chunk_copy(sources, hops, held, outs, minus, pos, sem.at[minus * near + pos])

    def wait(pos, minus, held, hops):
        pltpu.make_async_copy(refs[0].at[0], up_far.at[0], sem.at[minus * near + pos]).wait()

    each(start)
    each(wait)


DEPTH = 8


def sum_kernel(where_ref, table_ref, codes_ref, *refs):
    z, y, c = where_ref[0], where_ref[1], where_ref[2]
    spans = [(0, 0, TILES)]
    spans += [(k, lo, hi) for k in range(1, 5) for lo, hi in ((0, LEAD), (LEAD, CZ[k - 1]))]
    for late in range(2):
        near, far = CY[late]
        for minus in range(2):
            base = 5 + 4 * late + 2 * minus
            spans += [(base, 0, far), (base, far, near), (base + 1, 0, far)]
    spans += [(13 + i, 0, 8) for i in range(4)]
    count = len(spans)
    sources = [span + (ref,) for span, ref in zip(spans, refs[:count])]
    own_ref, sib_ref, list_ref, buf_ref, sem = refs[count:]
    own_ref[...] = jnp.zeros_like(own_ref)
    sib_ref[...] = jnp.zeros_like(sib_ref)

    def collect(row, n):
        for cs in range(2):
            for cd in range(2):
                code = table_ref[row, cs * 64 + z * 8 + y * 2 + cd]

                @pl.when(code >= 0)
                def _():
                    list_ref[n] = code
                n = n + (code >= 0).astype(jnp.int32)
        return n

    n = lax.fori_loop(0, 32, collect, jnp.int32(0))
    root = (z == 0) & (y == 0)

    def collect_root(row, n):
        code = codes_ref[row, c * 64]
        list_ref[n] = (((13 + row % 4) * 32 + row // 4) * 2 + c) * 16 + code % 16
        return n + 1

    n = lax.fori_loop(0, jnp.where(root, 32, 0), collect_root, n)

    def start(i):
        code = list_ref[i]
        source, held = code // 1024, (code // 32) % 32
        slot = lax.rem(i, DEPTH)
        for sid, lo, hi, ref in sources:
            @pl.when((source == sid) & (held >= lo) & (held < hi))
            def _():
                pltpu.make_async_copy(ref.at[held - lo], buf_ref.at[slot], sem.at[slot]).start()

    def prime(i, _):
        start(i)
        return 0

    def step(i, _):
        slot = lax.rem(i, DEPTH)
        pltpu.make_async_copy(refs[0].at[0], buf_ref.at[slot], sem.at[slot]).wait()
        code = list_ref[i]
        target = code % 16
        other = (code // 16) % 2

        @pl.when(other == 0)
        def _():
            own_ref[target] += buf_ref[slot]

        @pl.when(other == 1)
        def _():
            sib_ref[target] += buf_ref[slot]

        @pl.when(i + DEPTH < n)
        def _():
            start(i + DEPTH)
        return 0

    lax.fori_loop(0, jnp.minimum(n, DEPTH), prime, 0)
    lax.fori_loop(0, n, step, 0)


def slots_kernel(tile_ref, own_ref, out_ref, sem):
    def start(p, _):
        tile = tile_ref[p]

        @pl.when(tile >= 0)
        def _():
            pltpu.make_async_copy(own_ref.at[tile], out_ref.at[p], sem.at[p]).start()
        return 0

    def wait(p, _):
        @pl.when(tile_ref[p] >= 0)
        def _():
            pltpu.make_async_copy(own_ref.at[0], out_ref.at[p], sem.at[p]).wait()
        return 0

    lax.fori_loop(0, 64, start, 0)
    lax.fori_loop(0, 64, wait, 0)


def add_kernel(target_ref, arrived_ref, out_ref):
    step = pl.program_id(0)

    @pl.when(step == 0)
    def _():
        out_ref[...] = jnp.zeros_like(out_ref)

    for i in range(4):
        target = target_ref[step * 4 + i]

        @pl.when(target >= 0)
        def _():
            out_ref[target] += arrived_ref[i]


def tiles(*counts):
    return tuple(jax.ShapeDtypeStruct((n, T, T), F32) for n in counts)


def leaf_id(z, y, c):
    return ((z % 8) * 4 + y % 4) * 2 + c


PLACES = [(z, y, c) for z in range(8) for y in range(4) for c in range(2)]


def send(x, pairs):
    return lax.ppermute(x, "leaf", [(leaf_id(*a), leaf_id(*b)) for a, b in pairs])


def dense(work, zero, tile, slot, codes, where, a, b, c):
    outgoing = pl.pallas_call(
        slots_kernel,
        out_shape=tiles(64)[0],
        in_specs=[SMEM, ANY],
        out_specs=ANY,
        scratch_shapes=[pltpu.SemaphoreType.DMA((64,))],
        name="slots",
    )(tile, work)
    arrived = lax.all_to_all(outgoing, "leaf", split_axis=0, concat_axis=0, tiled=True)
    targets = lax.all_to_all(slot, "leaf", split_axis=0, concat_axis=0, tiled=True)
    return pl.pallas_call(
        add_kernel,
        out_shape=tiles(ASLOT)[0],
        grid=(16,),
        in_specs=[SMEM, pl.BlockSpec((4, T, T), lambda i: (i, 0, 0))],
        out_specs=pl.BlockSpec((ASLOT, T, T), lambda i: (0, 0, 0)),
        compiler_params=pltpu.CompilerParams(vmem_limit_bytes=32 << 20),
        name="add",
    )(targets, arrived)


def tie(x, *others):
    return lax.optimization_barrier((x,) + others)[0]


def turn(late, where, b, held):
    near, far = CY[late]
    return pl.pallas_call(
        lambda *refs: turn_kernel(late, *refs),
        out_shape=tiles(far, near - far, far, near - far),
        in_specs=[SMEM, SMEM] + [ANY] * len(held),
        out_specs=(VMEM,) * 4,
        scratch_shapes=[pltpu.SemaphoreType.DMA((2 * near,))],
        compiler_params=pltpu.CompilerParams(vmem_limit_bytes=16 << 20),
        name="turn",
    )(where, b, *held)


def sparse(work, zero, tile, slot, codes, where, a, b, c):
    swap = [((z, y, c), (z, y, 1 - c)) for z, y, c in PLACES]
    ring = [((z, y, c), (z + 1 - 2 * c, y, c)) for z, y, c in PLACES]
    hops = [[((z, y, c), (z, y + 1 - 2 * minus, c)) for z, y, c in PLACES] for minus in range(2)]
    other = send(work, swap)
    column = [zero]
    for z in range(1, 8):
        column.append(send(zero, [((z, y, c), (0, y, c)) for y in range(4) for c in range(2)]))
    lead, rest = pl.pallas_call(
        queue_kernel,
        out_shape=tiles(LEAD, CZ[0] - LEAD),
        in_specs=[SMEM, ANY, ANY],
        out_specs=(VMEM,) * 2,
        scratch_shapes=[pltpu.SemaphoreType.DMA((CZ[0],))],
        compiler_params=pltpu.CompilerParams(vmem_limit_bytes=16 << 20),
        name="queue",
    )(a, work, other)
    column = jnp.stack(column)
    after = [None]

    def along_z(lead, rest):
        lead, rest = send(lead, ring), send(rest[:CZ[len(after) - 1] - LEAD], ring)
        after.append([lead, rest])
        return lead, rest

    def along_y(lists):
        first = [send(x, hops[i // 2]) for i, x in enumerate(lists)]
        return first, [send(first[0], hops[0]), send(first[2], hops[1])]

    lead, rest = along_z(lead, rest)
    lists = turn(0, where, b, [work, lead, rest])
    lead, rest = along_z(lead, rest)
    lead = tie(lead, *lists)
    pass_on = send(column, [((0, 2, 0), (0, 1, 0)), ((0, 2, 1), (0, 3, 1))])
    row1 = send(column, [((0, 1, c), (0, 0, c)) for c in range(2)])
    row3 = send(column, [((0, 3, c), (0, 0, c)) for c in range(2)])
    row2 = send(pass_on, [((0, 1, 0), (0, 0, 0)), ((0, 3, 1), (0, 0, 1))])
    first, second = along_y(lists)
    lead, rest = along_z(lead, rest)
    lead = tie(lead, *first)
    lead, rest = along_z(lead, rest)
    early = [first[0], first[1], second[0], first[2], first[3], second[1]]
    lists = turn(1, where, b, after[2] + after[3] + after[4])
    lists = [tie(x, *early, row1, row2, row3) for x in lists]
    first, second = along_y(lists)
    last = [first[0], first[1], second[0], first[2], first[3], second[1]]
    held = [work] + after[1] + after[2] + after[3] + after[4] + early + last + [column, row1, row2, row3]
    own, theirs = pl.pallas_call(
        sum_kernel,
        out_shape=tiles(ASLOT, ASLOT),
        in_specs=[SMEM, SMEM, SMEM] + [ANY] * len(held),
        out_specs=(VMEM, VMEM),
        scratch_shapes=[pltpu.SMEM((256,), jnp.int32), pltpu.VMEM((DEPTH, T, T), F32), pltpu.SemaphoreType.DMA((DEPTH,))],
        compiler_params=pltpu.CompilerParams(vmem_limit_bytes=32 << 20),
        name="sum",
    )(where, c, codes, *held)
    return own + send(theirs, swap)


def local(front, pivot_tiles, send_table):
    place = lax.axis_index("front").astype(jnp.int32)
    leaf = lax.axis_index("leaf").astype(jnp.int32)
    where = jnp.stack([leaf // 8, (leaf // 2) % 4, leaf % 2])
    table = send_table[0, 0]
    used = table[0] >= 0
    tile = jnp.where(used, table[0] * 7 + table[1] - 1, -1)
    code = jnp.where(used, tile * 16 + table[2], -1)
    codes = lax.all_to_all(jnp.broadcast_to(code, (64, 64)), "leaf", split_axis=0, concat_axis=0, tiled=True).reshape(32, 128)
    up = [(i, (i + 1) % 4) for i in range(4)]
    down = [(i, (i - 1) % 4) for i in range(4)]
    own = [[front[0, r, 0, :, k * T:k * T + T].astype(F32) for k in range(2)] for r in range(2)]
    from_left = [[None, None], [None, None]]
    from_right = [[None, None], [None, None]]
    from_far = [[None, None], [None, None]]
    from_left[0][0] = lax.ppermute(own[0][0], "front", up)
    from_right[0][0] = lax.ppermute(own[0][0], "front", down)
    from_far[0][0] = lax.ppermute(tie(from_left[0][0], codes), "front", up)
    from_right[0][1] = lax.ppermute(tie(own[0][1], from_left[0][0], from_right[0][0]), "front", down)
    from_left[0][1] = lax.ppermute(tie(own[0][1], from_far[0][0]), "front", up)
    from_far[0][1] = lax.ppermute(from_right[0][1], "front", down)
    for k in range(2):
        from_left[1][k] = lax.ppermute(tie(own[1][k], from_far[0][0]), "front", up)
        from_right[1][k] = lax.ppermute(tie(own[1][k], from_far[0][0]), "front", down)
    from_far[1][0] = lax.ppermute(from_left[1][0], "front", up)
    from_far[1][1] = lax.ppermute(from_right[1][1], "front", down)
    by_q = [own, from_right, from_far, from_left]

    def of_owner(owner, r, k, *after):
        q = lax.rem(owner - place + 4, 4)
        if after:
            q = tie(q, *after)
        out = by_q[0][r][k]
        for i in range(1, 4):
            out = jnp.where(q == i, by_q[i][r][k], out)
        return out

    inv0 = pl.pallas_call(
        first_kernel,
        out_shape=jax.ShapeDtypeStruct((T, T), F32),
        in_specs=[VMEM],
        out_specs=VMEM,
        scratch_shapes=[pltpu.VMEM((B, 128), F32)],
        compiler_params=pltpu.CompilerParams(vmem_limit_bytes=16 << 20),
        name="first",
    )(of_owner(0, 0, 0))
    a, b, c, over = pl.pallas_call(
        plan_kernel,
        out_shape=(
            jax.ShapeDtypeStruct((1, 128), jnp.int32),
            jax.ShapeDtypeStruct((32, 128), jnp.int32),
            jax.ShapeDtypeStruct((32, 128), jnp.int32),
            jax.ShapeDtypeStruct((1, 1), F32),
        ),
        in_specs=[SMEM, VMEM],
        out_specs=(VMEM,) * 4,
        name="plan",
    )(where, tie(codes, inv0))
    others = [lax.ppermute(over, "front", [(i, (i + step) % 4) for i in range(4)]) for step in range(1, 4)]
    over = jnp.maximum(jnp.maximum(over, others[0]), jnp.maximum(others[1], others[2]))

    w10 = of_owner(1, 0, 0, inv0)
    w11 = of_owner(1, 0, 1, inv0)
    l10, inv1 = pl.pallas_call(
        second_kernel,
        out_shape=(jax.ShapeDtypeStruct((T, T), F32),) * 2,
        in_specs=[SMEM, VMEM, VMEM, VMEM],
        out_specs=(VMEM, VMEM),
        scratch_shapes=[pltpu.VMEM((B, 128), F32)],
        compiler_params=pltpu.CompilerParams(vmem_limit_bytes=16 << 20),
        name="second",
    )(pivot_tiles, inv0, w10, w11)

    received = [by_q[q][r][k] for q in range(1, 4) for r in range(2) for k in range(2)]
    factor, work, zero = pl.pallas_call(
        panel_kernel,
        out_shape=(jax.ShapeDtypeStruct((1, 2, 1, T, 2 * T), F32),) + tiles(TILES) + (jax.ShapeDtypeStruct((T, T), F32),),
        in_specs=[SMEM, SMEM] + [VMEM] * 16,
        out_specs=(VMEM, VMEM, VMEM),
        scratch_shapes=[pltpu.VMEM((8, T, 2 * T), BF16), pltpu.VMEM((8, T, 2 * T), BF16)],
        compiler_params=pltpu.CompilerParams(vmem_limit_bytes=40 << 20),
        name="panel",
    )(place.reshape(1), tile[0:1], inv0, l10, inv1, front, *received)
    ancestor = lax.cond(over[0, 0] > 0.0, dense, sparse, work, zero, tile, table[2], codes, where, a, b, c)
    return (factor, ancestor.reshape(1, 1, ASLOT, T, T))


def solution(mesh):
    in_specs = (P("leaf", None, "front", None, None), P("leaf"), P("leaf", "front", None, None))
    out_specs = (P("leaf", None, "front", None, None), P("leaf", "front", None, None, None))
    return jax.shard_map(local, mesh=mesh, in_specs=in_specs, out_specs=out_specs, check_vma=False)
```

```python
import functools

import jax
import jax.numpy as jnp
from jax import lax
from jax.experimental import pallas as pl
from jax.experimental.pallas import tpu as pltpu
from jax.sharding import PartitionSpec as P

PT = 2
ASLOT = 16
TILES = 14
N1, N2 = 15, 10
FY1, FY2 = 9, 6
FZ3, FZ4 = 10, 7
NY1, NY2 = 18, 12
BUF, ZN1, ZN2, YF1, YF2, YN1, YN2, ZF3, ZF4, ROOT = range(10)
N_CUT = (0, 5, 10, 15)
FY_CUT = (0, 6, 9)
FZ_CUT = (0, 4, 7, 10)
NY_CUT = (0, 6, 12, 18)
B = 64
T = 256
F32 = jnp.float32
BF16 = jnp.bfloat16
HIGHEST = lax.Precision.HIGHEST
VMEM = pl.BlockSpec(memory_space=pltpu.VMEM)
SMEM = pl.BlockSpec(memory_space=pltpu.SMEM)
ANY = pl.BlockSpec(memory_space=pl.ANY)
NN = (((1,), (0,)), ((), ()))
NT = (((1,), (1,)), ((), ()))
TN = (((0,), (0,)), ((), ()))


def dot(a, b, dims):
    return lax.dot_general(a, b, dims, precision=HIGHEST, preferred_element_type=F32)


def dot1(a, b, dims):
    return lax.dot_general(a, b, dims, preferred_element_type=F32)


def split(x):
    high = x.astype(BF16)
    return high, (x - high.astype(F32)).astype(BF16)


def split3(x):
    high = x.astype(BF16)
    rest = x - high.astype(F32)
    mid = rest.astype(BF16)
    return high, mid, (rest - mid.astype(F32)).astype(BF16)


def dot3(a, b, dims):
    ah, al = a
    bh, bl = b
    return dot1(ah, bh, dims) + (dot1(ah, bl, dims) + dot1(al, bh, dims))


def factor64(groups, f_ref):
    sub = lax.broadcasted_iota(jnp.int32, (8, 128), 0)

    def body(it, gs):
        cols = [[jnp.broadcast_to(g[:, t:t + 1], (8, 128)) for t in range(8)] for g in gs]
        rows = [jnp.broadcast_to(gs[0][t:t + 1, :], (8, 128)) for t in range(8)]
        s = [[jnp.broadcast_to(cols[0][t][u:u + 1, :], (8, 128)) if u >= t else None for t in range(8)] for u in range(8)]
        inv = [None] * 8
        for t in range(8):
            inv[t] = 1.0 / s[t][t]
            for u in range(t + 1, 8):
                low = s[u][t] * inv[t]
                for v in range(u, 8):
                    s[v][u] = s[v][u] - low * s[v][t]
                rows[u] = rows[u] - low * rows[t]
                for g in range(1, 8):
                    cols[g][u] = cols[g][u] - low * cols[g][t]
        done = jnp.zeros((8, 128), F32)
        for t in range(8):
            done = jnp.where(sub == t, rows[t] * lax.rsqrt(s[t][t]), done)
        f_ref[pl.ds(pl.multiple_of(it * 8, 8), 8), :] = pltpu.roll(done, it * 8, 1)
        scaled = [rows[t] * inv[t] for t in range(8)]
        left = []
        for g in range(1, 8):
            piece = gs[g]
            for t in range(8):
                piece = piece - cols[g][t] * scaled[t]
            left.append(pltpu.roll(piece, 120, 1))
        left.append(gs[0])
        return tuple(left)

    lax.fori_loop(0, 8, body, tuple(groups))


def factor256(x_ref, f_ref):
    lane = lax.broadcasted_iota(jnp.int32, (B, 128), 1)
    row = lax.broadcasted_iota(jnp.int32, (B, 128), 0)
    ident = (lane - B == row).astype(F32)
    col = lax.broadcasted_iota(jnp.int32, (B, T), 1)
    wide_row = lax.broadcasted_iota(jnp.int32, (B, T), 0)
    for k in range(T // B):
        lo = k * B
        strip = x_ref[lo:lo + B, :]
        block = strip[:, (k // 2) * 128:(k // 2) * 128 + 128]
        if k % 2:
            block = pltpu.roll(block, B, 1)
        both = jnp.where(lane < B, block, ident)
        factor64([both[8 * g:8 * g + 8, :] for g in range(8)], f_ref)
        block_inv = f_ref[...][:, B:]
        inside = (col >= lo) & (col < lo + B)
        strip = jnp.where(inside, (col - lo == wide_row).astype(F32), strip)
        out = dot(block_inv, strip, NN)
        x_ref[lo:lo + B, :] = jnp.where(col < lo + B, out, 0.0)
        if lo + B < T:
            rest = T - lo - B
            rest_col = lax.broadcasted_iota(jnp.int32, (rest, T), 1)
            old = x_ref[lo + B:, :]
            old = jnp.where((rest_col >= lo) & (rest_col < lo + B), 0.0, old)
            x_ref[lo + B:, :] = old - dot(out[:, lo + B:], out, TN)


def first_kernel(w00_ref, inv0_ref, f_ref):
    inv0_ref[...] = w00_ref[...]
    factor256(inv0_ref, f_ref)


def second_kernel(piv_ref, inv0_ref, w10_ref, w11_ref, l10_ref, inv1_ref, f_ref):
    l10 = dot(w10_ref[...], inv0_ref[...], NT)
    l10_ref[...] = l10
    inv1_ref[...] = jnp.zeros((T, T), F32)

    @pl.when(piv_ref[0] >= 2)
    def _():
        inv1_ref[...] = w11_ref[...] - dot(l10, l10, NT)
        factor256(inv1_ref, f_ref)


def iota(shape, dim):
    return lax.broadcasted_iota(jnp.int32, shape, dim)


def fdot(a, b):
    return lax.dot_general(a, b, (((1,), (0,)), ((), ())), preferred_element_type=F32)


def route(codes, z, y, c):
    shape, sq, rows = (32, 128), (128, 128), (32, 32)
    row, lane = iota(shape, 0), iota(shape, 1)
    zs, ys = row // 4, row % 4
    cs, zd, yd, cd = lane // 64, (lane // 8) % 8, (lane // 2) % 4, lane % 2
    dz, dy = (zd - zs + 8) % 8, (yd - ys + 4) % 4
    hops = jnp.minimum(dz, 8 - dz)
    far = hops > 2
    live = (codes >= 0) & ~((lane % 64 == 0) & far)
    tile = jnp.where(live, codes // 16, 0)
    slot = jnp.where(live, codes % 16, 0)
    la, lb = iota(sq, 0), iota(sq, 1)
    before = la < lb
    same_zd = (la // 8) % 8 == (lb // 8) % 8
    same_yd = (la // 2) % 4 == (lb // 2) % 4
    ra, rb = iota(rows, 0), iota(rows, 1)
    same_ys = ra % 4 == rb % 4
    same_zs = ra // 4 == rb // 4

    def f(x):
        return x.astype(F32)

    def count(mask, lanes, peers):
        rank = fdot(f(mask), f(before & lanes))
        total = fdot(f(mask), f(lanes))
        if peers is not None:
            rank = rank + fdot(f(peers & (rb < ra)), total)
            total = fdot(f(peers), total)
        return rank, total

    def halves(n_up, n_both, n_down):
        up = jnp.clip(jnp.floor((n_both + n_down - n_up + 1.0) * 0.5), 0.0, n_both)
        return up, n_both - up

    every = la >= 0
    over = jnp.full(shape, -1.0, F32)
    r1, n1 = count(live & (dz == 1), every, None)
    r2, n2 = count(live & (dz == 2), every, None)
    r6, n6 = count(live & (dz == 6), every, None)
    r7, n7 = count(live & (dz == 7), every, None)
    zpos = jnp.where(dz == 1, n2 + r1, jnp.where(dz == 2, r2, jnp.where(dz == 6, r6, n6 + r7)))
    over = jnp.maximum(over, jnp.maximum(n1 + n2, n7 + n6) - N1)
    over = jnp.maximum(over, jnp.maximum(n2, n6) - N2)

    def ring(mask, lanes, peers, near, distant):
        a1, m1 = count(mask & (dy == 1), lanes, peers)
        a2, m2 = count(mask & (dy == 2), lanes, peers)
        a3, m3 = count(mask & (dy == 3), lanes, peers)
        up, down = halves(m1, m2, m3)
        minus = (dy == 3) | ((dy == 2) & (a2 >= up))
        pos = jnp.where(dy == 1, up + a1, jnp.where(dy == 3, down + a3, jnp.where(a2 < up, a2, a2 - up)))
        excess = jnp.maximum(jnp.maximum(up + m1, down + m3) - near, jnp.maximum(up, down) - distant)
        return minus.astype(jnp.int32), pos.astype(jnp.int32), excess

    fy_core, fy_pos, excess = ring(live & far, every, None, FY1, FY2)
    over = jnp.maximum(over, excess)
    r3, n3 = count(live & (dz == 3), same_yd, same_zs)
    r4, n4 = count(live & (dz == 4), same_yd, same_zs)
    r5, n5 = count(live & (dz == 5), same_yd, same_zs)
    up, down = halves(n3, n4, n5)
    fz_pos = jnp.where(dz == 3, up + r3, jnp.where(dz == 5, down + r5, jnp.where(r4 < up, r4, r4 - up)))
    over = jnp.maximum(over, jnp.maximum(up + n3, down + n5) - FZ3)
    over = jnp.maximum(over, jnp.maximum(up, down) - FZ4)
    z_core = ((dz > 4) | ((dz == 4) & (r4 >= up))).astype(jnp.int32)
    ny_core, ny_pos, excess = ring(live & ~far, same_zd, same_ys, NY1, NY2)
    over = jnp.maximum(over, excess)
    zpos, fz_pos = zpos.astype(jnp.int32), fz_pos.astype(jnp.int32)

    def source(kind, core, held):
        return (kind * 2 + (core != c)) * 32 + held

    here = live & (row == z * 4 + y)
    queued = jnp.sum(jnp.where(here & ~far & (dz > 0) & (z_core == c), source(BUF, cs, tile) * 32 + zpos + 1, 0), axis=0, keepdims=True) - 1
    queued_far = jnp.sum(jnp.where(here & far & (dy > 0) & (fy_core == c), source(BUF, cs, tile) * 32 + fy_pos + 1, 0), axis=0, keepdims=True) - 1
    after_y = jnp.where(dy == 0, source(BUF, cs, tile), source(jnp.where(dy == 2, YF2, YF1), fy_core, fy_pos))
    turn_far = jnp.where(live & far & (zs == z) & (yd == y) & (z_core == c), after_y * 32 + fz_pos, -1)
    after_z = jnp.where(dz == 0, source(BUF, cs, tile), source(jnp.where(hops == 1, ZN1, ZN2), z_core, zpos))
    turn_near = jnp.where(live & ~far & (zd == z) & (ys == y) & (dy > 0) & (ny_core == c), after_z * 32 + ny_pos, -1)
    end_near = jnp.where(dy == 0, after_z, source(jnp.where(dy == 2, YN2, YN1), ny_core, ny_pos))
    end_far = source(jnp.where(dz == 4, ZF4, ZF3), z_core, fz_pos)
    mine = live & (zd == z) & (yd == y) & (cd == c)
    end = jnp.where(mine, jnp.where(far, end_far, end_near) * 16 + slot, -1)
    return queued, queued_far, turn_near, turn_far, end, jnp.max(over, keepdims=True)


def plan_kernel(where_ref, codes_ref, *out_refs):
    for ref, value in zip(out_refs, route(codes_ref[...], where_ref[0], where_ref[1], where_ref[2])):
        ref[...] = value


def panel_kernel(place_ref, first_ref, inv0_ref, l10_ref, inv1_ref, front_ref, *refs):
    pieces = refs[:12]
    factor_ref, out_ref, zero_ref, yh_ref, yl_ref = refs[12:]
    place = place_ref[0]
    a0 = split3(inv0_ref[...])
    low = split(l10_ref[...])
    inv1 = inv1_ref[...]
    for q in range(4):
        for r in range(2):
            if q == 0:
                p0 = front_ref[0, r, 0, :, 0:T]
                p1 = front_ref[0, r, 0, :, T:2 * T].astype(F32)
            else:
                p0 = pieces[(q - 1) * 4 + r * 2][...].astype(BF16)
                p1 = pieces[(q - 1) * 4 + r * 2 + 1][...]
            y0 = dot1(p0, a0[0], NT) + (dot1(p0, a0[1], NT) + dot1(p0, a0[2], NT))
            y0h, y0l = split(y0)
            p1 = p1 - dot3((y0h, y0l), low, NT)
            y1 = dot(p1, inv1, NT)
            if r == 0:
                owner = lax.rem(place + q, 4)
                y1 = jnp.where(owner > 0, y1, 0.0)
            y1h, y1l = split(y1)
            n = q * 2 + r
            yh_ref[n, :, 0:T] = y0h
            yl_ref[n, :, 0:T] = y0l
            yh_ref[n, :, T:2 * T] = y1h
            yl_ref[n, :, T:2 * T] = y1l
            if q == 0:
                factor_ref[0, r, 0, :, 0:T] = y0
                factor_ref[0, r, 0, :, T:2 * T] = y1
    for r in range(2):
        for n in range(8):
            column = lax.rem(place + n // 2, 4) + 4 * (n % 2)

            @pl.when(column > 0)
            def _():
                start = pl.multiple_of(column * T, T)
                tile = front_ref[0, r, 0, :, pl.ds(start, T)].astype(F32)
                own = (yh_ref[r], yl_ref[r])
                other = (yh_ref[n], yl_ref[n])
                tile = tile - dot3(own, other, NT)
                index = r * 7 + column - 1
                out_ref[index] = tile

                @pl.when(index == first_ref[0])
                def _():
                    zero_ref[...] = tile


def pieces_of(kind, cut, own, sib=None):
    spans = [(kind * 2, lo, hi, x) for lo, hi, x in zip(cut, cut[1:], own)]
    if sib is not None:
        spans += [(kind * 2 + 1, lo, hi, x) for lo, hi, x in zip(cut, cut[1:], sib)]
    return spans


def copy_from(sources, source, held, target_ref, sem):
    for sid, lo, hi, ref in sources:
        @pl.when((source == sid) & (held >= lo) & (held < hi))
        def _():
            pltpu.make_async_copy(ref.at[held - lo], target_ref, sem).start()


def gather_kernel(spans, cut, entries, where_ref, table_ref, *refs):
    sources = [span + (ref,) for span, ref in zip(spans, refs)]
    outs = refs[len(spans):-1]
    sem = refs[-1]

    def each(act):
        def body(e, _):
            code = table_ref[entries(e, where_ref[0], where_ref[1], where_ref[2])]

            @pl.when(code >= 0)
            def _():
                act(code // 1024, (code // 32) % 32, code % 32)
            return 0

        lax.fori_loop(0, 128, body, 0)

    def start(source, held, pos):
        for lo, hi, out in zip(cut, cut[1:], outs):
            @pl.when((pos >= lo) & (pos < hi))
            def _():
                copy_from(sources, source, held, out.at[pos - lo], sem.at[pos])

    def wait(source, held, pos):
        pltpu.make_async_copy(refs[0].at[0], outs[0].at[0], sem.at[pos]).wait()

    each(start)
    each(wait)


def chip_entries(e, z, y, c):
    return 0, e


def near_entries(e, z, y, c):
    return (e // 16) * 4 + y, ((e // 8) % 2) * 64 + z * 8 + e % 8


def far_entries(e, z, y, c):
    return z * 4 + e // 32, (e // 2 % 16) * 8 + y * 2 + e % 2


def gather(where, table, spans, cut, entries, name):
    return pl.pallas_call(
        lambda *refs: gather_kernel([span[:3] for span in spans], cut, entries, *refs),
        out_shape=tiles(*[hi - lo for lo, hi in zip(cut, cut[1:])]),
        in_specs=[SMEM, SMEM] + [ANY] * len(spans),
        out_specs=(VMEM,) * (len(cut) - 1),
        scratch_shapes=[pltpu.SemaphoreType.DMA((cut[-1],))],
        compiler_params=pltpu.CompilerParams(vmem_limit_bytes=16 << 20),
        name=name,
    )(where, table, *[span[3] for span in spans])


DEPTH = 8


def sum_kernel(spans, first, last, where_ref, table_ref, codes_ref, base_ref, *refs):
    z, y, c = where_ref[0], where_ref[1], where_ref[2]
    sources = [span + (ref,) for span, ref in zip(spans, refs)]
    out_ref, list_ref, buf_ref, sem = refs[len(spans):]
    if first == BUF:
        out_ref[...] = jnp.zeros_like(out_ref)
    else:
        out_ref[...] = base_ref[...]

    def collect(i, n):
        code = table_ref[i // 2, (i % 2) * 64 + z * 8 + y * 2 + c]
        kind = code // 1024
        take = (code >= 0) & (kind >= first) & (kind <= last)

        @pl.when(take)
        def _():
            list_ref[n] = code
        return n + take.astype(jnp.int32)

    n = lax.fori_loop(0, 64, collect, jnp.int32(0))
    if first == BUF:
        def collect_root(i, n):
            code = codes_ref[12 + i // 2, (i % 2) * 64]
            list_ref[n] = ((ROOT + (i // 2) % 4) * 64 + (i // 8) * 2 + i % 2) * 16 + code % 16
            return n + 1

        n = lax.fori_loop(0, jnp.where((z == 0) & (y == 0) & (c == 0), 24, 0), collect_root, n)

    def start(i):
        code = list_ref[i]
        slot = lax.rem(i, DEPTH)
        copy_from(sources, code // 512, (code // 16) % 32, buf_ref.at[slot], sem.at[slot])

    def prime(i, _):
        start(i)
        return 0

    def step(i, _):
        slot = lax.rem(i, DEPTH)
        pltpu.make_async_copy(refs[0].at[0], buf_ref.at[slot], sem.at[slot]).wait()
        out_ref[list_ref[i] % 16] += buf_ref[slot]

        @pl.when(i + DEPTH < n)
        def _():
            start(i + DEPTH)
        return 0

    lax.fori_loop(0, jnp.minimum(n, DEPTH), prime, 0)
    lax.fori_loop(0, n, step, 0)


def add_up(where, table, codes, base, spans, first, last, name):
    return pl.pallas_call(
        lambda *refs: sum_kernel([span[:3] for span in spans], first, last, *refs),
        out_shape=tiles(ASLOT)[0],
        in_specs=[SMEM, SMEM, SMEM, VMEM] + [ANY] * len(spans),
        out_specs=VMEM,
        scratch_shapes=[pltpu.SMEM((256,), jnp.int32), pltpu.VMEM((DEPTH, T, T), F32), pltpu.SemaphoreType.DMA((DEPTH,))],
        compiler_params=pltpu.CompilerParams(vmem_limit_bytes=32 << 20),
        name=name,
    )(where, table, codes, base, *[span[3] for span in spans])


def slots_kernel(tile_ref, own_ref, out_ref, sem):
    def start(p, _):
        tile = tile_ref[p]

        @pl.when(tile >= 0)
        def _():
            pltpu.make_async_copy(own_ref.at[tile], out_ref.at[p], sem.at[p]).start()
        return 0

    def wait(p, _):
        @pl.when(tile_ref[p] >= 0)
        def _():
            pltpu.make_async_copy(own_ref.at[0], out_ref.at[p], sem.at[p]).wait()
        return 0

    lax.fori_loop(0, 64, start, 0)
    lax.fori_loop(0, 64, wait, 0)


def add_kernel(target_ref, arrived_ref, out_ref):
    step = pl.program_id(0)

    @pl.when(step == 0)
    def _():
        out_ref[...] = jnp.zeros_like(out_ref)

    for i in range(4):
        target = target_ref[step * 4 + i]

        @pl.when(target >= 0)
        def _():
            out_ref[target] += arrived_ref[i]


def tiles(*counts):
    return tuple(jax.ShapeDtypeStruct((n, T, T), F32) for n in counts)


def leaf_id(z, y, c):
    return ((z % 8) * 4 + y % 4) * 2 + c


PLACES = [(z, y, c) for z in range(8) for y in range(4) for c in range(2)]


def send(x, pairs):
    return lax.ppermute(x, "leaf", [(leaf_id(*a), leaf_id(*b)) for a, b in pairs])


def dense(work, zero, tile, slot, codes, where, *tables):
    outgoing = pl.pallas_call(
        slots_kernel,
        out_shape=tiles(64)[0],
        in_specs=[SMEM, ANY],
        out_specs=ANY,
        scratch_shapes=[pltpu.SemaphoreType.DMA((64,))],
        name="slots",
    )(tile, work)
    arrived = lax.all_to_all(outgoing, "leaf", split_axis=0, concat_axis=0, tiled=True)
    targets = lax.all_to_all(slot, "leaf", split_axis=0, concat_axis=0, tiled=True)
    return pl.pallas_call(
        add_kernel,
        out_shape=tiles(ASLOT)[0],
        grid=(16,),
        in_specs=[SMEM, pl.BlockSpec((4, T, T), lambda i: (i, 0, 0))],
        out_specs=pl.BlockSpec((ASLOT, T, T), lambda i: (0, 0, 0)),
        compiler_params=pltpu.CompilerParams(vmem_limit_bytes=32 << 20),
        name="add",
    )(targets, arrived)


def tie(x, *others):
    return lax.optimization_barrier((x,) + others)[0]


def sparse(work, zero, tile, slot, codes, where, queued, queued_far, turn_near, turn_far, end):
    swap = [((z, y, c), (z, y, 1 - c)) for z, y, c in PLACES]
    along_z = [((z, y, c), (z + 1 - 2 * c, y, c)) for z, y, c in PLACES]
    along_y = [((z, y, c), (z, y + 1 - 2 * c, c)) for z, y, c in PLACES]

    def sends(xs, pairs):
        return [send(x, pairs) for x in xs]

    def after(xs, *others):
        n = len(xs)
        return list(lax.optimization_barrier(tuple(xs) + others)[:n])

    other = send(work, swap)
    root = [send(zero, [((z, y, c), (0, y, 0)) for y in range(4)]) for z in (3, 4, 5) for c in range(2)]
    both = pieces_of(BUF, (0, TILES), [work], [other])
    far_out = gather(where, queued_far, both, FY_CUT, chip_entries, "queue_far")
    near_out = gather(where, queued, both, N_CUT, chip_entries, "queue")
    near_out, far_out = after(near_out, *far_out), after(far_out, *near_out)
    n1 = sends(near_out, along_z)
    f1 = sends(far_out, along_y)
    f2 = sends(after(f1[:1], f1[1]), along_y)
    n2 = sends(after(n1[:2], n1[2], *f1), along_z)
    f1_other, f2_other, n1_other = sends(f1, swap), sends(f2, swap), sends(n1, swap)
    lists = gather(
        where, turn_far,
        both + pieces_of(YF1, FY_CUT, f1, f1_other) + pieces_of(YF2, FY_CUT[:2], f2, f2_other),
        FZ_CUT, far_entries, "turn_far")
    z1 = sends(after(lists, *n2), along_z)
    n2_other = sends(n2, swap)
    near_spans = both + pieces_of(ZN1, N_CUT, n1, n1_other) + pieces_of(ZN2, N_CUT[:3], n2, n2_other)
    lists = gather(where, turn_near, near_spans, NY_CUT, near_entries, "turn_near")
    column = jnp.stack(after(root, *n2))
    pass_on = send(column, [((0, 2, 0), (0, 1, 0))])
    row1 = send(column, [((0, 1, 0), (0, 0, 0))])
    row3 = send(column, [((0, 3, 0), (0, 0, 0))])
    row2 = send(pass_on, [((0, 1, 0), (0, 0, 0))])
    z2 = sends(after(z1, *lists, row1, row3), along_z)
    y1 = sends(lists[:2], along_y)
    y1 += sends(after(lists[2:], *z2, row2), along_y)
    z3 = sends(z2, along_z)
    y2 = sends(y1[:2], along_y)
    y1_other = sends(y1, swap)
    z4 = sends(after(z3, *y1)[:2], along_z)
    y2_other = sends(y2, swap)
    z3_other = sends(z3, swap)
    roots = [(2 * ROOT + 2 * i, 0, 6, x) for i, x in enumerate((column, row1, row2, row3))]
    spans = near_spans + pieces_of(YN1, NY_CUT, y1, y1_other) + pieces_of(YN2, NY_CUT[:3], y2, y2_other) + roots
    base = add_up(where, end, codes, jnp.zeros((8, 128), F32), spans, BUF, YN2, "sum_near")
    z4_other = sends(z4, swap)
    spans = pieces_of(ZF3, FZ_CUT, z3, z3_other) + pieces_of(ZF4, FZ_CUT[:3], z4, z4_other)
    return add_up(where, end, codes, base, spans, ZF3, ZF4, "sum_far")


def local(front, pivot_tiles, send_table):
    place = lax.axis_index("front").astype(jnp.int32)
    leaf = lax.axis_index("leaf").astype(jnp.int32)
    where = jnp.stack([leaf // 8, (leaf // 2) % 4, leaf % 2])
    table = send_table[0, 0]
    used = table[0] >= 0
    tile = jnp.where(used, table[0] * 7 + table[1] - 1, -1)
    code = jnp.where(used, tile * 16 + table[2], -1)
    wide = jnp.pad(code.astype(F32).reshape(1, 64), ((0, 7), (0, 64)))
    codes = lax.all_gather(wide, "leaf")[:, 0, :64].reshape(32, 128).astype(jnp.int32)
    up = [(i, (i + 1) % 4) for i in range(4)]
    down = [(i, (i - 1) % 4) for i in range(4)]
    own = [[front[0, r, 0, :, k * T:k * T + T].astype(F32) for k in range(2)] for r in range(2)]
    from_left = [[None, None], [None, None]]
    from_right = [[None, None], [None, None]]
    from_far = [[None, None], [None, None]]
    from_left[0][0] = lax.ppermute(own[0][0], "front", up)
    from_right[0][0] = lax.ppermute(own[0][0], "front", down)
    from_far[0][0] = lax.ppermute(from_left[0][0], "front", up)
    from_right[0][1] = lax.ppermute(tie(own[0][1], from_left[0][0], from_right[0][0]), "front", down)
    from_left[0][1] = lax.ppermute(tie(own[0][1], from_far[0][0]), "front", up)
    from_far[0][1] = lax.ppermute(from_right[0][1], "front", down)
    for k in range(2):
        from_left[1][k] = lax.ppermute(tie(own[1][k], from_far[0][0]), "front", up)
        from_right[1][k] = lax.ppermute(tie(own[1][k], from_far[0][0]), "front", down)
    from_far[1][0] = lax.ppermute(from_left[1][0], "front", up)
    from_far[1][1] = lax.ppermute(from_right[1][1], "front", down)
    by_q = [own, from_right, from_far, from_left]

    def of_owner(owner, r, k, *after):
        q = lax.rem(owner - place + 4, 4)
        if after:
            q = tie(q, *after)
        out = by_q[0][r][k]
        for i in range(1, 4):
            out = jnp.where(q == i, by_q[i][r][k], out)
        return out

    inv0 = pl.pallas_call(
        first_kernel,
        out_shape=jax.ShapeDtypeStruct((T, T), F32),
        in_specs=[VMEM],
        out_specs=VMEM,
        scratch_shapes=[pltpu.VMEM((B, 128), F32)],
        compiler_params=pltpu.CompilerParams(vmem_limit_bytes=16 << 20),
        name="first",
    )(of_owner(0, 0, 0))
    *tables, over = pl.pallas_call(
        plan_kernel,
        out_shape=tuple(jax.ShapeDtypeStruct((n, 128), jnp.int32) for n in (1, 1, 32, 32, 32)) + (jax.ShapeDtypeStruct((1, 1), F32),),
        in_specs=[SMEM, VMEM],
        out_specs=(VMEM,) * 6,
        name="plan",
    )(where, tie(codes, inv0))
    over = jnp.maximum(over, tie(lax.ppermute(over, "front", up), inv0))
    across = lax.ppermute(over, "front", [(i, (i + 2) % 4) for i in range(4)])

    w10 = of_owner(1, 0, 0, inv0)
    w11 = of_owner(1, 0, 1, inv0)
    l10, inv1 = pl.pallas_call(
        second_kernel,
        out_shape=(jax.ShapeDtypeStruct((T, T), F32),) * 2,
        in_specs=[SMEM, VMEM, VMEM, VMEM],
        out_specs=(VMEM, VMEM),
        scratch_shapes=[pltpu.VMEM((B, 128), F32)],
        compiler_params=pltpu.CompilerParams(vmem_limit_bytes=16 << 20),
        name="second",
    )(pivot_tiles, inv0, w10, w11)

    received = [by_q[q][r][k] for q in range(1, 4) for r in range(2) for k in range(2)]
    factor, work, zero = pl.pallas_call(
        panel_kernel,
        out_shape=(jax.ShapeDtypeStruct((1, 2, 1, T, 2 * T), F32),) + tiles(TILES) + (jax.ShapeDtypeStruct((T, T), F32),),
        in_specs=[SMEM, SMEM] + [VMEM] * 16,
        out_specs=(VMEM, VMEM, VMEM),
        scratch_shapes=[pltpu.VMEM((8, T, 2 * T), BF16), pltpu.VMEM((8, T, 2 * T), BF16)],
        compiler_params=pltpu.CompilerParams(vmem_limit_bytes=40 << 20),
        name="panel",
    )(place.reshape(1), tile[0:1], inv0, l10, inv1, front, *received)
    over = jnp.maximum(over, tie(across, zero))
    ancestor = lax.cond(over[0, 0] > 0.0, dense, sparse, work, zero, tile, table[2], codes, where, *tables)
    return (factor, ancestor.reshape(1, 1, ASLOT, T, T))


def solution(mesh):
    in_specs = (P("leaf", None, "front", None, None), P("leaf"), P("leaf", "front", None, None))
    out_specs = (P("leaf", None, "front", None, None), P("leaf", "front", None, None, None))
    return jax.shard_map(local, mesh=mesh, in_specs=in_specs, out_specs=out_specs, check_vma=False)
```

```python
import functools

import jax
import jax.numpy as jnp
from jax import lax
from jax.experimental import pallas as pl
from jax.experimental.pallas import tpu as pltpu
from jax.sharding import PartitionSpec as P

PT = 2
ASLOT = 16
TILES = 14
N1, N2 = 8, 5
FY1, FY2 = 5, 3
FZ = 5
NY1, NY2 = 9, 6
BUF, ZN1, ZN2, YF1, YF2, YN1, YN2, ZF3, ZF4, ROOT = range(10)
B = 64
T = 256
F32 = jnp.float32
BF16 = jnp.bfloat16
HIGHEST = lax.Precision.HIGHEST
VMEM = pl.BlockSpec(memory_space=pltpu.VMEM)
SMEM = pl.BlockSpec(memory_space=pltpu.SMEM)
ANY = pl.BlockSpec(memory_space=pl.ANY)
NN = (((1,), (0,)), ((), ()))
NT = (((1,), (1,)), ((), ()))
TN = (((0,), (0,)), ((), ()))


def dot(a, b, dims):
    return lax.dot_general(a, b, dims, precision=HIGHEST, preferred_element_type=F32)


def dot1(a, b, dims):
    return lax.dot_general(a, b, dims, preferred_element_type=F32)


def split(x):
    high = x.astype(BF16)
    return high, (x - high.astype(F32)).astype(BF16)


def split3(x):
    high = x.astype(BF16)
    rest = x - high.astype(F32)
    mid = rest.astype(BF16)
    return high, mid, (rest - mid.astype(F32)).astype(BF16)


def dot3(a, b, dims):
    ah, al = a
    bh, bl = b
    return dot1(ah, bh, dims) + (dot1(ah, bl, dims) + dot1(al, bh, dims))


def factor64(groups, f_ref):
    sub = lax.broadcasted_iota(jnp.int32, (8, 128), 0)

    def body(it, gs):
        cols = [[jnp.broadcast_to(g[:, t:t + 1], (8, 128)) for t in range(8)] for g in gs]
        rows = [jnp.broadcast_to(gs[0][t:t + 1, :], (8, 128)) for t in range(8)]
        s = [[jnp.broadcast_to(cols[0][t][u:u + 1, :], (8, 128)) if u >= t else None for t in range(8)] for u in range(8)]
        inv = [None] * 8
        for t in range(8):
            inv[t] = 1.0 / s[t][t]
            for u in range(t + 1, 8):
                low = s[u][t] * inv[t]
                for v in range(u, 8):
                    s[v][u] = s[v][u] - low * s[v][t]
                rows[u] = rows[u] - low * rows[t]
                for g in range(1, 8):
                    cols[g][u] = cols[g][u] - low * cols[g][t]
        done = jnp.zeros((8, 128), F32)
        for t in range(8):
            done = jnp.where(sub == t, rows[t] * lax.rsqrt(s[t][t]), done)
        f_ref[pl.ds(pl.multiple_of(it * 8, 8), 8), :] = pltpu.roll(done, it * 8, 1)
        scaled = [rows[t] * inv[t] for t in range(8)]
        left = []
        for g in range(1, 8):
            piece = gs[g]
            for t in range(8):
                piece = piece - cols[g][t] * scaled[t]
            left.append(pltpu.roll(piece, 120, 1))
        left.append(gs[0])
        return tuple(left)

    lax.fori_loop(0, 8, body, tuple(groups))


def factor256(x_ref, f_ref):
    lane = lax.broadcasted_iota(jnp.int32, (B, 128), 1)
    row = lax.broadcasted_iota(jnp.int32, (B, 128), 0)
    ident = (lane - B == row).astype(F32)
    col = lax.broadcasted_iota(jnp.int32, (B, T), 1)
    wide_row = lax.broadcasted_iota(jnp.int32, (B, T), 0)
    for k in range(T // B):
        lo = k * B
        strip = x_ref[lo:lo + B, :]
        block = strip[:, (k // 2) * 128:(k // 2) * 128 + 128]
        if k % 2:
            block = pltpu.roll(block, B, 1)
        both = jnp.where(lane < B, block, ident)
        factor64([both[8 * g:8 * g + 8, :] for g in range(8)], f_ref)
        block_inv = f_ref[...][:, B:]
        inside = (col >= lo) & (col < lo + B)
        strip = jnp.where(inside, (col - lo == wide_row).astype(F32), strip)
        out = dot(block_inv, strip, NN)
        x_ref[lo:lo + B, :] = jnp.where(col < lo + B, out, 0.0)
        if lo + B < T:
            rest = T - lo - B
            rest_col = lax.broadcasted_iota(jnp.int32, (rest, T), 1)
            old = x_ref[lo + B:, :]
            old = jnp.where((rest_col >= lo) & (rest_col < lo + B), 0.0, old)
            x_ref[lo + B:, :] = old - dot(out[:, lo + B:], out, TN)


def first_kernel(w00_ref, inv0_ref, f_ref):
    inv0_ref[...] = w00_ref[...]
    factor256(inv0_ref, f_ref)


def second_kernel(piv_ref, inv0_ref, w10_ref, w11_ref, l10_ref, inv1_ref, f_ref):
    l10 = dot(w10_ref[...], inv0_ref[...], NT)
    l10_ref[...] = l10
    inv1_ref[...] = jnp.zeros((T, T), F32)

    @pl.when(piv_ref[0] >= 2)
    def _():
        inv1_ref[...] = w11_ref[...] - dot(l10, l10, NT)
        factor256(inv1_ref, f_ref)


def iota(shape, dim):
    return lax.broadcasted_iota(jnp.int32, shape, dim)


def fdot(a, b):
    return lax.dot_general(a, b, (((1,), (0,)), ((), ())), preferred_element_type=F32)


def route(codes, z, y, c):
    shape, sq, rows = (32, 128), (128, 128), (32, 32)
    row, lane = iota(shape, 0), iota(shape, 1)
    zs, ys = row // 4, row % 4
    cs, zd, yd, cd = lane // 64, (lane // 8) % 8, (lane // 2) % 4, lane % 2
    dz, dy = (zd - zs + 8) % 8, (yd - ys + 4) % 4
    hops = jnp.minimum(dz, 8 - dz)
    far = hops > 2
    live = (codes >= 0) & ~((lane % 64 == 0) & far)
    tile = jnp.where(live, codes // 16, 0)
    slot = jnp.where(live, codes % 16, 0)
    la, lb = iota(sq, 0), iota(sq, 1)
    before = la < lb
    same_zd = (la // 8) % 8 == (lb // 8) % 8
    same_yd = (la // 2) % 4 == (lb // 2) % 4
    ra, rb = iota(rows, 0), iota(rows, 1)
    same_ys = ra % 4 == rb % 4
    same_zs = ra // 4 == rb // 4

    def f(x):
        return x.astype(F32)

    def count(mask, lanes, peers):
        rank = fdot(f(mask), f(before & lanes))
        total = fdot(f(mask), f(lanes))
        if peers is not None:
            rank = rank + fdot(f(peers & (rb < ra)), total)
            total = fdot(f(peers), total)
        return rank, total

    def halves(n_up, n_both, n_down):
        up = jnp.clip(jnp.floor((n_both + n_down - n_up + 1.0) * 0.5), 0.0, n_both)
        return up, n_both - up

    every = la >= 0
    over = jnp.full(shape, -1.0, F32)
    r1, n1 = count(live & (dz == 1), every, None)
    r2, n2 = count(live & (dz == 2), every, None)
    r6, n6 = count(live & (dz == 6), every, None)
    r7, n7 = count(live & (dz == 7), every, None)
    zpos = jnp.where(dz == 1, n2 + r1, jnp.where(dz == 2, r2, jnp.where(dz == 6, r6, n6 + r7)))
    over = jnp.maximum(over, jnp.maximum(n1 + n2, n7 + n6) - 2 * N1)
    over = jnp.maximum(over, jnp.maximum(n2, n6) - 2 * N2)

    def ring(mask, lanes, peers, near, distant):
        a1, m1 = count(mask & (dy == 1), lanes, peers)
        a2, m2 = count(mask & (dy == 2), lanes, peers)
        a3, m3 = count(mask & (dy == 3), lanes, peers)
        up, down = halves(m1, m2, m3)
        minus = (dy == 3) | ((dy == 2) & (a2 >= up))
        pos = jnp.where(dy == 1, up + a1, jnp.where(dy == 3, down + a3, jnp.where(a2 < up, a2, a2 - up)))
        excess = jnp.maximum(jnp.maximum(up + m1, down + m3) - near, jnp.maximum(up, down) - distant)
        return minus.astype(jnp.int32), pos.astype(jnp.int32), excess

    fy_way, fy_pos, excess = ring(live & far, every, None, 2 * FY1, 2 * FY2)
    over = jnp.maximum(over, excess)
    r3, n3 = count(live & (dz == 3), same_yd, same_zs)
    r4, n4 = count(live & (dz == 4), same_yd, same_zs)
    r5, n5 = count(live & (dz == 5), same_yd, same_zs)
    up, down = halves(n3, n4, n5)
    fz_pos = jnp.where(dz == 3, up + r3, jnp.where(dz == 5, down + r5, jnp.where(r4 < up, r4, r4 - up)))
    over = jnp.maximum(over, jnp.maximum(up + n3, down + n5) - 2 * FZ)
    z_way = ((dz > 4) | ((dz == 4) & (r4 >= up))).astype(jnp.int32)
    ny_way, ny_pos, excess = ring(live & ~far, same_zd, same_ys, 2 * NY1, 2 * NY2)
    over = jnp.maximum(over, excess)
    zpos, fz_pos = zpos.astype(jnp.int32), fz_pos.astype(jnp.int32)

    def at(kind, way, pos):
        return ((kind * 2 + way) * 2 + (pos % 2 != c)) * 16 + pos // 2

    def listed(mask, way, pos, code):
        key = jnp.where(mask & (pos % 2 == c), way * 16 + pos // 2, -1)
        acc = jnp.zeros(shape, jnp.int32)
        for r in range(32):
            acc = acc + jnp.where(key[r:r + 1, :] == row, code[r:r + 1, :] + 1, 0)
        column = jnp.sum(acc, axis=1, keepdims=True)
        return jnp.sum(jnp.where(lane == row, column, 0), axis=0, keepdims=True) - 1

    held = (BUF * 4 + (cs != c)) * 16 + tile
    here = live & (row == z * 4 + y)
    queued = listed(here & ~far & (dz > 0), z_way, zpos, held)
    queued_far = listed(here & far & (dy > 0), fy_way, fy_pos, held)
    after_y = jnp.where(dy == 0, held, at(jnp.where(dy == 2, YF2, YF1), fy_way, fy_pos))
    turn_far = listed(live & far & (zs == z) & (yd == y), z_way, fz_pos, after_y)
    after_z = jnp.where(dz == 0, held, at(jnp.where(hops == 1, ZN1, ZN2), z_way, zpos))
    turn_near = listed(live & ~far & (zd == z) & (ys == y) & (dy > 0), ny_way, ny_pos, after_z)
    end_near = jnp.where(dy == 0, after_z, at(jnp.where(dy == 2, YN2, YN1), ny_way, ny_pos))
    end_far = at(jnp.where(dz == 4, ZF4, ZF3), z_way, fz_pos)
    mine = live & (zd == z) & (yd == y) & (cd == c)
    end = jnp.where(mine, jnp.where(far, end_far, end_near) * 16 + slot, -1)
    return queued, queued_far, turn_near, turn_far, end, jnp.max(over, keepdims=True)


def plan_kernel(where_ref, codes_ref, *out_refs):
    for ref, value in zip(out_refs, route(codes_ref[...], where_ref[0], where_ref[1], where_ref[2])):
        ref[...] = value


def panel_kernel(place_ref, first_ref, inv0_ref, l10_ref, inv1_ref, front_ref, *refs):
    pieces = refs[:12]
    factor_ref, out_ref, zero_ref, yh_ref, yl_ref = refs[12:]
    place = place_ref[0]
    a0 = split3(inv0_ref[...])
    low = split(l10_ref[...])
    inv1 = inv1_ref[...]
    for q in range(4):
        for r in range(2):
            if q == 0:
                p0 = front_ref[0, r, 0, :, 0:T]
                p1 = front_ref[0, r, 0, :, T:2 * T].astype(F32)
            else:
                p0 = pieces[(q - 1) * 4 + r * 2][...].astype(BF16)
                p1 = pieces[(q - 1) * 4 + r * 2 + 1][...]
            y0 = dot1(p0, a0[0], NT) + (dot1(p0, a0[1], NT) + dot1(p0, a0[2], NT))
            y0h, y0l = split(y0)
            p1 = p1 - dot3((y0h, y0l), low, NT)
            y1 = dot(p1, inv1, NT)
            if r == 0:
                owner = lax.rem(place + q, 4)
                y1 = jnp.where(owner > 0, y1, 0.0)
            y1h, y1l = split(y1)
            n = q * 2 + r
            yh_ref[n, :, 0:T] = y0h
            yl_ref[n, :, 0:T] = y0l
            yh_ref[n, :, T:2 * T] = y1h
            yl_ref[n, :, T:2 * T] = y1l
            if q == 0:
                factor_ref[0, r, 0, :, 0:T] = y0
                factor_ref[0, r, 0, :, T:2 * T] = y1
    for r in range(2):
        for n in range(8):
            column = lax.rem(place + n // 2, 4) + 4 * (n % 2)

            @pl.when(column > 0)
            def _():
                start = pl.multiple_of(column * T, T)
                tile = front_ref[0, r, 0, :, pl.ds(start, T)].astype(F32)
                own = (yh_ref[r], yl_ref[r])
                other = (yh_ref[n], yl_ref[n])
                tile = tile - dot3(own, other, NT)
                index = r * 7 + column - 1
                out_ref[index] = tile

                @pl.when(index == first_ref[0])
                def _():
                    zero_ref[...] = tile


def arrays(kind, own, other):
    return [((kind * 2 + way) * 2 + sib, xs[way]) for way in range(len(own)) for sib, xs in ((0, own), (1, other))]


def copy_from(sources, code, target_ref, sem):
    for sid, ref in sources:
        @pl.when(code // 16 == sid)
        def _():
            pltpu.make_async_copy(ref.at[code % 16], target_ref, sem).start()


def gather_kernel(ids, size, table_ref, *refs):
    sources = list(zip(ids, refs))
    outs = refs[len(ids):-1]
    sem = refs[-1]
    for way, out in enumerate(outs):
        def start(i, _):
            code = table_ref[0, way * 16 + i]

            @pl.when(code >= 0)
            def _():
                copy_from(sources, code, out.at[i], sem.at[way * size + i])
            return 0

        lax.fori_loop(0, size, start, 0)
    for way, out in enumerate(outs):
        def wait(i, _):
            @pl.when(table_ref[0, way * 16 + i] >= 0)
            def _():
                pltpu.make_async_copy(refs[0].at[0], out.at[i], sem.at[way * size + i]).wait()
            return 0

        lax.fori_loop(0, size, wait, 0)


def gather(table, sources, size, name):
    return pl.pallas_call(
        lambda *refs: gather_kernel([sid for sid, _ in sources], size, *refs),
        out_shape=tiles(size, size),
        in_specs=[SMEM] + [ANY] * len(sources),
        out_specs=(VMEM,) * 2,
        scratch_shapes=[pltpu.SemaphoreType.DMA((2 * size,))],
        compiler_params=pltpu.CompilerParams(vmem_limit_bytes=16 << 20),
        name=name,
    )(table, *[x for _, x in sources])


DEPTH = 8


def sum_kernel(ids, first, last, where_ref, table_ref, codes_ref, base_ref, *refs):
    z, y, c = where_ref[0], where_ref[1], where_ref[2]
    sources = list(zip(ids, refs))
    out_ref, list_ref, buf_ref, sem = refs[len(ids):]
    if first == BUF:
        out_ref[...] = jnp.zeros_like(out_ref)
    else:
        out_ref[...] = base_ref[...]

    def collect(i, n):
        code = table_ref[i // 2, (i % 2) * 64 + z * 8 + y * 2 + c]
        kind = code // 1024
        take = (code >= 0) & (kind >= first) & (kind <= last)

        @pl.when(take)
        def _():
            list_ref[n] = code
        return n + take.astype(jnp.int32)

    n = lax.fori_loop(0, 64, collect, jnp.int32(0))
    if first == BUF:
        def collect_root(i, n):
            code = codes_ref[12 + i // 2, (i % 2) * 64]
            list_ref[n] = ((ROOT * 4 + i % 2) * 16 + ((i // 2) % 4) * 3 + i // 8) * 16 + code % 16
            return n + 1

        n = lax.fori_loop(0, jnp.where((z == 0) & (y == 0) & (c == 0), 24, 0), collect_root, n)

    def start(i):
        code = list_ref[i]
        slot = lax.rem(i, DEPTH)
        copy_from(sources, code // 16, buf_ref.at[slot], sem.at[slot])

    def prime(i, _):
        start(i)
        return 0

    def step(i, _):
        slot = lax.rem(i, DEPTH)
        pltpu.make_async_copy(refs[0].at[0], buf_ref.at[slot], sem.at[slot]).wait()
        out_ref[list_ref[i] % 16] += buf_ref[slot]

        @pl.when(i + DEPTH < n)
        def _():
            start(i + DEPTH)
        return 0

    lax.fori_loop(0, jnp.minimum(n, DEPTH), prime, 0)
    lax.fori_loop(0, n, step, 0)


def add_up(where, table, codes, base, sources, first, last, name):
    return pl.pallas_call(
        lambda *refs: sum_kernel([sid for sid, _ in sources], first, last, *refs),
        out_shape=tiles(ASLOT)[0],
        in_specs=[SMEM, SMEM, SMEM, VMEM] + [ANY] * len(sources),
        out_specs=VMEM,
        scratch_shapes=[pltpu.SMEM((256,), jnp.int32), pltpu.VMEM((DEPTH, T, T), F32), pltpu.SemaphoreType.DMA((DEPTH,))],
        compiler_params=pltpu.CompilerParams(vmem_limit_bytes=32 << 20),
        name=name,
    )(where, table, codes, base, *[x for _, x in sources])


def slots_kernel(tile_ref, own_ref, out_ref, sem):
    def start(p, _):
        tile = tile_ref[p]

        @pl.when(tile >= 0)
        def _():
            pltpu.make_async_copy(own_ref.at[tile], out_ref.at[p], sem.at[p]).start()
        return 0

    def wait(p, _):
        @pl.when(tile_ref[p] >= 0)
        def _():
            pltpu.make_async_copy(own_ref.at[0], out_ref.at[p], sem.at[p]).wait()
        return 0

    lax.fori_loop(0, 64, start, 0)
    lax.fori_loop(0, 64, wait, 0)


def add_kernel(target_ref, arrived_ref, out_ref):
    step = pl.program_id(0)

    @pl.when(step == 0)
    def _():
        out_ref[...] = jnp.zeros_like(out_ref)

    for i in range(4):
        target = target_ref[step * 4 + i]

        @pl.when(target >= 0)
        def _():
            out_ref[target] += arrived_ref[i]


def tiles(*counts):
    return tuple(jax.ShapeDtypeStruct((n, T, T), F32) for n in counts)


def leaf_id(z, y, c):
    return ((z % 8) * 4 + y % 4) * 2 + c


PLACES = [(z, y, c) for z in range(8) for y in range(4) for c in range(2)]


def send(x, pairs):
    return lax.ppermute(x, "leaf", [(leaf_id(*a), leaf_id(*b)) for a, b in pairs])


def dense(work, zero, tile, slot, codes, where, *tables):
    outgoing = pl.pallas_call(
        slots_kernel,
        out_shape=tiles(64)[0],
        in_specs=[SMEM, ANY],
        out_specs=ANY,
        scratch_shapes=[pltpu.SemaphoreType.DMA((64,))],
        name="slots",
    )(tile, work)
    arrived = lax.all_to_all(outgoing, "leaf", split_axis=0, concat_axis=0, tiled=True)
    targets = lax.all_to_all(slot, "leaf", split_axis=0, concat_axis=0, tiled=True)
    return pl.pallas_call(
        add_kernel,
        out_shape=tiles(ASLOT)[0],
        grid=(16,),
        in_specs=[SMEM, pl.BlockSpec((4, T, T), lambda i: (i, 0, 0))],
        out_specs=pl.BlockSpec((ASLOT, T, T), lambda i: (0, 0, 0)),
        compiler_params=pltpu.CompilerParams(vmem_limit_bytes=32 << 20),
        name="add",
    )(targets, arrived)


def tie(x, *others):
    return lax.optimization_barrier((x,) + others)[0]


def sparse(work, zero, tile, slot, codes, where, queued, queued_far, turn_near, turn_far, end):
    swap = [((z, y, c), (z, y, 1 - c)) for z, y, c in PLACES]
    along_z = [[((z, y, c), (z + s, y, c)) for z, y, c in PLACES] for s in (1, -1)]
    along_y = [[((z, y, c), (z, y + s, c)) for z, y, c in PLACES] for s in (1, -1)]

    def sends(xs, ways):
        return [send(x, way) for x, way in zip(xs, ways)]

    def swaps(xs):
        return [send(x, swap) for x in xs]

    def after(xs, *others):
        return list(lax.optimization_barrier(tuple(xs) + others)[:len(xs)])

    other = send(work, swap)
    root = [send(zero, [((z, y, c), (0, y, c)) for y in range(4) for c in range(2)]) for z in (3, 4, 5)]
    both = arrays(BUF, [work], [other])
    far_list = gather(queued_far, both, FY1, "queue_far")
    near_list = gather(queued, both, N1, "queue")
    near_list, far_list = after(near_list, *far_list, *root), after(far_list, *near_list)
    n1 = sends(near_list, along_z)
    f1 = sends(far_list, along_y)
    f2 = sends([x[:FY2] for x in f1], along_y)
    n2 = sends(after([x[:N2] for x in n1], *f1), along_z)
    column = jnp.stack(after(root, *n1))
    pass_on = send(column, [((0, 2, 0), (0, 1, 0)), ((0, 2, 1), (0, 3, 1))])
    row1 = send(column, [((0, 1, c), (0, 0, c)) for c in range(2)])
    row3 = send(column, [((0, 3, c), (0, 0, c)) for c in range(2)])
    far_list = gather(turn_far, both + arrays(YF1, f1, swaps(f1)) + arrays(YF2, f2, swaps(f2)), FZ, "turn_far")
    z1 = sends(after(far_list, *n2, pass_on, row1, row3), along_z)
    row2 = send(pass_on, [((0, 1, 0), (0, 0, 0)), ((0, 3, 1), (0, 0, 1))])
    n1_other = swaps(after(n1, *far_list))
    near_sources = both + arrays(ZN1, n1, n1_other) + arrays(ZN2, n2, swaps(n2))
    near_list = gather(turn_near, near_sources, NY1, "turn_near")
    z2 = sends(after(z1, *near_list, row2), along_z)
    y1 = sends(near_list, along_y)
    z3 = sends(z2, along_z)
    y2 = sends([x[:NY2] for x in y1], along_y)
    z4 = sends(after(z3, *y1), along_z)
    roots = jnp.concatenate([column, row1, row2, row3])
    roots = arrays(ROOT, [roots], [send(roots, [((0, 0, 1), (0, 0, 0))])])
    near_sources = near_sources + arrays(YN1, y1, swaps(y1)) + arrays(YN2, y2, swaps(y2)) + roots
    base = add_up(where, end, codes, jnp.zeros((8, 128), F32), near_sources, BUF, YN2, "sum_near")
    far_sources = arrays(ZF3, z3, swaps(z3)) + arrays(ZF4, z4, swaps(z4))
    return add_up(where, end, codes, base, far_sources, ZF3, ZF4, "sum_far")


def local(front, pivot_tiles, send_table):
    place = lax.axis_index("front").astype(jnp.int32)
    leaf = lax.axis_index("leaf").astype(jnp.int32)
    where = jnp.stack([leaf // 8, (leaf // 2) % 4, leaf % 2])
    table = send_table[0, 0]
    used = table[0] >= 0
    tile = jnp.where(used, table[0] * 7 + table[1] - 1, -1)
    code = jnp.where(used, tile * 16 + table[2], -1)
    up = [(i, (i + 1) % 4) for i in range(4)]
    down = [(i, (i - 1) % 4) for i in range(4)]
    own = [[front[0, r, 0, :, k * T:k * T + T].astype(F32) for k in range(2)] for r in range(2)]
    from_left = [[None, None], [None, None]]
    from_right = [[None, None], [None, None]]
    from_far = [[None, None], [None, None]]
    from_left[0][0] = lax.ppermute(own[0][0], "front", up)
    from_right[0][0] = lax.ppermute(own[0][0], "front", down)
    from_far[0][0] = lax.ppermute(from_left[0][0], "front", up)
    codes = lax.all_to_all(jnp.broadcast_to(tie(code, from_left[0][0]), (64, 64)), "leaf", split_axis=0, concat_axis=0, tiled=True).reshape(32, 128)
    from_right[0][1] = lax.ppermute(tie(own[0][1], from_left[0][0], from_right[0][0]), "front", down)
    from_left[0][1] = lax.ppermute(tie(own[0][1], from_far[0][0]), "front", up)
    from_far[0][1] = lax.ppermute(from_right[0][1], "front", down)
    for k in range(2):
        from_left[1][k] = lax.ppermute(tie(own[1][k], from_far[0][0]), "front", up)
        from_right[1][k] = lax.ppermute(tie(own[1][k], from_far[0][0]), "front", down)
    from_far[1][0] = lax.ppermute(from_left[1][0], "front", up)
    from_far[1][1] = lax.ppermute(from_right[1][1], "front", down)
    by_q = [own, from_right, from_far, from_left]

    def of_owner(owner, r, k, *after):
        q = lax.rem(owner - place + 4, 4)
        if after:
            q = tie(q, *after)
        out = by_q[0][r][k]
        for i in range(1, 4):
            out = jnp.where(q == i, by_q[i][r][k], out)
        return out

    inv0 = pl.pallas_call(
        first_kernel,
        out_shape=jax.ShapeDtypeStruct((T, T), F32),
        in_specs=[VMEM],
        out_specs=VMEM,
        scratch_shapes=[pltpu.VMEM((B, 128), F32)],
        compiler_params=pltpu.CompilerParams(vmem_limit_bytes=16 << 20),
        name="first",
    )(of_owner(0, 0, 0, codes))
    *tables, over = pl.pallas_call(
        plan_kernel,
        out_shape=tuple(jax.ShapeDtypeStruct((n, 128), jnp.int32) for n in (1, 1, 1, 1, 32)) + (jax.ShapeDtypeStruct((1, 1), F32),),
        in_specs=[SMEM, VMEM],
        out_specs=(VMEM,) * 6,
        name="plan",
    )(where, tie(codes, inv0))
    over = jnp.maximum(over, tie(lax.ppermute(over, "front", up), inv0))
    across = lax.ppermute(over, "front", [(i, (i + 2) % 4) for i in range(4)])

    w10 = of_owner(1, 0, 0, inv0)
    w11 = of_owner(1, 0, 1, inv0)
    l10, inv1 = pl.pallas_call(
        second_kernel,
        out_shape=(jax.ShapeDtypeStruct((T, T), F32),) * 2,
        in_specs=[SMEM, VMEM, VMEM, VMEM],
        out_specs=(VMEM, VMEM),
        scratch_shapes=[pltpu.VMEM((B, 128), F32)],
        compiler_params=pltpu.CompilerParams(vmem_limit_bytes=16 << 20),
        name="second",
    )(pivot_tiles, inv0, w10, w11)

    received = [by_q[q][r][k] for q in range(1, 4) for r in range(2) for k in range(2)]
    factor, work, zero = pl.pallas_call(
        panel_kernel,
        out_shape=(jax.ShapeDtypeStruct((1, 2, 1, T, 2 * T), F32),) + tiles(TILES) + (jax.ShapeDtypeStruct((T, T), F32),),
        in_specs=[SMEM, SMEM] + [VMEM] * 16,
        out_specs=(VMEM, VMEM, VMEM),
        scratch_shapes=[pltpu.VMEM((8, T, 2 * T), BF16), pltpu.VMEM((8, T, 2 * T), BF16)],
        compiler_params=pltpu.CompilerParams(vmem_limit_bytes=40 << 20),
        name="panel",
    )(place.reshape(1), tile[0:1], inv0, l10, inv1, front, *received)
    over = jnp.maximum(over, tie(across, zero))
    ancestor = lax.cond(over[0, 0] > 0.0, dense, sparse, work, zero, tile, table[2], codes, where, *tables)
    return (factor, ancestor.reshape(1, 1, ASLOT, T, T))


def solution(mesh):
    in_specs = (P("leaf", None, "front", None, None), P("leaf"), P("leaf", "front", None, None))
    out_specs = (P("leaf", None, "front", None, None), P("leaf", "front", None, None, None))
    return jax.shard_map(local, mesh=mesh, in_specs=in_specs, out_specs=out_specs, check_vma=False)
```

```python
import functools

import jax
import jax.numpy as jnp
from jax import lax
from jax.experimental import pallas as pl
from jax.experimental.pallas import tpu as pltpu
from jax.sharding import PartitionSpec as P

PT = 2
ASLOT = 16
TILES = 14
N1, N2 = 8, 5
FY1, FY2 = 5, 3
FZ = 5
NY1, NY2 = 11, 7
BUF, ZN1, ZN2, YF1, YF2, YN1, YN2, ZF3, ZF4, ROOT = range(10)
B = 64
T = 256
F32 = jnp.float32
BF16 = jnp.bfloat16
HIGHEST = lax.Precision.HIGHEST
VMEM = pl.BlockSpec(memory_space=pltpu.VMEM)
SMEM = pl.BlockSpec(memory_space=pltpu.SMEM)
ANY = pl.BlockSpec(memory_space=pl.ANY)
NN = (((1,), (0,)), ((), ()))
NT = (((1,), (1,)), ((), ()))
TN = (((0,), (0,)), ((), ()))


def dot(a, b, dims):
    return lax.dot_general(a, b, dims, precision=HIGHEST, preferred_element_type=F32)


def dot1(a, b, dims):
    return lax.dot_general(a, b, dims, preferred_element_type=F32)


def split(x):
    high = x.astype(BF16)
    return high, (x - high.astype(F32)).astype(BF16)


def split3(x):
    high = x.astype(BF16)
    rest = x - high.astype(F32)
    mid = rest.astype(BF16)
    return high, mid, (rest - mid.astype(F32)).astype(BF16)


def dot3(a, b, dims):
    ah, al = a
    bh, bl = b
    return dot1(ah, bh, dims) + (dot1(ah, bl, dims) + dot1(al, bh, dims))


def factor64(groups, f_ref):
    sub = lax.broadcasted_iota(jnp.int32, (8, 128), 0)

    def body(it, gs):
        cols = [[jnp.broadcast_to(g[:, t:t + 1], (8, 128)) for t in range(8)] for g in gs]
        rows = [jnp.broadcast_to(gs[0][t:t + 1, :], (8, 128)) for t in range(8)]
        s = [[jnp.broadcast_to(cols[0][t][u:u + 1, :], (8, 128)) if u >= t else None for t in range(8)] for u in range(8)]
        inv = [None] * 8
        for t in range(8):
            inv[t] = 1.0 / s[t][t]
            for u in range(t + 1, 8):
                low = s[u][t] * inv[t]
                for v in range(u, 8):
                    s[v][u] = s[v][u] - low * s[v][t]
                rows[u] = rows[u] - low * rows[t]
                for g in range(1, 8):
                    cols[g][u] = cols[g][u] - low * cols[g][t]
        done = jnp.zeros((8, 128), F32)
        for t in range(8):
            done = jnp.where(sub == t, rows[t] * lax.rsqrt(s[t][t]), done)
        f_ref[pl.ds(pl.multiple_of(it * 8, 8), 8), :] = pltpu.roll(done, it * 8, 1)
        scaled = [rows[t] * inv[t] for t in range(8)]
        left = []
        for g in range(1, 8):
            piece = gs[g]
            for t in range(8):
                piece = piece - cols[g][t] * scaled[t]
            left.append(pltpu.roll(piece, 120, 1))
        left.append(gs[0])
        return tuple(left)

    lax.fori_loop(0, 8, body, tuple(groups))


def factor256(x_ref, f_ref):
    lane = lax.broadcasted_iota(jnp.int32, (B, 128), 1)
    row = lax.broadcasted_iota(jnp.int32, (B, 128), 0)
    ident = (lane - B == row).astype(F32)
    col = lax.broadcasted_iota(jnp.int32, (B, T), 1)
    wide_row = lax.broadcasted_iota(jnp.int32, (B, T), 0)
    for k in range(T // B):
        lo = k * B
        strip = x_ref[lo:lo + B, :]
        block = strip[:, (k // 2) * 128:(k // 2) * 128 + 128]
        if k % 2:
            block = pltpu.roll(block, B, 1)
        both = jnp.where(lane < B, block, ident)
        factor64([both[8 * g:8 * g + 8, :] for g in range(8)], f_ref)
        block_inv = f_ref[...][:, B:]
        inside = (col >= lo) & (col < lo + B)
        strip = jnp.where(inside, (col - lo == wide_row).astype(F32), strip)
        out = dot(block_inv, strip, NN)
        x_ref[lo:lo + B, :] = jnp.where(col < lo + B, out, 0.0)
        if lo + B < T:
            rest = T - lo - B
            rest_col = lax.broadcasted_iota(jnp.int32, (rest, T), 1)
            old = x_ref[lo + B:, :]
            old = jnp.where((rest_col >= lo) & (rest_col < lo + B), 0.0, old)
            x_ref[lo + B:, :] = old - dot(out[:, lo + B:], out, TN)


def first_kernel(w00_ref, inv0_ref, f_ref):
    inv0_ref[...] = w00_ref[...]
    factor256(inv0_ref, f_ref)


def second_kernel(piv_ref, inv0_ref, w10_ref, w11_ref, l10_ref, inv1_ref, f_ref):
    l10 = dot(w10_ref[...], inv0_ref[...], NT)
    l10_ref[...] = l10
    inv1_ref[...] = jnp.zeros((T, T), F32)

    @pl.when(piv_ref[0] >= 2)
    def _():
        inv1_ref[...] = w11_ref[...] - dot(l10, l10, NT)
        factor256(inv1_ref, f_ref)


def iota(shape, dim):
    return lax.broadcasted_iota(jnp.int32, shape, dim)


def fdot(a, b):
    return lax.dot_general(a, b, (((1,), (0,)), ((), ())), preferred_element_type=F32)


def route(codes, z, y, c):
    shape, sq, rows = (32, 128), (128, 128), (32, 32)
    row, lane = iota(shape, 0), iota(shape, 1)
    zs, ys = row // 4, row % 4
    cs, zd, yd, cd = lane // 64, (lane // 8) % 8, (lane // 2) % 4, lane % 2
    dz, dy = (zd - zs + 8) % 8, (yd - ys + 4) % 4
    hops = jnp.minimum(dz, 8 - dz)
    far = hops > 2
    used = codes >= 0
    rooted = used & (lane % 64 == 0) & far
    live = used & ~rooted
    near = used & (~far | rooted)
    tile = jnp.where(used, codes // 16, 0)
    slot = jnp.where(used, codes % 16, 0)
    la, lb = iota(sq, 0), iota(sq, 1)
    before = la < lb
    same_zd = (la // 8) % 8 == (lb // 8) % 8
    same_yd = (la // 2) % 4 == (lb // 2) % 4
    ra, rb = iota(rows, 0), iota(rows, 1)
    same_ys = ra % 4 == rb % 4
    same_zs = ra // 4 == rb // 4

    def f(x):
        return x.astype(F32)

    def count(mask, lanes, peers):
        rank = fdot(f(mask), f(before & lanes))
        total = fdot(f(mask), f(lanes))
        if peers is not None:
            rank = rank + fdot(f(peers & (rb < ra)), total)
            total = fdot(f(peers), total)
        return rank, total

    def halves(n_up, n_both, n_down):
        up = jnp.clip(jnp.floor((n_both + n_down - n_up + 1.0) * 0.5), 0.0, n_both)
        return up, n_both - up

    every = la >= 0
    over = jnp.full(shape, -1.0, F32)
    r1, n1 = count(live & (dz == 1), every, None)
    r2, n2 = count(live & (dz == 2), every, None)
    r6, n6 = count(live & (dz == 6), every, None)
    r7, n7 = count(live & (dz == 7), every, None)
    zpos = jnp.where(dz == 1, n2 + r1, jnp.where(dz == 2, r2, jnp.where(dz == 6, r6, n6 + r7)))
    over = jnp.maximum(over, jnp.maximum(n1 + n2, n7 + n6) - 2 * N1)
    over = jnp.maximum(over, jnp.maximum(n2, n6) - 2 * N2)

    def ring(mask, lanes, peers, near, distant):
        a1, m1 = count(mask & (dy == 1), lanes, peers)
        a2, m2 = count(mask & (dy == 2), lanes, peers)
        a3, m3 = count(mask & (dy == 3), lanes, peers)
        up, down = halves(m1, m2, m3)
        minus = (dy == 3) | ((dy == 2) & (a2 >= up))
        pos = jnp.where(dy == 1, up + a1, jnp.where(dy == 3, down + a3, jnp.where(a2 < up, a2, a2 - up)))
        excess = jnp.maximum(jnp.maximum(up + m1, down + m3) - near, jnp.maximum(up, down) - distant)
        return minus.astype(jnp.int32), pos.astype(jnp.int32), excess

    fy_way, fy_pos, excess = ring(live & far, every, None, 2 * FY1, 2 * FY2)
    over = jnp.maximum(over, excess)
    r3, n3 = count(live & (dz == 3), same_yd, same_zs)
    r4, n4 = count(live & (dz == 4), same_yd, same_zs)
    r5, n5 = count(live & (dz == 5), same_yd, same_zs)
    up, down = halves(n3, n4, n5)
    fz_pos = jnp.where(dz == 3, up + r3, jnp.where(dz == 5, down + r5, jnp.where(r4 < up, r4, r4 - up)))
    over = jnp.maximum(over, jnp.maximum(up + n3, down + n5) - 2 * FZ)
    z_way = ((dz > 4) | ((dz == 4) & (r4 >= up))).astype(jnp.int32)
    ny_way, ny_pos, excess = ring(near, same_zd, same_ys, 2 * NY1, 2 * NY2)
    over = jnp.maximum(over, excess)
    zpos, fz_pos = zpos.astype(jnp.int32), fz_pos.astype(jnp.int32)

    def at(kind, way, pos):
        return ((kind * 2 + way) * 2 + (pos % 2 != c)) * 16 + pos // 2

    def listed(mask, way, pos, code):
        key = jnp.where(mask & (pos % 2 == c), way * 16 + pos // 2, -1)
        acc = jnp.zeros(shape, jnp.int32)
        for r in range(32):
            acc = acc + jnp.where(key[r:r + 1, :] == row, code[r:r + 1, :] + 1, 0)
        column = jnp.sum(acc, axis=1, keepdims=True)
        return jnp.sum(jnp.where(lane == row, column, 0), axis=0, keepdims=True) - 1

    held = (BUF * 4 + (cs != c)) * 16 + tile
    here = live & (row == z * 4 + y)
    queued = listed(here & ~far & (dz > 0), z_way, zpos, held)
    queued_far = listed(here & far & (dy > 0), fy_way, fy_pos, held)
    after_y = jnp.where(dy == 0, held, at(jnp.where(dy == 2, YF2, YF1), fy_way, fy_pos))
    turn_far = listed(live & far & (zs == z) & (yd == y), z_way, fz_pos, after_y)
    after_z = jnp.where(dz == 0, held, at(jnp.where(hops == 1, ZN1, ZN2), z_way, zpos))
    after_z = jnp.where(rooted, (ROOT * 4 + (cs != c)) * 16 + zs - 3, after_z)
    turn_near = listed(near & (zd == z) & (ys == y) & (dy > 0), ny_way, ny_pos, after_z)
    end_near = jnp.where(dy == 0, after_z, at(jnp.where(dy == 2, YN2, YN1), ny_way, ny_pos))
    end_far = at(jnp.where(dz == 4, ZF4, ZF3), z_way, fz_pos)
    mine = (zd == z) & (yd == y)
    mine_near = mine & near & (jnp.where(dy == 0, cd, ny_pos % 2) == c)
    mine_far = mine & live & far & (cd == c)
    end = jnp.where(mine_near | mine_far, (jnp.where(mine_far, end_far, end_near) * 2 + (cd != c)) * 16 + slot, -1)
    return queued, queued_far, turn_near, turn_far, end, jnp.max(over, keepdims=True)


def plan_kernel(where_ref, codes_ref, *out_refs):
    for ref, value in zip(out_refs, route(codes_ref[...], where_ref[0], where_ref[1], where_ref[2])):
        ref[...] = value


def panel_kernel(place_ref, first_ref, inv0_ref, l10_ref, inv1_ref, front_ref, *refs):
    pieces = refs[:12]
    factor_ref, out_ref, zero_ref, yh_ref, yl_ref = refs[12:]
    place = place_ref[0]
    a0 = split3(inv0_ref[...])
    low = split(l10_ref[...])
    inv1 = inv1_ref[...]
    for q in range(4):
        for r in range(2):
            if q == 0:
                p0 = front_ref[0, r, 0, :, 0:T]
                p1 = front_ref[0, r, 0, :, T:2 * T].astype(F32)
            else:
                p0 = pieces[(q - 1) * 4 + r * 2][...].astype(BF16)
                p1 = pieces[(q - 1) * 4 + r * 2 + 1][...]
            y0 = dot1(p0, a0[0], NT) + (dot1(p0, a0[1], NT) + dot1(p0, a0[2], NT))
            y0h, y0l = split(y0)
            p1 = p1 - dot3((y0h, y0l), low, NT)
            y1 = dot(p1, inv1, NT)
            if r == 0:
                owner = lax.rem(place + q, 4)
                y1 = jnp.where(owner > 0, y1, 0.0)
            y1h, y1l = split(y1)
            n = q * 2 + r
            yh_ref[n, :, 0:T] = y0h
            yl_ref[n, :, 0:T] = y0l
            yh_ref[n, :, T:2 * T] = y1h
            yl_ref[n, :, T:2 * T] = y1l
            if q == 0:
                factor_ref[0, r, 0, :, 0:T] = y0
                factor_ref[0, r, 0, :, T:2 * T] = y1
    for r in range(2):
        for n in range(8):
            column = lax.rem(place + n // 2, 4) + 4 * (n % 2)

            @pl.when(column > 0)
            def _():
                start = pl.multiple_of(column * T, T)
                tile = front_ref[0, r, 0, :, pl.ds(start, T)].astype(F32)
                own = (yh_ref[r], yl_ref[r])
                other = (yh_ref[n], yl_ref[n])
                tile = tile - dot3(own, other, NT)
                index = r * 7 + column - 1
                out_ref[index] = tile

                @pl.when(index == first_ref[0])
                def _():
                    zero_ref[...] = tile


def arrays(kind, own, other=()):
    out = []
    for sib, xs in ((0, own), (1, other)):
        for way, x in enumerate(xs):
            out.append(((kind * 2 + way) * 2 + sib,) + (x if isinstance(x, tuple) else (0, x)))
    return out


def copy_from(sources, code, target_ref, sem):
    for sid, first, ref in sources:
        @pl.when(code // 16 == sid)
        def _():
            pltpu.make_async_copy(ref.at[first + code % 16], target_ref, sem).start()


def operands(sources):
    xs, numbered = [], []
    for sid, first, x in sources:
        where = [i for i, other in enumerate(xs) if other is x]
        if not where:
            xs.append(x)
        numbered.append((sid, first, where[0] if where else len(xs) - 1))
    return numbered, xs


def gather_kernel(numbered, size, table_ref, *refs):
    sources = [(sid, first, refs[i]) for sid, first, i in numbered]
    *outs, sem = refs[-3:]
    for way, out in enumerate(outs):
        def start(i, _):
            code = table_ref[0, way * 16 + i]

            @pl.when(code >= 0)
            def _():
                copy_from(sources, code, out.at[i], sem.at[way * size + i])
            return 0

        lax.fori_loop(0, size, start, 0)
    for way, out in enumerate(outs):
        def wait(i, _):
            @pl.when(table_ref[0, way * 16 + i] >= 0)
            def _():
                pltpu.make_async_copy(refs[0].at[0], out.at[i], sem.at[way * size + i]).wait()
            return 0

        lax.fori_loop(0, size, wait, 0)


def gather(table, sources, size, name):
    numbered, xs = operands(sources)
    return pl.pallas_call(
        lambda *refs: gather_kernel(numbered, size, *refs),
        out_shape=tiles(size, size),
        in_specs=[SMEM] + [ANY] * len(xs),
        out_specs=(VMEM,) * 2,
        scratch_shapes=[pltpu.SemaphoreType.DMA((2 * size,))],
        compiler_params=pltpu.CompilerParams(vmem_limit_bytes=10 << 20),
        cost_estimate=pl.CostEstimate(flops=0, bytes_accessed=120 << 20, transcendentals=0),
        name=name,
    )(table, *xs)


DEPTH = 8


def sum_kernel(numbered, near, where_ref, table_ref, *refs):
    z, y = where_ref[0], where_ref[1]
    if near:
        *ins, own_ref, other_ref, list_ref, buf_ref, sem = refs
        own_ref[...] = jnp.zeros_like(own_ref)
        other_ref[...] = jnp.zeros_like(other_ref)
    else:
        a_ref, b_ref, *ins, own_ref, list_ref, buf_ref, sem = refs
    sources = [(sid, first, ins[i]) for sid, first, i in numbered]

    def collect(i, n):
        code = table_ref[i // 4, (i // 2 % 2) * 64 + z * 8 + y * 2 + i % 2]
        kind = code // 2048
        take = (code >= 0) & (((kind == ZF3) | (kind == ZF4)) != near)

        @pl.when(take)
        def _():
            list_ref[n] = code
        return n + take.astype(jnp.int32)

    n = lax.fori_loop(0, 128, collect, jnp.int32(0))

    def start(i):
        slot = lax.rem(i, DEPTH)
        copy_from(sources, list_ref[i] // 32, buf_ref.at[slot], sem.at[slot])

    def prime(i, _):
        start(i)
        return 0

    def step(i, _):
        slot = lax.rem(i, DEPTH)
        pltpu.make_async_copy(ins[0].at[0], buf_ref.at[slot], sem.at[slot]).wait()
        code = list_ref[i]
        if near:
            @pl.when((code // 16) % 2 == 0)
            def _():
                own_ref[code % 16] += buf_ref[slot]

            @pl.when((code // 16) % 2 == 1)
            def _():
                other_ref[code % 16] += buf_ref[slot]
        else:
            own_ref[code % 16] += buf_ref[slot]

        @pl.when(i + DEPTH < n)
        def _():
            start(i + DEPTH)
        return 0

    lax.fori_loop(0, jnp.minimum(n, DEPTH), prime, 0)
    if not near:
        own_ref[...] = a_ref[...] + b_ref[...]
    lax.fori_loop(0, n, step, 0)


def add_up(where, table, sources, name, *sums):
    numbered, xs = operands(sources)
    near = not sums
    return pl.pallas_call(
        lambda *refs: sum_kernel(numbered, near, *refs),
        out_shape=tiles(ASLOT, ASLOT) if near else tiles(ASLOT)[0],
        in_specs=[SMEM, SMEM] + [VMEM] * len(sums) + [ANY] * len(xs),
        out_specs=(VMEM, VMEM) if near else VMEM,
        scratch_shapes=[pltpu.SMEM((256,), jnp.int32), pltpu.VMEM((DEPTH, T, T), F32), pltpu.SemaphoreType.DMA((DEPTH,))],
        compiler_params=pltpu.CompilerParams(vmem_limit_bytes=18 << 20),
        cost_estimate=pl.CostEstimate(flops=0, bytes_accessed=240 << 20, transcendentals=0),
        name=name,
    )(where, table, *sums, *xs)


def slots_kernel(tile_ref, own_ref, out_ref, sem):
    def start(p, _):
        tile = tile_ref[p]

        @pl.when(tile >= 0)
        def _():
            pltpu.make_async_copy(own_ref.at[tile], out_ref.at[p], sem.at[p]).start()
        return 0

    def wait(p, _):
        @pl.when(tile_ref[p] >= 0)
        def _():
            pltpu.make_async_copy(own_ref.at[0], out_ref.at[p], sem.at[p]).wait()
        return 0

    lax.fori_loop(0, 64, start, 0)
    lax.fori_loop(0, 64, wait, 0)


def add_kernel(target_ref, arrived_ref, out_ref):
    step = pl.program_id(0)

    @pl.when(step == 0)
    def _():
        out_ref[...] = jnp.zeros_like(out_ref)

    for i in range(4):
        target = target_ref[step * 4 + i]

        @pl.when(target >= 0)
        def _():
            out_ref[target] += arrived_ref[i]


def tiles(*counts):
    return tuple(jax.ShapeDtypeStruct((n, T, T), F32) for n in counts)


def leaf_id(z, y, c):
    return ((z % 8) * 4 + y % 4) * 2 + c


PLACES = [(z, y, c) for z in range(8) for y in range(4) for c in range(2)]


def send(x, pairs):
    return lax.ppermute(x, "leaf", [(leaf_id(*a), leaf_id(*b)) for a, b in pairs])


def dense(work, zero, tile, slot, where, *tables):
    outgoing = pl.pallas_call(
        slots_kernel,
        out_shape=tiles(64)[0],
        in_specs=[SMEM, ANY],
        out_specs=ANY,
        scratch_shapes=[pltpu.SemaphoreType.DMA((64,))],
        name="slots",
    )(tile, work)
    arrived = lax.all_to_all(outgoing, "leaf", split_axis=0, concat_axis=0, tiled=True)
    targets = lax.all_to_all(slot, "leaf", split_axis=0, concat_axis=0, tiled=True)
    return pl.pallas_call(
        add_kernel,
        out_shape=tiles(ASLOT)[0],
        grid=(16,),
        in_specs=[SMEM, pl.BlockSpec((4, T, T), lambda i: (i, 0, 0))],
        out_specs=pl.BlockSpec((ASLOT, T, T), lambda i: (0, 0, 0)),
        compiler_params=pltpu.CompilerParams(vmem_limit_bytes=32 << 20),
        name="add",
    )(targets, arrived)


def tie(x, *others):
    return lax.optimization_barrier((x,) + others)[0]


def sparse(work, zero, tile, slot, where, queued, queued_far, turn_near, turn_far, end):
    swap = [((z, y, c), (z, y, 1 - c)) for z, y, c in PLACES]
    along_z = [[((z, y, c), (z + s, y, c)) for z, y, c in PLACES] for s in (1, -1)]
    along_y = [[((z, y, c), (z, y + s, c)) for z, y, c in PLACES] for s in (1, -1)]

    def sends(xs, ways):
        return [send(x, way) for x, way in zip(xs, ways)]

    def swaps(xs):
        return [send(x, swap) for x in xs]

    def after(xs, *others):
        return list(lax.optimization_barrier(tuple(xs) + others)[:len(xs)])

    other = send(work, swap)
    root = [send(zero, [((z, y, c), (0, y, c)) for y in range(4) for c in range(2)]) for z in (3, 4, 5)]
    both = arrays(BUF, [work], [other])
    far_list = gather(queued_far, both, FY1, "queue_far")
    near_list = gather(queued, both, N1, "queue")
    n1 = sends(after(near_list, *far_list), along_z)
    f1 = sends(after(far_list, *near_list), along_y)
    f2 = sends([x[:FY2] for x in f1], along_y)
    n2 = sends(after([x[:N2] for x in n1], *f1), along_z)
    column = jnp.stack(after(root, *f1))
    mixed = send(after([jnp.concatenate([*f1, *f2, column])], *n1)[0], swap)
    cuts = (0, FY1, 2 * FY1, 2 * FY1 + FY2, 2 * FY1 + 2 * FY2)
    parts = [(cut, mixed) for cut in cuts]
    far_list = gather(turn_far, both + arrays(YF1, f1, parts[0:2]) + arrays(YF2, f2, parts[2:4]), FZ, "turn_far")
    z1 = sends(after(far_list, *n2), along_z)
    n1_other = swaps(after(n1, *far_list))
    near_sources = both + arrays(ZN1, n1, n1_other) + arrays(ZN2, n2, swaps(n2)) + arrays(ROOT, [column], parts[4:])
    near_list = gather(turn_near, near_sources, NY1, "turn_near")
    z2 = sends(after(z1, *near_list), along_z)
    y1 = sends(near_list, along_y)
    z3 = sends(z2, along_z)
    y2 = sends(after([x[:NY2] for x in y1], *z2), along_y)
    z4 = sends(after(z3, *y1), along_z)
    own, theirs = add_up(where, end, near_sources + arrays(YN1, y1) + arrays(YN2, after(y2, *z4)), "sum_near")
    far_sources = arrays(ZF3, z3, swaps(after(z3, *z4))) + arrays(ZF4, z4, swaps(z4))
    return add_up(where, end, far_sources, "sum_far", own, send(theirs, swap))


def local(front, pivot_tiles, send_table):
    place = lax.axis_index("front").astype(jnp.int32)
    leaf = lax.axis_index("leaf").astype(jnp.int32)
    where = jnp.stack([leaf // 8, (leaf // 2) % 4, leaf % 2])
    table = send_table[0, 0]
    used = table[0] >= 0
    tile = jnp.where(used, table[0] * 7 + table[1] - 1, -1)
    code = jnp.where(used, tile * 16 + table[2], -1)
    up = [(i, (i + 1) % 4) for i in range(4)]
    down = [(i, (i - 1) % 4) for i in range(4)]
    own = [[front[0, r, 0, :, k * T:k * T + T].astype(F32) for k in range(2)] for r in range(2)]
    from_left = [[None, None], [None, None]]
    from_right = [[None, None], [None, None]]
    from_far = [[None, None], [None, None]]
    from_left[0][0] = lax.ppermute(own[0][0], "front", up)
    from_right[0][0] = lax.ppermute(own[0][0], "front", down)
    from_far[0][0] = lax.ppermute(from_left[0][0], "front", up)
    codes = lax.all_to_all(jnp.broadcast_to(tie(code, from_left[0][0]), (64, 64)), "leaf", split_axis=0, concat_axis=0, tiled=True).reshape(32, 128)
    from_right[0][1] = lax.ppermute(tie(own[0][1], from_left[0][0], from_right[0][0]), "front", down)
    from_left[0][1] = lax.ppermute(tie(own[0][1], from_far[0][0]), "front", up)
    from_far[0][1] = lax.ppermute(from_right[0][1], "front", down)
    for k in range(2):
        from_left[1][k] = lax.ppermute(tie(own[1][k], from_far[0][0]), "front", up)
        from_right[1][k] = lax.ppermute(tie(own[1][k], from_far[0][0]), "front", down)
    from_far[1][0] = lax.ppermute(from_left[1][0], "front", up)
    from_far[1][1] = lax.ppermute(from_right[1][1], "front", down)
    by_q = [own, from_right, from_far, from_left]

    def of_owner(owner, r, k, *after):
        q = lax.rem(owner - place + 4, 4)
        if after:
            q = tie(q, *after)
        out = by_q[0][r][k]
        for i in range(1, 4):
            out = jnp.where(q == i, by_q[i][r][k], out)
        return out

    inv0 = pl.pallas_call(
        first_kernel,
        out_shape=jax.ShapeDtypeStruct((T, T), F32),
        in_specs=[VMEM],
        out_specs=VMEM,
        scratch_shapes=[pltpu.VMEM((B, 128), F32)],
        compiler_params=pltpu.CompilerParams(vmem_limit_bytes=16 << 20),
        name="first",
    )(of_owner(0, 0, 0))
    *tables, over = pl.pallas_call(
        plan_kernel,
        out_shape=tuple(jax.ShapeDtypeStruct((n, 128), jnp.int32) for n in (1, 1, 1, 1, 32)) + (jax.ShapeDtypeStruct((1, 1), F32),),
        in_specs=[SMEM, VMEM],
        out_specs=(VMEM,) * 6,
        name="plan",
    )(where, tie(codes, inv0))
    over = jnp.maximum(over, tie(lax.ppermute(over, "front", up), inv0))
    across = lax.ppermute(over, "front", [(i, (i + 2) % 4) for i in range(4)])

    w10 = of_owner(1, 0, 0, inv0)
    w11 = of_owner(1, 0, 1, inv0)
    l10, inv1 = pl.pallas_call(
        second_kernel,
        out_shape=(jax.ShapeDtypeStruct((T, T), F32),) * 2,
        in_specs=[SMEM, VMEM, VMEM, VMEM],
        out_specs=(VMEM, VMEM),
        scratch_shapes=[pltpu.VMEM((B, 128), F32)],
        compiler_params=pltpu.CompilerParams(vmem_limit_bytes=16 << 20),
        name="second",
    )(pivot_tiles, inv0, w10, w11)

    received = [by_q[q][r][k] for q in range(1, 4) for r in range(2) for k in range(2)]
    factor, work, zero = pl.pallas_call(
        panel_kernel,
        out_shape=(jax.ShapeDtypeStruct((1, 2, 1, T, 2 * T), F32),) + tiles(TILES) + (jax.ShapeDtypeStruct((T, T), F32),),
        in_specs=[SMEM, SMEM] + [VMEM] * 16,
        out_specs=(VMEM, VMEM, VMEM),
        scratch_shapes=[pltpu.VMEM((8, T, 2 * T), BF16), pltpu.VMEM((8, T, 2 * T), BF16)],
        compiler_params=pltpu.CompilerParams(vmem_limit_bytes=40 << 20),
        name="panel",
    )(place.reshape(1), tile[0:1], inv0, l10, inv1, front, *received)
    over = jnp.maximum(over, tie(across, zero))
    ancestor = lax.cond(over[0, 0] > 0.0, dense, sparse, work, zero, tile, table[2], where, *tables)
    return (factor, ancestor.reshape(1, 1, ASLOT, T, T))


def solution(mesh):
    in_specs = (P("leaf", None, "front", None, None), P("leaf"), P("leaf", "front", None, None))
    out_specs = (P("leaf", None, "front", None, None), P("leaf", "front", None, None, None))
    return jax.shard_map(local, mesh=mesh, in_specs=in_specs, out_specs=out_specs, check_vma=False)
```

```python
import functools

import jax
import jax.numpy as jnp
from jax import lax
from jax.experimental import pallas as pl
from jax.experimental.pallas import tpu as pltpu
from jax.sharding import PartitionSpec as P

PT = 2
ASLOT = 16
TILES = 14
N1, N2 = 8, 5
FY1, FY2 = 5, 3
FZ = 5
NY1, NY2 = 11, 7
BUF, ZN1, ZN2, YF1, YF2, YN1, YN2, ZF3, ZF4, ROOT = range(10)
B = 64
T = 256
F32 = jnp.float32
BF16 = jnp.bfloat16
HIGHEST = lax.Precision.HIGHEST
VMEM = pl.BlockSpec(memory_space=pltpu.VMEM)
SMEM = pl.BlockSpec(memory_space=pltpu.SMEM)
ANY = pl.BlockSpec(memory_space=pl.ANY)
NN = (((1,), (0,)), ((), ()))
NT = (((1,), (1,)), ((), ()))
TN = (((0,), (0,)), ((), ()))


def dot(a, b, dims):
    return lax.dot_general(a, b, dims, precision=HIGHEST, preferred_element_type=F32)


def dot1(a, b, dims):
    return lax.dot_general(a, b, dims, preferred_element_type=F32)


def split(x):
    high = x.astype(BF16)
    return high, (x - high.astype(F32)).astype(BF16)


def split3(x):
    high = x.astype(BF16)
    rest = x - high.astype(F32)
    mid = rest.astype(BF16)
    return high, mid, (rest - mid.astype(F32)).astype(BF16)


def dot3(a, b, dims):
    ah, al = a
    bh, bl = b
    return dot1(ah, bh, dims) + (dot1(ah, bl, dims) + dot1(al, bh, dims))


def factor64(groups, f_ref):
    sub = lax.broadcasted_iota(jnp.int32, (8, 128), 0)

    def body(it, gs):
        cols = [[jnp.broadcast_to(g[:, t:t + 1], (8, 128)) for t in range(8)] for g in gs]
        rows = [jnp.broadcast_to(gs[0][t:t + 1, :], (8, 128)) for t in range(8)]
        s = [[jnp.broadcast_to(cols[0][t][u:u + 1, :], (8, 128)) if u >= t else None for t in range(8)] for u in range(8)]
        inv = [None] * 8
        for t in range(8):
            inv[t] = 1.0 / s[t][t]
            for u in range(t + 1, 8):
                low = s[u][t] * inv[t]
                for v in range(u, 8):
                    s[v][u] = s[v][u] - low * s[v][t]
                rows[u] = rows[u] - low * rows[t]
                for g in range(1, 8):
                    cols[g][u] = cols[g][u] - low * cols[g][t]
        done = jnp.zeros((8, 128), F32)
        for t in range(8):
            done = jnp.where(sub == t, rows[t] * lax.rsqrt(s[t][t]), done)
        f_ref[pl.ds(pl.multiple_of(it * 8, 8), 8), :] = pltpu.roll(done, it * 8, 1)
        scaled = [rows[t] * inv[t] for t in range(8)]
        left = []
        for g in range(1, 8):
            piece = gs[g]
            for t in range(8):
                piece = piece - cols[g][t] * scaled[t]
            left.append(pltpu.roll(piece, 120, 1))
        left.append(gs[0])
        return tuple(left)

    lax.fori_loop(0, 8, body, tuple(groups))


def factor256(x_ref, f_ref):
    lane = lax.broadcasted_iota(jnp.int32, (B, 128), 1)
    row = lax.broadcasted_iota(jnp.int32, (B, 128), 0)
    ident = (lane - B == row).astype(F32)
    col = lax.broadcasted_iota(jnp.int32, (B, T), 1)
    wide_row = lax.broadcasted_iota(jnp.int32, (B, T), 0)
    for k in range(T // B):
        lo = k * B
        strip = x_ref[lo:lo + B, :]
        block = strip[:, (k // 2) * 128:(k // 2) * 128 + 128]
        if k % 2:
            block = pltpu.roll(block, B, 1)
        both = jnp.where(lane < B, block, ident)
        factor64([both[8 * g:8 * g + 8, :] for g in range(8)], f_ref)
        block_inv = f_ref[...][:, B:]
        inside = (col >= lo) & (col < lo + B)
        strip = jnp.where(inside, (col - lo == wide_row).astype(F32), strip)
        out = dot(block_inv, strip, NN)
        x_ref[lo:lo + B, :] = jnp.where(col < lo + B, out, 0.0)
        if lo + B < T:
            rest = T - lo - B
            rest_col = lax.broadcasted_iota(jnp.int32, (rest, T), 1)
            old = x_ref[lo + B:, :]
            old = jnp.where((rest_col >= lo) & (rest_col < lo + B), 0.0, old)
            x_ref[lo + B:, :] = old - dot(out[:, lo + B:], out, TN)


def first_kernel(w00_ref, inv0_ref, f_ref):
    inv0_ref[...] = w00_ref[...]
    factor256(inv0_ref, f_ref)


def second_kernel(piv_ref, inv0_ref, w10_ref, w11_ref, l10_ref, inv1_ref, f_ref):
    l10 = dot(w10_ref[...], inv0_ref[...], NT)
    l10_ref[...] = l10
    inv1_ref[...] = jnp.zeros((T, T), F32)

    @pl.when(piv_ref[0] >= 2)
    def _():
        inv1_ref[...] = w11_ref[...] - dot(l10, l10, NT)
        factor256(inv1_ref, f_ref)


def iota(shape, dim):
    return lax.broadcasted_iota(jnp.int32, shape, dim)


def fdot(a, b):
    return lax.dot_general(a, b, (((1,), (0,)), ((), ())), preferred_element_type=F32)


def route(codes, z, y, c):
    shape, sq, rows = (32, 128), (128, 128), (32, 32)
    row, lane = iota(shape, 0), iota(shape, 1)
    zs, ys = row // 4, row % 4
    cs, zd, yd, cd = lane // 64, (lane // 8) % 8, (lane // 2) % 4, lane % 2
    dz, dy = (zd - zs + 8) % 8, (yd - ys + 4) % 4
    hops = jnp.minimum(dz, 8 - dz)
    far = hops > 2
    used = codes >= 0
    rooted = used & (lane % 64 == 0) & far
    live = used & ~rooted
    near = used & (~far | rooted)
    tile = jnp.where(used, codes // 16, 0)
    slot = jnp.where(used, codes % 16, 0)
    la, lb = iota(sq, 0), iota(sq, 1)
    before = la < lb
    same_zd = (la // 8) % 8 == (lb // 8) % 8
    same_yd = (la // 2) % 4 == (lb // 2) % 4
    ra, rb = iota(rows, 0), iota(rows, 1)
    same_ys = ra % 4 == rb % 4
    same_zs = ra // 4 == rb // 4

    def f(x):
        return x.astype(F32)

    def count(mask, lanes, peers):
        rank = fdot(f(mask), f(before & lanes))
        total = fdot(f(mask), f(lanes))
        if peers is not None:
            rank = rank + fdot(f(peers & (rb < ra)), total)
            total = fdot(f(peers), total)
        return rank, total

    def halves(n_up, n_both, n_down):
        up = jnp.clip(jnp.floor((n_both + n_down - n_up + 1.0) * 0.5), 0.0, n_both)
        return up, n_both - up

    every = la >= 0
    over = jnp.full(shape, -1.0, F32)
    r1, n1 = count(live & (dz == 1), every, None)
    r2, n2 = count(live & (dz == 2), every, None)
    r6, n6 = count(live & (dz == 6), every, None)
    r7, n7 = count(live & (dz == 7), every, None)
    zpos = jnp.where(dz == 1, n2 + r1, jnp.where(dz == 2, r2, jnp.where(dz == 6, r6, n6 + r7)))
    over = jnp.maximum(over, jnp.maximum(n1 + n2, n7 + n6) - 2 * N1)
    over = jnp.maximum(over, jnp.maximum(n2, n6) - 2 * N2)

    def ring(mask, lanes, peers, near, distant):
        a1, m1 = count(mask & (dy == 1), lanes, peers)
        a2, m2 = count(mask & (dy == 2), lanes, peers)
        a3, m3 = count(mask & (dy == 3), lanes, peers)
        up, down = halves(m1, m2, m3)
        minus = (dy == 3) | ((dy == 2) & (a2 >= up))
        pos = jnp.where(dy == 1, up + a1, jnp.where(dy == 3, down + a3, jnp.where(a2 < up, a2, a2 - up)))
        excess = jnp.maximum(jnp.maximum(up + m1, down + m3) - near, jnp.maximum(up, down) - distant)
        return minus.astype(jnp.int32), pos.astype(jnp.int32), excess

    fy_way, fy_pos, excess = ring(live & far, every, None, 2 * FY1, 2 * FY2)
    over = jnp.maximum(over, excess)
    r3, n3 = count(live & (dz == 3), same_yd, same_zs)
    r4, n4 = count(live & (dz == 4), same_yd, same_zs)
    r5, n5 = count(live & (dz == 5), same_yd, same_zs)
    up, down = halves(n3, n4, n5)
    fz_pos = jnp.where(dz == 3, up + r3, jnp.where(dz == 5, down + r5, jnp.where(r4 < up, r4, r4 - up)))
    over = jnp.maximum(over, jnp.maximum(up + n3, down + n5) - 2 * FZ)
    z_way = ((dz > 4) | ((dz == 4) & (r4 >= up))).astype(jnp.int32)
    ny_way, ny_pos, excess = ring(near, same_zd, same_ys, 2 * NY1, 2 * NY2)
    over = jnp.maximum(over, excess)
    zpos, fz_pos = zpos.astype(jnp.int32), fz_pos.astype(jnp.int32)

    def at(kind, way, pos):
        return ((kind * 2 + way) * 2 + (pos % 2 != c)) * 16 + pos // 2

    def listed(mask, way, pos, code):
        key = jnp.where(mask & (pos % 2 == c), way * 16 + pos // 2, -1)
        acc = jnp.zeros(shape, jnp.int32)
        for r in range(32):
            acc = acc + jnp.where(key[r:r + 1, :] == row, code[r:r + 1, :] + 1, 0)
        column = jnp.sum(acc, axis=1, keepdims=True)
        return jnp.sum(jnp.where(lane == row, column, 0), axis=0, keepdims=True) - 1

    held = (BUF * 4 + (cs != c)) * 16 + tile
    here = live & (row == z * 4 + y)
    queued = listed(here & ~far & (dz > 0), z_way, zpos, held)
    queued_far = listed(here & far & (dy > 0), fy_way, fy_pos, held)
    after_y = jnp.where(dy == 0, held, at(jnp.where(dy == 2, YF2, YF1), fy_way, fy_pos))
    turn_far = listed(live & far & (zs == z) & (yd == y), z_way, fz_pos, after_y)
    after_z = jnp.where(dz == 0, held, at(jnp.where(hops == 1, ZN1, ZN2), z_way, zpos))
    after_z = jnp.where(rooted, (ROOT * 4 + (cs != c)) * 16 + zs - 3, after_z)
    turn_near = listed(near & (zd == z) & (ys == y) & (dy > 0), ny_way, ny_pos, after_z)
    end_near = jnp.where(dy == 0, after_z, at(jnp.where(dy == 2, YN2, YN1), ny_way, ny_pos))
    end_far = at(jnp.where(dz == 4, ZF4, ZF3), z_way, fz_pos)
    keeper = jnp.where(far & ~rooted, fz_pos % 2, jnp.where(dy > 0, ny_pos % 2, cd))
    mine = used & (zd == z) & (yd == y) & (keeper == c)
    end = jnp.where(mine, (jnp.where(live & far, end_far, end_near) * 2 + (cd != c)) * 16 + slot, -1)
    return queued, queued_far, turn_near, turn_far, end, jnp.max(over, keepdims=True)


def plan_kernel(where_ref, codes_ref, *out_refs):
    for ref, value in zip(out_refs, route(codes_ref[...], where_ref[0], where_ref[1], where_ref[2])):
        ref[...] = value


def panel_kernel(place_ref, first_ref, inv0_ref, l10_ref, inv1_ref, front_ref, *refs):
    pieces = refs[:12]
    factor_ref, out_ref, zero_ref, yh_ref, yl_ref = refs[12:]
    place = place_ref[0]
    a0 = split3(inv0_ref[...])
    low = split(l10_ref[...])
    inv1 = inv1_ref[...]
    for q in range(4):
        for r in range(2):
            if q == 0:
                p0 = front_ref[0, r, 0, :, 0:T]
                p1 = front_ref[0, r, 0, :, T:2 * T].astype(F32)
            else:
                p0 = pieces[(q - 1) * 4 + r * 2][...].astype(BF16)
                p1 = pieces[(q - 1) * 4 + r * 2 + 1][...]
            y0 = dot1(p0, a0[0], NT) + (dot1(p0, a0[1], NT) + dot1(p0, a0[2], NT))
            y0h, y0l = split(y0)
            p1 = p1 - dot3((y0h, y0l), low, NT)
            y1 = dot(p1, inv1, NT)
            if r == 0:
                owner = lax.rem(place + q, 4)
                y1 = jnp.where(owner > 0, y1, 0.0)
            y1h, y1l = split(y1)
            n = q * 2 + r
            yh_ref[n, :, 0:T] = y0h
            yl_ref[n, :, 0:T] = y0l
            yh_ref[n, :, T:2 * T] = y1h
            yl_ref[n, :, T:2 * T] = y1l
            if q == 0:
                factor_ref[0, r, 0, :, 0:T] = y0
                factor_ref[0, r, 0, :, T:2 * T] = y1
    for r in range(2):
        for n in range(8):
            column = lax.rem(place + n // 2, 4) + 4 * (n % 2)

            @pl.when(column > 0)
            def _():
                start = pl.multiple_of(column * T, T)
                tile = front_ref[0, r, 0, :, pl.ds(start, T)].astype(F32)
                own = (yh_ref[r], yl_ref[r])
                other = (yh_ref[n], yl_ref[n])
                tile = tile - dot3(own, other, NT)
                index = r * 7 + column - 1
                out_ref[index] = tile

                @pl.when(index == first_ref[0])
                def _():
                    zero_ref[...] = tile


def arrays(kind, own, other=()):
    out = []
    for sib, xs in ((0, own), (1, other)):
        for way, x in enumerate(xs):
            out.append(((kind * 2 + way) * 2 + sib,) + (x if isinstance(x, tuple) else (0, x)))
    return out


def copy_from(sources, code, target_ref, sem):
    for sid, first, ref in sources:
        @pl.when(code // 16 == sid)
        def _():
            pltpu.make_async_copy(ref.at[first + code % 16], target_ref, sem).start()


def operands(sources):
    xs, numbered = [], []
    for sid, first, x in sources:
        where = [i for i, other in enumerate(xs) if other is x]
        if not where:
            xs.append(x)
        numbered.append((sid, first, where[0] if where else len(xs) - 1))
    return numbered, xs


def gather_kernel(numbered, size, table_ref, *refs):
    sources = [(sid, first, refs[i]) for sid, first, i in numbered]
    *outs, sem = refs[-3:]
    for way, out in enumerate(outs):
        def start(i, _):
            code = table_ref[0, way * 16 + i]

            @pl.when(code >= 0)
            def _():
                copy_from(sources, code, out.at[i], sem.at[way * size + i])
            return 0

        lax.fori_loop(0, size, start, 0)
    for way, out in enumerate(outs):
        def wait(i, _):
            @pl.when(table_ref[0, way * 16 + i] >= 0)
            def _():
                pltpu.make_async_copy(refs[0].at[0], out.at[i], sem.at[way * size + i]).wait()
            return 0

        lax.fori_loop(0, size, wait, 0)


def gather(table, sources, size, name, mebibytes=120):
    numbered, xs = operands(sources)
    return pl.pallas_call(
        lambda *refs: gather_kernel(numbered, size, *refs),
        out_shape=tiles(size, size),
        in_specs=[SMEM] + [ANY] * len(xs),
        out_specs=(VMEM,) * 2,
        scratch_shapes=[pltpu.SemaphoreType.DMA((2 * size,))],
        compiler_params=pltpu.CompilerParams(vmem_limit_bytes=10 << 20),
        cost_estimate=pl.CostEstimate(flops=0, bytes_accessed=mebibytes << 20, transcendentals=0),
        name=name,
    )(table, *xs)


DEPTH = 12


def sum_kernel(numbered, where_ref, table_ref, *refs):
    *ins, own_ref, other_ref, list_ref, buf_ref, sem = refs
    z, y = where_ref[0], where_ref[1]
    sources = [(sid, first, ins[i]) for sid, first, i in numbered]

    def collect(i, n):
        code = table_ref[i // 4, (i // 2 % 2) * 64 + z * 8 + y * 2 + i % 2]

        @pl.when(code >= 0)
        def _():
            list_ref[n] = code
        return n + (code >= 0).astype(jnp.int32)

    n = lax.fori_loop(0, 128, collect, jnp.int32(0))

    def start(i):
        slot = lax.rem(i, DEPTH)
        copy_from(sources, list_ref[i] // 32, buf_ref.at[slot], sem.at[slot])

    def prime(i, _):
        start(i)
        return 0

    def step(i, _):
        slot = lax.rem(i, DEPTH)
        pltpu.make_async_copy(ins[0].at[0], buf_ref.at[slot], sem.at[slot]).wait()
        code = list_ref[i]

        @pl.when((code // 16) % 2 == 0)
        def _():
            own_ref[code % 16] += buf_ref[slot]

        @pl.when((code // 16) % 2 == 1)
        def _():
            other_ref[code % 16] += buf_ref[slot]

        @pl.when(i + DEPTH < n)
        def _():
            start(i + DEPTH)
        return 0

    lax.fori_loop(0, jnp.minimum(n, DEPTH), prime, 0)
    own_ref[...] = jnp.zeros_like(own_ref)
    other_ref[...] = jnp.zeros_like(other_ref)
    lax.fori_loop(0, n, step, 0)


def add_up(where, table, sources):
    numbered, xs = operands(sources)
    return pl.pallas_call(
        lambda *refs: sum_kernel(numbered, *refs),
        out_shape=tiles(ASLOT, ASLOT),
        in_specs=[SMEM, SMEM] + [ANY] * len(xs),
        out_specs=(VMEM, VMEM),
        scratch_shapes=[pltpu.SMEM((256,), jnp.int32), pltpu.VMEM((DEPTH, T, T), F32), pltpu.SemaphoreType.DMA((DEPTH,))],
        compiler_params=pltpu.CompilerParams(vmem_limit_bytes=16 << 20),
        cost_estimate=pl.CostEstimate(flops=0, bytes_accessed=30 << 20, transcendentals=0),
        name="sum",
    )(where, table, *xs)


def slots_kernel(tile_ref, own_ref, out_ref, sem):
    def start(p, _):
        tile = tile_ref[p]

        @pl.when(tile >= 0)
        def _():
            pltpu.make_async_copy(own_ref.at[tile], out_ref.at[p], sem.at[p]).start()
        return 0

    def wait(p, _):
        @pl.when(tile_ref[p] >= 0)
        def _():
            pltpu.make_async_copy(own_ref.at[0], out_ref.at[p], sem.at[p]).wait()
        return 0

    lax.fori_loop(0, 64, start, 0)
    lax.fori_loop(0, 64, wait, 0)


def add_kernel(target_ref, arrived_ref, out_ref):
    step = pl.program_id(0)

    @pl.when(step == 0)
    def _():
        out_ref[...] = jnp.zeros_like(out_ref)

    for i in range(4):
        target = target_ref[step * 4 + i]

        @pl.when(target >= 0)
        def _():
            out_ref[target] += arrived_ref[i]


def tiles(*counts):
    return tuple(jax.ShapeDtypeStruct((n, T, T), F32) for n in counts)


def leaf_id(z, y, c):
    return ((z % 8) * 4 + y % 4) * 2 + c


PLACES = [(z, y, c) for z in range(8) for y in range(4) for c in range(2)]


def send(x, pairs):
    return lax.ppermute(x, "leaf", [(leaf_id(*a), leaf_id(*b)) for a, b in pairs])


def dense(work, zero, tile, slot, where, *tables):
    outgoing = pl.pallas_call(
        slots_kernel,
        out_shape=tiles(64)[0],
        in_specs=[SMEM, ANY],
        out_specs=ANY,
        scratch_shapes=[pltpu.SemaphoreType.DMA((64,))],
        name="slots",
    )(tile, work)
    arrived = lax.all_to_all(outgoing, "leaf", split_axis=0, concat_axis=0, tiled=True)
    targets = lax.all_to_all(slot, "leaf", split_axis=0, concat_axis=0, tiled=True)
    return pl.pallas_call(
        add_kernel,
        out_shape=tiles(ASLOT)[0],
        grid=(16,),
        in_specs=[SMEM, pl.BlockSpec((4, T, T), lambda i: (i, 0, 0))],
        out_specs=pl.BlockSpec((ASLOT, T, T), lambda i: (0, 0, 0)),
        compiler_params=pltpu.CompilerParams(vmem_limit_bytes=32 << 20),
        name="add",
    )(targets, arrived)


def tie(x, *others):
    return lax.optimization_barrier((x,) + others)[0]


def sparse(work, zero, tile, slot, where, queued, queued_far, turn_near, turn_far, end):
    swap = [((z, y, c), (z, y, 1 - c)) for z, y, c in PLACES]
    along_z = [[((z, y, c), (z + s, y, c)) for z, y, c in PLACES] for s in (1, -1)]
    along_y = [[((z, y, c), (z, y + s, c)) for z, y, c in PLACES] for s in (1, -1)]

    def sends(xs, ways):
        return [send(x, way) for x, way in zip(xs, ways)]

    def swaps(xs):
        return [send(x, swap) for x in xs]

    def after(xs, *others):
        return list(lax.optimization_barrier(tuple(xs) + others)[:len(xs)])

    other = send(work, swap)
    root = [send(zero, [((z, y, c), (0, y, c)) for y in range(4) for c in range(2)]) for z in (3, 4, 5)]
    both = arrays(BUF, [work], [other])
    near_list = gather(queued, both, N1, "queue")
    n1 = sends(near_list, along_z)
    far_list = gather(tie(queued_far, *near_list), both, FY1, "queue_far", 1)
    f1 = sends(after(far_list, *root), along_y)
    f2 = sends([x[:FY2] for x in f1], along_y)
    n2 = sends(after([x[:N2] for x in n1], *f1), along_z)
    mixed = send(after([jnp.concatenate([*f1, *f2])], *n1)[0], swap)
    parts = [(cut, mixed) for cut in (0, FY1, 2 * FY1, 2 * FY1 + FY2)]
    far_list = gather(turn_far, both + arrays(YF1, f1, parts[0:2]) + arrays(YF2, f2, parts[2:4]), FZ, "turn_far")
    z1 = sends(after(far_list, *n2), along_z)
    column = jnp.stack(after(root, *f1))
    *n1_other, column_other = swaps(after([*n1, column], *far_list))
    near_sources = both + arrays(ZN1, n1, n1_other) + arrays(ZN2, n2, swaps(n2)) + arrays(ROOT, [column], [column_other])
    near_list = gather(turn_near, near_sources, NY1, "turn_near")
    z2 = sends(after(z1, *near_list), along_z)
    y1 = sends(near_list, along_y)
    z3 = sends(z2, along_z)
    y2 = sends(after([x[:NY2] for x in y1], *z2), along_y)
    z4 = sends(after(z3, *y1), along_z)
    sources = near_sources + arrays(YN1, y1) + arrays(YN2, y2) + arrays(ZF3, z3) + arrays(ZF4, z4)
    own, theirs = add_up(where, end, sources)
    return own + send(theirs, swap)


def local(front, pivot_tiles, send_table):
    place = lax.axis_index("front").astype(jnp.int32)
    leaf = lax.axis_index("leaf").astype(jnp.int32)
    where = jnp.stack([leaf // 8, (leaf // 2) % 4, leaf % 2])
    table = send_table[0, 0]
    used = table[0] >= 0
    tile = jnp.where(used, table[0] * 7 + table[1] - 1, -1)
    code = jnp.where(used, tile * 16 + table[2], -1)
    up = [(i, (i + 1) % 4) for i in range(4)]
    down = [(i, (i - 1) % 4) for i in range(4)]
    own = [[front[0, r, 0, :, k * T:k * T + T].astype(F32) for k in range(2)] for r in range(2)]
    def across(x, shift, *others):
        return lax.ppermute(tie(x, *others) if others else x, "front", [(i, (i + shift) % 4) for i in range(4)])

    left00 = across(own[0][0], 1)
    right0 = across(jnp.stack(own[0]), -1)
    far00 = across(left00, 1)
    far01 = across(right0[1], -1)
    codes = lax.all_to_all(jnp.broadcast_to(tie(code, left00), (64, 64)), "leaf", split_axis=0, concat_axis=0, tiled=True).reshape(32, 128)
    left3 = across(jnp.stack([own[0][1], own[1][0], own[1][1]]), 1, far00)
    right2 = across(jnp.stack([own[1][0], own[1][1]]), -1, far00)
    far10 = across(left3[1], 1)
    far11 = across(right2[1], -1)
    from_left = [[left00, left3[0]], [left3[1], left3[2]]]
    from_right = [[right0[0], right0[1]], [right2[0], right2[1]]]
    from_far = [[far00, far01], [far10, far11]]
    by_q = [own, from_right, from_far, from_left]

    def of_owner(owner, r, k, *after):
        q = lax.rem(owner - place + 4, 4)
        if after:
            q = tie(q, *after)
        out = by_q[0][r][k]
        for i in range(1, 4):
            out = jnp.where(q == i, by_q[i][r][k], out)
        return out

    inv0 = pl.pallas_call(
        first_kernel,
        out_shape=jax.ShapeDtypeStruct((T, T), F32),
        in_specs=[VMEM],
        out_specs=VMEM,
        scratch_shapes=[pltpu.VMEM((B, 128), F32)],
        compiler_params=pltpu.CompilerParams(vmem_limit_bytes=16 << 20),
        cost_estimate=pl.CostEstimate(flops=0, bytes_accessed=20 << 20, transcendentals=0),
        name="first",
    )(of_owner(0, 0, 0))
    *tables, over = pl.pallas_call(
        plan_kernel,
        out_shape=tuple(jax.ShapeDtypeStruct((n, 128), jnp.int32) for n in (1, 1, 1, 1, 32)) + (jax.ShapeDtypeStruct((1, 1), F32),),
        in_specs=[SMEM, VMEM],
        out_specs=(VMEM,) * 6,
        cost_estimate=pl.CostEstimate(flops=0, bytes_accessed=6 << 20, transcendentals=0),
        name="plan",
    )(where, tie(codes, inv0))
    w10 = of_owner(1, 0, 0, inv0)
    w11 = of_owner(1, 0, 1, inv0)
    l10, inv1 = pl.pallas_call(
        second_kernel,
        out_shape=(jax.ShapeDtypeStruct((T, T), F32),) * 2,
        in_specs=[SMEM, VMEM, VMEM, VMEM],
        out_specs=(VMEM, VMEM),
        scratch_shapes=[pltpu.VMEM((B, 128), F32)],
        compiler_params=pltpu.CompilerParams(vmem_limit_bytes=16 << 20),
        cost_estimate=pl.CostEstimate(flops=0, bytes_accessed=40 << 20, transcendentals=0),
        name="second",
    )(pivot_tiles, inv0, w10, w11)

    received = [by_q[q][r][k] for q in range(1, 4) for r in range(2) for k in range(2)]
    factor, work, zero = pl.pallas_call(
        panel_kernel,
        out_shape=(jax.ShapeDtypeStruct((1, 2, 1, T, 2 * T), F32),) + tiles(TILES) + (jax.ShapeDtypeStruct((T, T), F32),),
        in_specs=[SMEM, SMEM] + [VMEM] * 16,
        out_specs=(VMEM, VMEM, VMEM),
        scratch_shapes=[pltpu.VMEM((8, T, 2 * T), BF16), pltpu.VMEM((8, T, 2 * T), BF16)],
        compiler_params=pltpu.CompilerParams(vmem_limit_bytes=40 << 20),
        cost_estimate=pl.CostEstimate(flops=0, bytes_accessed=40 << 20, transcendentals=0),
        name="panel",
    )(place.reshape(1), tile[0:1], inv0, l10, inv1, front, *received)
    ancestor = lax.cond(over[0, 0] > 0.0, dense, sparse, work, zero, tile, table[2], where, *tables)
    return (factor, ancestor.reshape(1, 1, ASLOT, T, T))


def solution(mesh):
    in_specs = (P("leaf", None, "front", None, None), P("leaf"), P("leaf", "front", None, None))
    out_specs = (P("leaf", None, "front", None, None), P("leaf", "front", None, None, None))
    return jax.shard_map(local, mesh=mesh, in_specs=in_specs, out_specs=out_specs, check_vma=False)
```

```python
import functools

import jax
import jax.numpy as jnp
from jax import lax
from jax.experimental import pallas as pl
from jax.experimental.pallas import tpu as pltpu
from jax.sharding import PartitionSpec as P

PT = 2
ASLOT = 16
TILES = 14
N1, N2 = 8, 5
FY1, FY2 = 5, 3
FZ, FZ4 = 5, 4
NY1, NY2 = 11, 7
BUF, ZN1, ZN2, YF1, YF2, YN1, YN2, ZF3, ZF4, ROOT = range(10)
B = 64
T = 256
F32 = jnp.float32
BF16 = jnp.bfloat16
HIGHEST = lax.Precision.HIGHEST
VMEM = pl.BlockSpec(memory_space=pltpu.VMEM)
SMEM = pl.BlockSpec(memory_space=pltpu.SMEM)
ANY = pl.BlockSpec(memory_space=pl.ANY)
NN = (((1,), (0,)), ((), ()))
NT = (((1,), (1,)), ((), ()))
TN = (((0,), (0,)), ((), ()))


def dot(a, b, dims):
    return lax.dot_general(a, b, dims, precision=HIGHEST, preferred_element_type=F32)


def dot1(a, b, dims):
    return lax.dot_general(a, b, dims, preferred_element_type=F32)


def split(x):
    high = x.astype(BF16)
    return high, (x - high.astype(F32)).astype(BF16)


def split3(x):
    high = x.astype(BF16)
    rest = x - high.astype(F32)
    mid = rest.astype(BF16)
    return high, mid, (rest - mid.astype(F32)).astype(BF16)


def dot3(a, b, dims):
    ah, al = a
    bh, bl = b
    return dot1(ah, bh, dims) + (dot1(ah, bl, dims) + dot1(al, bh, dims))


def factor64(groups, f_ref):
    sub = lax.broadcasted_iota(jnp.int32, (8, 128), 0)

    def body(it, gs):
        count = len(gs)
        cols = [[jnp.broadcast_to(g[:, t:t + 1], (8, 128)) for t in range(8)] for g in gs]
        rows = [jnp.broadcast_to(gs[0][t:t + 1, :], (8, 128)) for t in range(8)]
        s = [[jnp.broadcast_to(cols[0][t][u:u + 1, :], (8, 128)) if u >= t else None for t in range(8)] for u in range(8)]
        inv = [None] * 8
        for t in range(8):
            inv[t] = 1.0 / s[t][t]
            for u in range(t + 1, 8):
                low = s[u][t] * inv[t]
                for v in range(u, 8):
                    s[v][u] = s[v][u] - low * s[v][t]
                rows[u] = rows[u] - low * rows[t]
                for g in range(1, count):
                    cols[g][u] = cols[g][u] - low * cols[g][t]
        done = jnp.zeros((8, 128), F32)
        for t in range(8):
            done = jnp.where(sub == t, rows[t] * lax.rsqrt(s[t][t]), done)
        f_ref[pl.ds(pl.multiple_of(it * 8, 8), 8), :] = pltpu.roll(done, it * 8, 1)
        scaled = [rows[t] * inv[t] for t in range(8)]
        left = []
        for g in range(1, count):
            piece = gs[g]
            for t in range(8):
                piece = piece - cols[g][t] * scaled[t]
            left.append(pltpu.roll(piece, 120, 1))
        left.append(gs[0])
        return tuple(left)

    groups = tuple(groups)
    for first in range(0, 8, 2):
        groups = lax.fori_loop(first, first + 2, body, groups)[:6 - first]


def factor256(x_ref, f_ref):
    lane = lax.broadcasted_iota(jnp.int32, (B, 128), 1)
    row = lax.broadcasted_iota(jnp.int32, (B, 128), 0)
    ident = (lane - B == row).astype(F32)
    col = lax.broadcasted_iota(jnp.int32, (B, T), 1)
    wide_row = lax.broadcasted_iota(jnp.int32, (B, T), 0)
    for k in range(T // B):
        lo = k * B
        strip = x_ref[lo:lo + B, :]
        block = strip[:, (k // 2) * 128:(k // 2) * 128 + 128]
        if k % 2:
            block = pltpu.roll(block, B, 1)
        both = jnp.where(lane < B, block, ident)
        factor64([both[8 * g:8 * g + 8, :] for g in range(8)], f_ref)
        block_inv = f_ref[...][:, B:]
        inside = (col >= lo) & (col < lo + B)
        strip = jnp.where(inside, (col - lo == wide_row).astype(F32), strip)
        out = dot(block_inv, strip, NN)
        x_ref[lo:lo + B, :] = jnp.where(col < lo + B, out, 0.0)
        if lo + B < T:
            rest = T - lo - B
            rest_col = lax.broadcasted_iota(jnp.int32, (rest, T), 1)
            old = x_ref[lo + B:, :]
            old = jnp.where((rest_col >= lo) & (rest_col < lo + B), 0.0, old)
            x_ref[lo + B:, :] = old - dot(out[:, lo + B:], out, TN)


def first_kernel(w00_ref, inv0_ref, f_ref):
    inv0_ref[...] = w00_ref[...]
    factor256(inv0_ref, f_ref)


def second_kernel(piv_ref, inv0_ref, w10_ref, w11_ref, l10_ref, inv1_ref, f_ref):
    l10 = dot(w10_ref[...], inv0_ref[...], NT)
    l10_ref[...] = l10
    inv1_ref[...] = jnp.zeros((T, T), F32)

    @pl.when(piv_ref[0] >= 2)
    def _():
        inv1_ref[...] = w11_ref[...] - dot(l10, l10, NT)
        factor256(inv1_ref, f_ref)


def iota(shape, dim):
    return lax.broadcasted_iota(jnp.int32, shape, dim)


def fdot(a, b):
    return lax.dot_general(a, b, (((1,), (0,)), ((), ())), preferred_element_type=F32)


def route(codes, z, y, c):
    shape, sq, rows = (32, 128), (128, 128), (32, 32)
    row, lane = iota(shape, 0), iota(shape, 1)
    zs, ys = row // 4, row % 4
    cs, zd, yd, cd = lane // 64, (lane // 8) % 8, (lane // 2) % 4, lane % 2
    dz, dy = (zd - zs + 8) % 8, (yd - ys + 4) % 4
    hops = jnp.minimum(dz, 8 - dz)
    far = hops > 2
    used = codes >= 0
    rooted = used & (lane % 64 == 0) & far
    live = used & ~rooted
    near = used & (~far | rooted)
    tile = jnp.where(used, codes // 16, 0)
    slot = jnp.where(used, codes % 16, 0)
    la, lb = iota(sq, 0), iota(sq, 1)
    before = la < lb
    same_zd = (la // 8) % 8 == (lb // 8) % 8
    same_yd = (la // 2) % 4 == (lb // 2) % 4
    ra, rb = iota(rows, 0), iota(rows, 1)
    same_ys = ra % 4 == rb % 4
    same_zs = ra // 4 == rb // 4

    def f(x):
        return x.astype(F32)

    def count(mask, lanes, peers):
        rank = fdot(f(mask), f(before & lanes))
        total = fdot(f(mask), f(lanes))
        if peers is not None:
            rank = rank + fdot(f(peers & (rb < ra)), total)
            total = fdot(f(peers), total)
        return rank, total

    def halves(n_up, n_both, n_down):
        up = jnp.clip(jnp.floor((n_both + n_down - n_up + 1.0) * 0.5), 0.0, n_both)
        return up, n_both - up

    every = la >= 0
    over = jnp.full(shape, -1.0, F32)
    r1, n1 = count(live & (dz == 1), every, None)
    r2, n2 = count(live & (dz == 2), every, None)
    r6, n6 = count(live & (dz == 6), every, None)
    r7, n7 = count(live & (dz == 7), every, None)
    zpos = jnp.where(dz == 1, n2 + r1, jnp.where(dz == 2, r2, jnp.where(dz == 6, r6, n6 + r7)))
    over = jnp.maximum(over, jnp.maximum(n1 + n2, n7 + n6) - 2 * N1)
    over = jnp.maximum(over, jnp.maximum(n2, n6) - 2 * N2)

    def ring(mask, lanes, peers, near, distant):
        a1, m1 = count(mask & (dy == 1), lanes, peers)
        a2, m2 = count(mask & (dy == 2), lanes, peers)
        a3, m3 = count(mask & (dy == 3), lanes, peers)
        up, down = halves(m1, m2, m3)
        minus = (dy == 3) | ((dy == 2) & (a2 >= up))
        pos = jnp.where(dy == 1, up + a1, jnp.where(dy == 3, down + a3, jnp.where(a2 < up, a2, a2 - up)))
        excess = jnp.maximum(jnp.maximum(up + m1, down + m3) - near, jnp.maximum(up, down) - distant)
        return minus.astype(jnp.int32), pos.astype(jnp.int32), excess

    fy_way, fy_pos, excess = ring(live & far, every, None, 2 * FY1, 2 * FY2)
    over = jnp.maximum(over, excess)
    r3, n3 = count(live & (dz == 3), same_yd, same_zs)
    r4, n4 = count(live & (dz == 4), same_yd, same_zs)
    r5, n5 = count(live & (dz == 5), same_yd, same_zs)
    up, down = halves(n3, n4, n5)
    fz_pos = jnp.where(dz == 3, up + r3, jnp.where(dz == 5, down + r5, jnp.where(r4 < up, r4, r4 - up)))
    over = jnp.maximum(over, jnp.maximum(up + n3, down + n5) - 2 * FZ)
    over = jnp.maximum(over, jnp.maximum(up, down) - 2 * FZ4)
    z_way = ((dz > 4) | ((dz == 4) & (r4 >= up))).astype(jnp.int32)
    ny_way, ny_pos, excess = ring(near, same_zd, same_ys, 2 * NY1, 2 * NY2)
    over = jnp.maximum(over, excess)
    zpos, fz_pos = zpos.astype(jnp.int32), fz_pos.astype(jnp.int32)

    def at(kind, way, pos):
        return ((kind * 2 + way) * 2 + (pos % 2 != c)) * 16 + pos // 2

    def listed(mask, way, pos, code):
        key = jnp.where(mask & (pos % 2 == c), way * 16 + pos // 2, -1)
        acc = jnp.zeros(shape, jnp.int32)
        for r in range(32):
            acc = acc + jnp.where(key[r:r + 1, :] == row, code[r:r + 1, :] + 1, 0)
        column = jnp.sum(acc, axis=1, keepdims=True)
        return jnp.sum(jnp.where(lane == row, column, 0), axis=0, keepdims=True) - 1

    held = (BUF * 4 + (cs != c)) * 16 + tile
    here = live & (row == z * 4 + y)
    queued = listed(here & ~far & (dz > 0), z_way, zpos, held)
    queued_far = listed(here & far & (dy > 0), fy_way, fy_pos, held)
    after_y = jnp.where(dy == 0, held, at(jnp.where(dy == 2, YF2, YF1), fy_way, fy_pos))
    turn_far = listed(live & far & (zs == z) & (yd == y), z_way, fz_pos, after_y)
    after_z = jnp.where(dz == 0, held, at(jnp.where(hops == 1, ZN1, ZN2), z_way, zpos))
    after_z = jnp.where(rooted, (ROOT * 4 + (cs != c)) * 16 + zs - 3, after_z)
    turn_near = listed(near & (zd == z) & (ys == y) & (dy > 0), ny_way, ny_pos, after_z)
    end_near = jnp.where(dy == 0, after_z, at(jnp.where(dy == 2, YN2, YN1), ny_way, ny_pos))
    end_far = at(jnp.where(dz == 4, ZF4, ZF3), z_way, fz_pos)
    keeper = jnp.where(far & ~rooted, fz_pos % 2, jnp.where(dy > 0, ny_pos % 2, cd))
    mine = used & (zd == z) & (yd == y) & (keeper == c)
    end = jnp.where(mine, (jnp.where(live & far, end_far, end_near) * 2 + (cd != c)) * 16 + slot, -1)
    return queued, queued_far, turn_near, turn_far, end, jnp.max(over, keepdims=True)


def plan_kernel(where_ref, codes_ref, *out_refs):
    for ref, value in zip(out_refs, route(codes_ref[...], where_ref[0], where_ref[1], where_ref[2])):
        ref[...] = value


def panel_kernel(place_ref, first_ref, inv0_ref, l10_ref, inv1_ref, front_ref, *refs):
    pieces = refs[:12]
    factor_ref, out_ref, zero_ref, yh_ref, yl_ref = refs[12:]
    place = place_ref[0]
    a0 = split3(inv0_ref[...])
    low = split(l10_ref[...])
    inv1 = inv1_ref[...]
    for q in range(4):
        for r in range(2):
            if q == 0:
                p0 = front_ref[0, r, 0, :, 0:T]
                p1 = front_ref[0, r, 0, :, T:2 * T].astype(F32)
            else:
                p0 = pieces[(q - 1) * 4 + r * 2][...].astype(BF16)
                p1 = pieces[(q - 1) * 4 + r * 2 + 1][...]
            y0 = dot1(p0, a0[0], NT) + (dot1(p0, a0[1], NT) + dot1(p0, a0[2], NT))
            y0h, y0l = split(y0)
            p1 = p1 - dot3((y0h, y0l), low, NT)
            y1 = dot(p1, inv1, NT)
            if r == 0:
                owner = lax.rem(place + q, 4)
                y1 = jnp.where(owner > 0, y1, 0.0)
            y1h, y1l = split(y1)
            n = q * 2 + r
            yh_ref[n, :, 0:T] = y0h
            yl_ref[n, :, 0:T] = y0l
            yh_ref[n, :, T:2 * T] = y1h
            yl_ref[n, :, T:2 * T] = y1l
            if q == 0:
                factor_ref[0, r, 0, :, 0:T] = y0
                factor_ref[0, r, 0, :, T:2 * T] = y1
    for r in range(2):
        for n in range(8):
            column = lax.rem(place + n // 2, 4) + 4 * (n % 2)

            @pl.when(column > 0)
            def _():
                start = pl.multiple_of(column * T, T)
                tile = front_ref[0, r, 0, :, pl.ds(start, T)].astype(F32)
                own = (yh_ref[r], yl_ref[r])
                other = (yh_ref[n], yl_ref[n])
                tile = tile - dot3(own, other, NT)
                index = r * 7 + column - 1
                out_ref[index] = tile

                @pl.when(index == first_ref[0])
                def _():
                    zero_ref[...] = tile


def arrays(kind, own, other=()):
    out = []
    for sib, xs in ((0, own), (1, other)):
        for way, x in enumerate(xs):
            out.append(((kind * 2 + way) * 2 + sib,) + (x if isinstance(x, tuple) else (0, x)))
    return out


def copy_from(sources, code, target_ref, sem):
    for sid, first, ref in sources:
        @pl.when(code // 16 == sid)
        def _():
            pltpu.make_async_copy(ref.at[first + code % 16], target_ref, sem).start()


def operands(sources):
    xs, numbered = [], []
    for sid, first, x in sources:
        where = [i for i, other in enumerate(xs) if other is x]
        if not where:
            xs.append(x)
        numbered.append((sid, first, where[0] if where else len(xs) - 1))
    return numbered, xs


def gather_kernel(numbered, size, table_ref, *refs):
    sources = [(sid, first, refs[i]) for sid, first, i in numbered]
    *outs, sem = refs[-3:]
    for way, out in enumerate(outs):
        def start(i, _):
            code = table_ref[0, way * 16 + i]

            @pl.when(code >= 0)
            def _():
                copy_from(sources, code, out.at[i], sem.at[way * size + i])
            return 0

        lax.fori_loop(0, size, start, 0)
    for way, out in enumerate(outs):
        def wait(i, _):
            @pl.when(table_ref[0, way * 16 + i] >= 0)
            def _():
                pltpu.make_async_copy(refs[0].at[0], out.at[i], sem.at[way * size + i]).wait()
            return 0

        lax.fori_loop(0, size, wait, 0)


def gather(table, sources, size, name, *first):
    numbered, xs = operands(sources)
    xs = xs + list(first)
    return pl.pallas_call(
        lambda *refs: gather_kernel(numbered, size, *refs),
        out_shape=tiles(size, size),
        in_specs=[SMEM] + [ANY] * len(xs),
        out_specs=(VMEM,) * 2,
        scratch_shapes=[pltpu.SemaphoreType.DMA((2 * size,))],
        compiler_params=pltpu.CompilerParams(vmem_limit_bytes=10 << 20),
        cost_estimate=pl.CostEstimate(flops=0, bytes_accessed=8 << 20, transcendentals=0),
        name=name,
    )(table, *xs)


DEPTH = 12


def sum_kernel(numbered, other, where_ref, table_ref, *refs):
    *ins, out_ref, list_ref, buf_ref, sem = refs
    z, y = where_ref[0], where_ref[1]
    sources = [(sid, first, ins[i]) for sid, first, i in numbered]

    def collect(i, n):
        code = table_ref[i // 4, (i // 2 % 2) * 64 + z * 8 + y * 2 + i % 2]

        take = (code >= 0) & ((code // 16) % 2 == other)

        @pl.when(take)
        def _():
            list_ref[n] = code
        return n + take.astype(jnp.int32)

    n = lax.fori_loop(0, 128, collect, jnp.int32(0))

    def start(i):
        slot = lax.rem(i, DEPTH)
        copy_from(sources, list_ref[i] // 32, buf_ref.at[slot], sem.at[slot])

    def prime(i, _):
        start(i)
        return 0

    def step(i, _):
        slot = lax.rem(i, DEPTH)
        pltpu.make_async_copy(ins[0].at[0], buf_ref.at[slot], sem.at[slot]).wait()
        out_ref[list_ref[i] % 16] += buf_ref[slot]

        @pl.when(i + DEPTH < n)
        def _():
            start(i + DEPTH)
        return 0

    lax.fori_loop(0, jnp.minimum(n, DEPTH), prime, 0)
    out_ref[...] = jnp.zeros_like(out_ref)
    lax.fori_loop(0, n, step, 0)


def add_up(where, table, sources, other):
    numbered, xs = operands(sources)
    return pl.pallas_call(
        lambda *refs: sum_kernel(numbered, other, *refs),
        out_shape=tiles(ASLOT)[0],
        in_specs=[SMEM, SMEM] + [ANY] * len(xs),
        out_specs=VMEM,
        scratch_shapes=[pltpu.SMEM((256,), jnp.int32), pltpu.VMEM((DEPTH, T, T), F32), pltpu.SemaphoreType.DMA((DEPTH,))],
        compiler_params=pltpu.CompilerParams(vmem_limit_bytes=16 << 20),
        cost_estimate=pl.CostEstimate(flops=0, bytes_accessed=30 << 20, transcendentals=0),
        name="sum_other" if other else "sum_own",
    )(where, table, *xs)


def slots_kernel(tile_ref, own_ref, out_ref, sem):
    def start(p, _):
        tile = tile_ref[p]

        @pl.when(tile >= 0)
        def _():
            pltpu.make_async_copy(own_ref.at[tile], out_ref.at[p], sem.at[p]).start()
        return 0

    def wait(p, _):
        @pl.when(tile_ref[p] >= 0)
        def _():
            pltpu.make_async_copy(own_ref.at[0], out_ref.at[p], sem.at[p]).wait()
        return 0

    lax.fori_loop(0, 64, start, 0)
    lax.fori_loop(0, 64, wait, 0)


def add_kernel(target_ref, arrived_ref, out_ref):
    step = pl.program_id(0)

    @pl.when(step == 0)
    def _():
        out_ref[...] = jnp.zeros_like(out_ref)

    for i in range(4):
        target = target_ref[step * 4 + i]

        @pl.when(target >= 0)
        def _():
            out_ref[target] += arrived_ref[i]


def tiles(*counts):
    return tuple(jax.ShapeDtypeStruct((n, T, T), F32) for n in counts)


def leaf_id(z, y, c):
    return ((z % 8) * 4 + y % 4) * 2 + c


PLACES = [(z, y, c) for z in range(8) for y in range(4) for c in range(2)]


def send(x, pairs):
    return lax.ppermute(x, "leaf", [(leaf_id(*a), leaf_id(*b)) for a, b in pairs])


def dense(work, zero, tile, slot, where, *tables):
    outgoing = pl.pallas_call(
        slots_kernel,
        out_shape=tiles(64)[0],
        in_specs=[SMEM, ANY],
        out_specs=ANY,
        scratch_shapes=[pltpu.SemaphoreType.DMA((64,))],
        name="slots",
    )(tile, work)
    arrived = lax.all_to_all(outgoing, "leaf", split_axis=0, concat_axis=0, tiled=True)
    targets = lax.all_to_all(slot, "leaf", split_axis=0, concat_axis=0, tiled=True)
    return pl.pallas_call(
        add_kernel,
        out_shape=tiles(ASLOT)[0],
        grid=(16,),
        in_specs=[SMEM, pl.BlockSpec((4, T, T), lambda i: (i, 0, 0))],
        out_specs=pl.BlockSpec((ASLOT, T, T), lambda i: (0, 0, 0)),
        compiler_params=pltpu.CompilerParams(vmem_limit_bytes=32 << 20),
        name="add",
    )(targets, arrived)


def tie(x, *others):
    return lax.optimization_barrier((x,) + others)[0]


def sparse(work, zero, tile, slot, where, queued, queued_far, turn_near, turn_far, end):
    swap = [((z, y, c), (z, y, 1 - c)) for z, y, c in PLACES]
    along_z = [[((z, y, c), (z + s, y, c)) for z, y, c in PLACES] for s in (1, -1)]
    along_y = [[((z, y, c), (z, y + s, c)) for z, y, c in PLACES] for s in (1, -1)]

    def sends(xs, ways):
        return [send(x, way) for x, way in zip(xs, ways)]

    def swaps(xs):
        return [send(x, swap) for x in xs]

    def after(xs, *others):
        return list(lax.optimization_barrier(tuple(xs) + others)[:len(xs)])

    other = send(work, swap)
    root = [send(zero, [((z, y, c), (0, y, c)) for y in range(4) for c in range(2)]) for z in (3, 4, 5)]
    both = arrays(BUF, [work], [other])
    near_list = gather(queued, both, N1, "queue")
    n1 = sends(near_list, along_z)
    far_list = gather(tie(queued_far, *near_list), both, FY1, "queue_far")
    f1 = sends(after(far_list, *root), along_y)
    f2 = sends([x[:FY2] for x in f1], along_y)
    n2 = sends(after([x[:N2] for x in n1], *f1), along_z)
    mixed = send(after([jnp.concatenate([*f1, *f2])], *n1)[0], swap)
    parts = [(cut, mixed) for cut in (0, FY1, 2 * FY1, 2 * FY1 + FY2)]
    column = jnp.stack(after(root, *f1))
    column_other = send(after([column], *n1)[0], swap)
    far_list = gather(turn_far, both + arrays(YF1, f1, parts[0:2]) + arrays(YF2, f2, parts[2:4]), FZ, "turn_far", column_other)
    n1_other = swaps(after(n1, *far_list))
    z1 = sends(after(far_list, *n2, *n1_other), along_z)
    near_sources = both + arrays(ZN1, n1, n1_other) + arrays(ZN2, n2, swaps(n2)) + arrays(ROOT, [column], [column_other])
    near_list = gather(turn_near, near_sources, NY1, "turn_near")
    z2 = sends(after(z1, *near_list), along_z)
    y1 = sends(near_list, along_y)
    z3 = sends(z2, along_z)
    y2 = sends(after([x[:NY2] for x in y1], *z2), along_y)
    z4 = sends(after([x[:FZ4] for x in z3], *y1), along_z)
    sources = near_sources + arrays(YN1, y1) + arrays(YN2, y2) + arrays(ZF3, z3) + arrays(ZF4, z4)
    theirs = add_up(where, end, sources, 1)
    own = add_up(tie(where, theirs), end, sources, 0)
    return own + send(theirs, swap)


def local(front, pivot_tiles, send_table):
    place = lax.axis_index("front").astype(jnp.int32)
    leaf = lax.axis_index("leaf").astype(jnp.int32)
    where = jnp.stack([leaf // 8, (leaf // 2) % 4, leaf % 2])
    table = send_table[0, 0]
    used = table[0] >= 0
    tile = jnp.where(used, table[0] * 7 + table[1] - 1, -1)
    code = jnp.where(used, tile * 16 + table[2], -1)
    up = [(i, (i + 1) % 4) for i in range(4)]
    down = [(i, (i - 1) % 4) for i in range(4)]
    own = [[front[0, r, 0, :, k * T:k * T + T].astype(F32) for k in range(2)] for r in range(2)]
    def across(x, shift, *others):
        return lax.ppermute(tie(x, *others) if others else x, "front", [(i, (i + shift) % 4) for i in range(4)])

    left00 = across(own[0][0], 1)
    right0 = across(jnp.stack(own[0]), -1)
    far00 = across(left00, 1)
    far01 = across(right0[1], -1)
    left3 = across(jnp.stack([own[0][1], own[1][0], own[1][1]]), 1, far00)
    right2 = across(jnp.stack([own[1][0], own[1][1]]), -1, far00)
    far10 = across(left3[1], 1)
    far11 = across(right2[1], -1)
    from_left = [[left00, left3[0]], [left3[1], left3[2]]]
    from_right = [[right0[0], right0[1]], [right2[0], right2[1]]]
    from_far = [[far00, far01], [far10, far11]]
    by_q = [own, from_right, from_far, from_left]

    def of_owner(owner, r, k, *after):
        q = lax.rem(owner - place + 4, 4)
        if after:
            q = tie(q, *after)
        out = by_q[0][r][k]
        for i in range(1, 4):
            out = jnp.where(q == i, by_q[i][r][k], out)
        return out

    inv0 = pl.pallas_call(
        first_kernel,
        out_shape=jax.ShapeDtypeStruct((T, T), F32),
        in_specs=[VMEM],
        out_specs=VMEM,
        scratch_shapes=[pltpu.VMEM((B, 128), F32)],
        compiler_params=pltpu.CompilerParams(vmem_limit_bytes=16 << 20),
        cost_estimate=pl.CostEstimate(flops=0, bytes_accessed=20 << 20, transcendentals=0),
        name="first",
    )(of_owner(0, 0, 0))
    codes = lax.all_to_all(jnp.broadcast_to(tie(code, inv0), (64, 64)), "leaf", split_axis=0, concat_axis=0, tiled=True).reshape(32, 128)
    *tables, over = pl.pallas_call(
        plan_kernel,
        out_shape=tuple(jax.ShapeDtypeStruct((n, 128), jnp.int32) for n in (1, 1, 1, 1, 32)) + (jax.ShapeDtypeStruct((1, 1), F32),),
        in_specs=[SMEM, VMEM],
        out_specs=(VMEM,) * 6,
        cost_estimate=pl.CostEstimate(flops=0, bytes_accessed=6 << 20, transcendentals=0),
        name="plan",
    )(where, codes)
    w10 = of_owner(1, 0, 0, inv0)
    w11 = of_owner(1, 0, 1, inv0)
    l10, inv1 = pl.pallas_call(
        second_kernel,
        out_shape=(jax.ShapeDtypeStruct((T, T), F32),) * 2,
        in_specs=[SMEM, VMEM, VMEM, VMEM],
        out_specs=(VMEM, VMEM),
        scratch_shapes=[pltpu.VMEM((B, 128), F32)],
        compiler_params=pltpu.CompilerParams(vmem_limit_bytes=16 << 20),
        cost_estimate=pl.CostEstimate(flops=0, bytes_accessed=40 << 20, transcendentals=0),
        name="second",
    )(pivot_tiles, inv0, w10, w11)

    received = [by_q[q][r][k] for q in range(1, 4) for r in range(2) for k in range(2)]
    factor, work, zero = pl.pallas_call(
        panel_kernel,
        out_shape=(jax.ShapeDtypeStruct((1, 2, 1, T, 2 * T), F32),) + tiles(TILES) + (jax.ShapeDtypeStruct((T, T), F32),),
        in_specs=[SMEM, SMEM] + [VMEM] * 16,
        out_specs=(VMEM, VMEM, VMEM),
        scratch_shapes=[pltpu.VMEM((8, T, 2 * T), BF16), pltpu.VMEM((8, T, 2 * T), BF16)],
        compiler_params=pltpu.CompilerParams(vmem_limit_bytes=40 << 20),
        cost_estimate=pl.CostEstimate(flops=0, bytes_accessed=40 << 20, transcendentals=0),
        name="panel",
    )(place.reshape(1), tile[0:1], inv0, l10, inv1, front, *received)
    ancestor = lax.cond(over[0, 0] > 0.0, dense, sparse, work, zero, tile, table[2], where, *tables)
    return (factor, ancestor.reshape(1, 1, ASLOT, T, T))


def solution(mesh):
    in_specs = (P("leaf", None, "front", None, None), P("leaf"), P("leaf", "front", None, None))
    out_specs = (P("leaf", None, "front", None, None), P("leaf", "front", None, None, None))
    return jax.shard_map(local, mesh=mesh, in_specs=in_specs, out_specs=out_specs, check_vma=False)
```

```python
import functools

import jax
import jax.numpy as jnp
from jax import lax
from jax.experimental import pallas as pl
from jax.experimental.pallas import tpu as pltpu
from jax.sharding import PartitionSpec as P

PT = 2
ASLOT = 16
TILES = 14
N1, N2 = 8, 5
FY1, FY2 = 5, 3
FZ, FZ4 = 5, 4
NY1, NY2 = 11, 7
BUF, ZN1, ZN2, YF1, YF2, YN1, YN2, ZF3, ZF4, ROOT = range(10)
B = 64
T = 256
F32 = jnp.float32
BF16 = jnp.bfloat16
HIGHEST = lax.Precision.HIGHEST
VMEM = pl.BlockSpec(memory_space=pltpu.VMEM)
SMEM = pl.BlockSpec(memory_space=pltpu.SMEM)
ANY = pl.BlockSpec(memory_space=pl.ANY)
NN = (((1,), (0,)), ((), ()))
NT = (((1,), (1,)), ((), ()))
TN = (((0,), (0,)), ((), ()))


def dot(a, b, dims):
    return lax.dot_general(a, b, dims, precision=HIGHEST, preferred_element_type=F32)


def dot1(a, b, dims):
    return lax.dot_general(a, b, dims, preferred_element_type=F32)


def split(x):
    high = x.astype(BF16)
    return high, (x - high.astype(F32)).astype(BF16)


def split3(x):
    high = x.astype(BF16)
    rest = x - high.astype(F32)
    mid = rest.astype(BF16)
    return high, mid, (rest - mid.astype(F32)).astype(BF16)


def dot3(a, b, dims):
    ah, al = a
    bh, bl = b
    return dot1(ah, bh, dims) + (dot1(ah, bl, dims) + dot1(al, bh, dims))


def factor64(groups, f_ref):
    sub = lax.broadcasted_iota(jnp.int32, (8, 128), 0)

    def body(it, gs):
        count = len(gs)
        cols = [[jnp.broadcast_to(g[:, t:t + 1], (8, 128)) for t in range(8)] for g in gs]
        rows = [jnp.broadcast_to(gs[0][t:t + 1, :], (8, 128)) for t in range(8)]
        s = [[jnp.broadcast_to(cols[0][t][u:u + 1, :], (8, 128)) if u >= t else None for t in range(8)] for u in range(8)]
        inv = [None] * 8
        for t in range(8):
            inv[t] = 1.0 / s[t][t]
            for u in range(t + 1, 8):
                low = s[u][t] * inv[t]
                for v in range(u, 8):
                    s[v][u] = s[v][u] - low * s[v][t]
                rows[u] = rows[u] - low * rows[t]
                for g in range(1, count):
                    cols[g][u] = cols[g][u] - low * cols[g][t]
        done = jnp.zeros((8, 128), F32)
        for t in range(8):
            done = jnp.where(sub == t, rows[t] * lax.rsqrt(s[t][t]), done)
        f_ref[pl.ds(pl.multiple_of(it * 8, 8), 8), :] = pltpu.roll(done, it * 8, 1)
        scaled = [rows[t] * inv[t] for t in range(8)]
        left = []
        for g in range(1, count):
            piece = gs[g]
            for t in range(8):
                piece = piece - cols[g][t] * scaled[t]
            left.append(pltpu.roll(piece, 120, 1))
        left.append(gs[0])
        return tuple(left)

    groups = tuple(groups)
    for first in range(0, 8, 2):
        groups = lax.fori_loop(first, first + 2, body, groups)[:6 - first]


def factor256(x_ref, f_ref):
    lane = lax.broadcasted_iota(jnp.int32, (B, 128), 1)
    row = lax.broadcasted_iota(jnp.int32, (B, 128), 0)
    ident = (lane - B == row).astype(F32)
    col = lax.broadcasted_iota(jnp.int32, (B, T), 1)
    wide_row = lax.broadcasted_iota(jnp.int32, (B, T), 0)
    for k in range(T // B):
        lo = k * B
        strip = x_ref[lo:lo + B, :]
        block = strip[:, (k // 2) * 128:(k // 2) * 128 + 128]
        if k % 2:
            block = pltpu.roll(block, B, 1)
        both = jnp.where(lane < B, block, ident)
        factor64([both[8 * g:8 * g + 8, :] for g in range(8)], f_ref)
        block_inv = f_ref[...][:, B:]
        inside = (col >= lo) & (col < lo + B)
        strip = jnp.where(inside, (col - lo == wide_row).astype(F32), strip)
        out = dot(block_inv, strip, NN)
        x_ref[lo:lo + B, :] = jnp.where(col < lo + B, out, 0.0)
        if lo + B < T:
            rest = T - lo - B
            rest_col = lax.broadcasted_iota(jnp.int32, (rest, T), 1)
            old = x_ref[lo + B:, :]
            old = jnp.where((rest_col >= lo) & (rest_col < lo + B), 0.0, old)
            x_ref[lo + B:, :] = old - dot(out[:, lo + B:], out, TN)


def first_kernel(w00_ref, inv0_ref, f_ref):
    inv0_ref[...] = w00_ref[...]
    factor256(inv0_ref, f_ref)


def second_kernel(piv_ref, inv0_ref, w10_ref, w11_ref, l10_ref, inv1_ref, f_ref):
    l10 = dot(w10_ref[...], inv0_ref[...], NT)
    l10_ref[...] = l10
    inv1_ref[...] = jnp.zeros((T, T), F32)

    @pl.when(piv_ref[0] >= 2)
    def _():
        inv1_ref[...] = w11_ref[...] - dot(l10, l10, NT)
        factor256(inv1_ref, f_ref)


def iota(shape, dim):
    return lax.broadcasted_iota(jnp.int32, shape, dim)


def fdot(a, b):
    return lax.dot_general(a, b, (((1,), (0,)), ((), ())), preferred_element_type=F32)


def route(codes, z, y, c):
    shape, sq, rows = (32, 128), (128, 128), (32, 32)
    row, lane = iota(shape, 0), iota(shape, 1)
    zs, ys = row // 4, row % 4
    cs, zd, yd, cd = lane // 64, (lane // 8) % 8, (lane // 2) % 4, lane % 2
    dz, dy = (zd - zs + 8) % 8, (yd - ys + 4) % 4
    hops = jnp.minimum(dz, 8 - dz)
    far = hops > 2
    used = codes >= 0
    rooted = used & (lane % 64 == 0) & far
    live = used & ~rooted
    near = used & (~far | rooted)
    tile = jnp.where(used, codes // 16, 0)
    slot = jnp.where(used, codes % 16, 0)
    la, lb = iota(sq, 0), iota(sq, 1)
    before = la < lb
    same_zd = (la // 8) % 8 == (lb // 8) % 8
    same_yd = (la // 2) % 4 == (lb // 2) % 4
    ra, rb = iota(rows, 0), iota(rows, 1)
    same_ys = ra % 4 == rb % 4
    same_zs = ra // 4 == rb // 4

    def f(x):
        return x.astype(F32)

    def count(mask, lanes, peers):
        rank = fdot(f(mask), f(before & lanes))
        total = fdot(f(mask), f(lanes))
        if peers is not None:
            rank = rank + fdot(f(peers & (rb < ra)), total)
            total = fdot(f(peers), total)
        return rank, total

    def halves(n_up, n_both, n_down):
        up = jnp.clip(jnp.floor((n_both + n_down - n_up + 1.0) * 0.5), 0.0, n_both)
        return up, n_both - up

    every = la >= 0
    over = jnp.full(shape, -1.0, F32)
    r1, n1 = count(live & (dz == 1), every, None)
    r2, n2 = count(live & (dz == 2), every, None)
    r6, n6 = count(live & (dz == 6), every, None)
    r7, n7 = count(live & (dz == 7), every, None)
    zpos = jnp.where(dz == 1, n2 + r1, jnp.where(dz == 2, r2, jnp.where(dz == 6, r6, n6 + r7)))
    over = jnp.maximum(over, jnp.maximum(n1 + n2, n7 + n6) - 2 * N1)
    over = jnp.maximum(over, jnp.maximum(n2, n6) - 2 * N2)

    def ring(mask, lanes, peers, near, distant):
        a1, m1 = count(mask & (dy == 1), lanes, peers)
        a2, m2 = count(mask & (dy == 2), lanes, peers)
        a3, m3 = count(mask & (dy == 3), lanes, peers)
        up, down = halves(m1, m2, m3)
        minus = (dy == 3) | ((dy == 2) & (a2 >= up))
        pos = jnp.where(dy == 1, up + a1, jnp.where(dy == 3, down + a3, jnp.where(a2 < up, a2, a2 - up)))
        excess = jnp.maximum(jnp.maximum(up + m1, down + m3) - near, jnp.maximum(up, down) - distant)
        return minus.astype(jnp.int32), pos.astype(jnp.int32), excess

    fy_way, fy_pos, excess = ring(live & far, every, None, 2 * FY1, 2 * FY2)
    over = jnp.maximum(over, excess)
    r3, n3 = count(live & (dz == 3), same_yd, same_zs)
    r4, n4 = count(live & (dz == 4), same_yd, same_zs)
    r5, n5 = count(live & (dz == 5), same_yd, same_zs)
    up, down = halves(n3, n4, n5)
    fz_pos = jnp.where(dz == 3, up + r3, jnp.where(dz == 5, down + r5, jnp.where(r4 < up, r4, r4 - up)))
    over = jnp.maximum(over, jnp.maximum(up + n3, down + n5) - 2 * FZ)
    over = jnp.maximum(over, jnp.maximum(up, down) - 2 * FZ4)
    z_way = ((dz > 4) | ((dz == 4) & (r4 >= up))).astype(jnp.int32)
    ny_way, ny_pos, excess = ring(near, same_zd, same_ys, 2 * NY1, 2 * NY2)
    over = jnp.maximum(over, excess)
    zpos, fz_pos = zpos.astype(jnp.int32), fz_pos.astype(jnp.int32)

    def at(kind, way, pos):
        return ((kind * 2 + way) * 2 + (pos % 2 != c)) * 16 + pos // 2

    def listed(mask, way, pos, code):
        key = jnp.where(mask & (pos % 2 == c), way * 16 + pos // 2, -1)
        acc = jnp.zeros(shape, jnp.int32)
        for r in range(32):
            acc = acc + jnp.where(key[r:r + 1, :] == row, code[r:r + 1, :] + 1, 0)
        column = jnp.sum(acc, axis=1, keepdims=True)
        return jnp.sum(jnp.where(lane == row, column, 0), axis=0, keepdims=True) - 1

    held = (BUF * 4 + (cs != c)) * 16 + tile
    here = live & (row == z * 4 + y)
    queued = listed(here & ~far & (dz > 0), z_way, zpos, held)
    queued_far = listed(here & far & (dy > 0), fy_way, fy_pos, held)
    after_y = jnp.where(dy == 0, held, at(jnp.where(dy == 2, YF2, YF1), fy_way, fy_pos))
    turn_far = listed(live & far & (zs == z) & (yd == y), z_way, fz_pos, after_y)
    after_z = jnp.where(dz == 0, held, at(jnp.where(hops == 1, ZN1, ZN2), z_way, zpos))
    after_z = jnp.where(rooted, (ROOT * 4 + (cs != c)) * 16 + zs - 3, after_z)
    turn_near = listed(near & (zd == z) & (ys == y) & (dy > 0), ny_way, ny_pos, after_z)
    end_near = jnp.where(dy == 0, after_z, at(jnp.where(dy == 2, YN2, YN1), ny_way, ny_pos))
    end_far = at(jnp.where(dz == 4, ZF4, ZF3), z_way, fz_pos)
    keeper = jnp.where(far & ~rooted, fz_pos % 2, jnp.where(dy > 0, ny_pos % 2, cd))
    mine = used & (zd == z) & (yd == y) & (keeper == c)
    end = jnp.where(mine, (jnp.where(live & far, end_far, end_near) * 2 + (cd != c)) * 16 + slot, -1)
    return queued, queued_far, turn_near, turn_far, end, jnp.max(over, keepdims=True)


def plan_kernel(where_ref, codes_ref, *out_refs):
    for ref, value in zip(out_refs, route(codes_ref[...], where_ref[0], where_ref[1], where_ref[2])):
        ref[...] = value


def panel_kernel(place_ref, first_ref, inv0_ref, l10_ref, inv1_ref, front_ref, *refs):
    right0, right2, far00, far01, far10, far11, left00, left3, factor_ref, zero_ref, yh_ref, yl_ref = refs
    pieces = [
        right0.at[0], right0.at[1], right2.at[0], right2.at[1], far00, far01, far10, far11,
        left00, left3.at[0], left3.at[1], left3.at[2],
    ]
    place = place_ref[0]
    a0 = split3(inv0_ref[...])
    low = split(l10_ref[...])
    inv1 = inv1_ref[...]
    for q in range(4):
        for r in range(2):
            if q == 0:
                p0 = front_ref[0, r, 0, :, 0:T]
                p1 = front_ref[0, r, 0, :, T:2 * T].astype(F32)
            else:
                p0 = pieces[(q - 1) * 4 + r * 2][...].astype(BF16)
                p1 = pieces[(q - 1) * 4 + r * 2 + 1][...]
            y0 = dot1(p0, a0[0], NT) + (dot1(p0, a0[1], NT) + dot1(p0, a0[2], NT))
            y0h, y0l = split(y0)
            p1 = p1 - dot3((y0h, y0l), low, NT)
            y1 = dot(p1, inv1, NT)
            if r == 0:
                owner = lax.rem(place + q, 4)
                y1 = jnp.where(owner > 0, y1, 0.0)
            y1h, y1l = split(y1)
            n = q * 2 + r
            yh_ref[n, :, 0:T] = y0h
            yl_ref[n, :, 0:T] = y0l
            yh_ref[n, :, T:2 * T] = y1h
            yl_ref[n, :, T:2 * T] = y1l
            if q == 0:
                factor_ref[0, r, 0, :, 0:T] = y0
                factor_ref[0, r, 0, :, T:2 * T] = y1
    row = first_ref[0] // 7
    column = first_ref[0] % 7 + 1
    n = lax.rem(column % 4 - place + 4, 4) * 2 + column // 4
    start = pl.multiple_of(column * T, T)
    tile = front_ref[0, row, 0, :, pl.ds(start, T)].astype(F32)
    zero_ref[...] = tile - dot3((yh_ref[row], yl_ref[row]), (yh_ref[n], yl_ref[n]), NT)


def update_kernel(place_ref, front_ref, yh_ref, yl_ref, out_ref):
    place = place_ref[0]
    for r in range(2):
        for n in range(8):
            column = lax.rem(place + n // 2, 4) + 4 * (n % 2)

            @pl.when(column > 0)
            def _():
                start = pl.multiple_of(column * T, T)
                tile = front_ref[0, r, 0, :, pl.ds(start, T)].astype(F32)
                own = (yh_ref[r], yl_ref[r])
                other = (yh_ref[n], yl_ref[n])
                out_ref[r * 7 + column - 1] = tile - dot3(own, other, NT)


def arrays(kind, own, other=()):
    out = []
    for sib, xs in ((0, own), (1, other)):
        for way, x in enumerate(xs):
            out.append(((kind * 2 + way) * 2 + sib,) + (x if isinstance(x, tuple) else (0, x)))
    return out


def copy_from(sources, code, target_ref, sem):
    for sid, first, ref in sources:
        @pl.when(code // 16 == sid)
        def _():
            pltpu.make_async_copy(ref.at[first + code % 16], target_ref, sem).start()


def operands(sources):
    xs, numbered = [], []
    for sid, first, x in sources:
        where = [i for i, other in enumerate(xs) if other is x]
        if not where:
            xs.append(x)
        numbered.append((sid, first, where[0] if where else len(xs) - 1))
    return numbered, xs


def gather_kernel(numbered, size, table_ref, *refs):
    sources = [(sid, first, refs[i]) for sid, first, i in numbered]
    *outs, sem = refs[-3:]
    for way, out in enumerate(outs):
        def start(i, _):
            code = table_ref[0, way * 16 + i]

            @pl.when(code >= 0)
            def _():
                copy_from(sources, code, out.at[i], sem.at[way * size + i])
            return 0

        lax.fori_loop(0, size, start, 0)
    for way, out in enumerate(outs):
        def wait(i, _):
            @pl.when(table_ref[0, way * 16 + i] >= 0)
            def _():
                pltpu.make_async_copy(refs[0].at[0], out.at[i], sem.at[way * size + i]).wait()
            return 0

        lax.fori_loop(0, size, wait, 0)


def gather(table, sources, size, name, *first):
    numbered, xs = operands(sources)
    xs = xs + list(first)
    return pl.pallas_call(
        lambda *refs: gather_kernel(numbered, size, *refs),
        out_shape=tiles(size, size),
        in_specs=[SMEM] + [ANY] * len(xs),
        out_specs=(VMEM,) * 2,
        scratch_shapes=[pltpu.SemaphoreType.DMA((2 * size,))],
        compiler_params=pltpu.CompilerParams(vmem_limit_bytes=10 << 20),
        cost_estimate=pl.CostEstimate(flops=0, bytes_accessed=8 << 20, transcendentals=0),
        name=name,
    )(table, *xs)


DEPTH = 12


def sum_kernel(numbered, other, where_ref, table_ref, *refs):
    *ins, out_ref, list_ref, buf_ref, sem = refs
    z, y = where_ref[0], where_ref[1]
    sources = [(sid, first, ins[i]) for sid, first, i in numbered]

    def collect(i, n):
        code = table_ref[i // 4, (i // 2 % 2) * 64 + z * 8 + y * 2 + i % 2]

        take = (code >= 0) & ((code // 16) % 2 == other)

        @pl.when(take)
        def _():
            list_ref[n] = code
        return n + take.astype(jnp.int32)

    n = lax.fori_loop(0, 128, collect, jnp.int32(0))

    def start(i):
        slot = lax.rem(i, DEPTH)
        copy_from(sources, list_ref[i] // 32, buf_ref.at[slot], sem.at[slot])

    def prime(i, _):
        start(i)
        return 0

    def step(i, _):
        slot = lax.rem(i, DEPTH)
        pltpu.make_async_copy(ins[0].at[0], buf_ref.at[slot], sem.at[slot]).wait()
        out_ref[list_ref[i] % 16] += buf_ref[slot]

        @pl.when(i + DEPTH < n)
        def _():
            start(i + DEPTH)
        return 0

    lax.fori_loop(0, jnp.minimum(n, DEPTH), prime, 0)
    out_ref[...] = jnp.zeros_like(out_ref)
    lax.fori_loop(0, n, step, 0)


def add_up(where, table, sources, other):
    numbered, xs = operands(sources)
    return pl.pallas_call(
        lambda *refs: sum_kernel(numbered, other, *refs),
        out_shape=tiles(ASLOT)[0],
        in_specs=[SMEM, SMEM] + [ANY] * len(xs),
        out_specs=VMEM,
        scratch_shapes=[pltpu.SMEM((256,), jnp.int32), pltpu.VMEM((DEPTH, T, T), F32), pltpu.SemaphoreType.DMA((DEPTH,))],
        compiler_params=pltpu.CompilerParams(vmem_limit_bytes=16 << 20),
        cost_estimate=pl.CostEstimate(flops=0, bytes_accessed=30 << 20, transcendentals=0),
        name="sum_other" if other else "sum_own",
    )(where, table, *xs)


def slots_kernel(tile_ref, own_ref, out_ref, sem):
    def start(p, _):
        tile = tile_ref[p]

        @pl.when(tile >= 0)
        def _():
            pltpu.make_async_copy(own_ref.at[tile], out_ref.at[p], sem.at[p]).start()
        return 0

    def wait(p, _):
        @pl.when(tile_ref[p] >= 0)
        def _():
            pltpu.make_async_copy(own_ref.at[0], out_ref.at[p], sem.at[p]).wait()
        return 0

    lax.fori_loop(0, 64, start, 0)
    lax.fori_loop(0, 64, wait, 0)


def add_kernel(target_ref, arrived_ref, out_ref):
    step = pl.program_id(0)

    @pl.when(step == 0)
    def _():
        out_ref[...] = jnp.zeros_like(out_ref)

    for i in range(4):
        target = target_ref[step * 4 + i]

        @pl.when(target >= 0)
        def _():
            out_ref[target] += arrived_ref[i]


def tiles(*counts):
    return tuple(jax.ShapeDtypeStruct((n, T, T), F32) for n in counts)


def leaf_id(z, y, c):
    return ((z % 8) * 4 + y % 4) * 2 + c


PLACES = [(z, y, c) for z in range(8) for y in range(4) for c in range(2)]


def send(x, pairs):
    return lax.ppermute(x, "leaf", [(leaf_id(*a), leaf_id(*b)) for a, b in pairs])


def dense(work, root, tile, slot, where, *tables):
    outgoing = pl.pallas_call(
        slots_kernel,
        out_shape=tiles(64)[0],
        in_specs=[SMEM, ANY],
        out_specs=ANY,
        scratch_shapes=[pltpu.SemaphoreType.DMA((64,))],
        name="slots",
    )(tile, work)
    arrived = lax.all_to_all(outgoing, "leaf", split_axis=0, concat_axis=0, tiled=True)
    targets = lax.all_to_all(slot, "leaf", split_axis=0, concat_axis=0, tiled=True)
    return pl.pallas_call(
        add_kernel,
        out_shape=tiles(ASLOT)[0],
        grid=(16,),
        in_specs=[SMEM, pl.BlockSpec((4, T, T), lambda i: (i, 0, 0))],
        out_specs=pl.BlockSpec((ASLOT, T, T), lambda i: (0, 0, 0)),
        compiler_params=pltpu.CompilerParams(vmem_limit_bytes=32 << 20),
        name="add",
    )(targets, arrived)


def tie(x, *others):
    return lax.optimization_barrier((x,) + others)[0]


def sparse(work, root, tile, slot, where, queued, queued_far, turn_near, turn_far, end):
    swap = [((z, y, c), (z, y, 1 - c)) for z, y, c in PLACES]
    along_z = [[((z, y, c), (z + s, y, c)) for z, y, c in PLACES] for s in (1, -1)]
    along_y = [[((z, y, c), (z, y + s, c)) for z, y, c in PLACES] for s in (1, -1)]

    def sends(xs, ways):
        return [send(x, way) for x, way in zip(xs, ways)]

    def swaps(xs):
        return [send(x, swap) for x in xs]

    def after(xs, *others):
        return list(lax.optimization_barrier(tuple(xs) + others)[:len(xs)])

    other = send(work, swap)
    both = arrays(BUF, [work], [other])
    near_list = gather(queued, both, N1, "queue")
    n1 = sends(near_list, along_z)
    far_list = gather(tie(queued_far, *near_list), both, FY1, "queue_far")
    f1 = sends(far_list, along_y)
    f2 = sends([x[:FY2] for x in f1], along_y)
    n2 = sends(after([x[:N2] for x in n1], *f1), along_z)
    mixed = send(after([jnp.concatenate([*f1, *f2])], *n1)[0], swap)
    parts = [(cut, mixed) for cut in (0, FY1, 2 * FY1, 2 * FY1 + FY2)]
    column = jnp.stack(root)
    column_other = send(after([column], *n1)[0], swap)
    far_list = gather(turn_far, both + arrays(YF1, f1, parts[0:2]) + arrays(YF2, f2, parts[2:4]), FZ, "turn_far", column_other)
    n1_other = swaps(after(n1, *far_list))
    z1 = sends(after(far_list, *n2, *n1_other), along_z)
    near_sources = both + arrays(ZN1, n1, n1_other) + arrays(ZN2, n2, swaps(n2)) + arrays(ROOT, [column], [column_other])
    near_list = gather(turn_near, near_sources, NY1, "turn_near")
    z2 = sends(after(z1, *near_list), along_z)
    y1 = sends(near_list, along_y)
    z3 = sends(z2, along_z)
    y2 = sends(after([x[:NY2] for x in y1], *z2), along_y)
    z4 = sends(after([x[:FZ4] for x in z3], *y1), along_z)
    sources = near_sources + arrays(YN1, y1) + arrays(YN2, y2) + arrays(ZF3, z3) + arrays(ZF4, z4)
    theirs = add_up(where, end, sources, 1)
    own = add_up(tie(where, theirs), end, sources, 0)
    return own + send(theirs, swap)


def local(front, pivot_tiles, send_table):
    place = lax.axis_index("front").astype(jnp.int32)
    leaf = lax.axis_index("leaf").astype(jnp.int32)
    where = jnp.stack([leaf // 8, (leaf // 2) % 4, leaf % 2])
    table = send_table[0, 0]
    used = table[0] >= 0
    tile = jnp.where(used, table[0] * 7 + table[1] - 1, -1)
    code = jnp.where(used, tile * 16 + table[2], -1)
    up = [(i, (i + 1) % 4) for i in range(4)]
    down = [(i, (i - 1) % 4) for i in range(4)]
    own = [[front[0, r, 0, :, k * T:k * T + T].astype(F32) for k in range(2)] for r in range(2)]
    def across(x, shift, *others):
        return lax.ppermute(tie(x, *others) if others else x, "front", [(i, (i + shift) % 4) for i in range(4)])

    codes = lax.all_to_all(jnp.broadcast_to(code, (64, 64)), "leaf", split_axis=0, concat_axis=0, tiled=True).reshape(32, 128)
    left00 = across(own[0][0], 1)
    right0 = across(jnp.stack(own[0]), -1)
    far00 = across(left00, 1, codes)
    far01 = across(right0[1], -1)
    left3 = across(jnp.stack([own[0][1], own[1][0], own[1][1]]), 1, far00, far01)
    right2 = across(jnp.stack(own[1]), -1, far00, far01)
    far10 = across(left3[1], 1)
    far11 = across(right2[1], -1)
    from_left = [[left00, left3[0]], [left3[1], left3[2]]]
    from_right = [[right0[0], right0[1]], [right2[0], right2[1]]]
    from_far = [[far00, far01], [far10, far11]]
    by_q = [own, from_right, from_far, from_left]

    def of_owner(owner, r, k, *after):
        q = lax.rem(owner - place + 4, 4)
        if after:
            q = tie(q, *after)
        out = by_q[0][r][k]
        for i in range(1, 4):
            out = jnp.where(q == i, by_q[i][r][k], out)
        return out

    inv0 = pl.pallas_call(
        first_kernel,
        out_shape=jax.ShapeDtypeStruct((T, T), F32),
        in_specs=[VMEM],
        out_specs=VMEM,
        scratch_shapes=[pltpu.VMEM((B, 128), F32)],
        compiler_params=pltpu.CompilerParams(vmem_limit_bytes=16 << 20),
        cost_estimate=pl.CostEstimate(flops=0, bytes_accessed=20 << 20, transcendentals=0),
        name="first",
    )(of_owner(0, 0, 0))
    *tables, over = pl.pallas_call(
        plan_kernel,
        out_shape=tuple(jax.ShapeDtypeStruct((n, 128), jnp.int32) for n in (1, 1, 1, 1, 32)) + (jax.ShapeDtypeStruct((1, 1), F32),),
        in_specs=[SMEM, VMEM],
        out_specs=(VMEM,) * 6,
        cost_estimate=pl.CostEstimate(flops=0, bytes_accessed=6 << 20, transcendentals=0),
        name="plan",
    )(where, codes)
    w10 = of_owner(1, 0, 0, inv0)
    w11 = of_owner(1, 0, 1, inv0)
    l10, inv1 = pl.pallas_call(
        second_kernel,
        out_shape=(jax.ShapeDtypeStruct((T, T), F32),) * 2,
        in_specs=[SMEM, VMEM, VMEM, VMEM],
        out_specs=(VMEM, VMEM),
        scratch_shapes=[pltpu.VMEM((B, 128), F32)],
        compiler_params=pltpu.CompilerParams(vmem_limit_bytes=16 << 20),
        cost_estimate=pl.CostEstimate(flops=0, bytes_accessed=40 << 20, transcendentals=0),
        name="second",
    )(pivot_tiles, inv0, w10, w11)

    received = [right0, right2, far00, far01, far10, far11, left00, left3]
    factor, zero, yh, yl = pl.pallas_call(
        panel_kernel,
        out_shape=(jax.ShapeDtypeStruct((1, 2, 1, T, 2 * T), F32), jax.ShapeDtypeStruct((T, T), F32))
        + (jax.ShapeDtypeStruct((8, T, 2 * T), BF16),) * 2,
        in_specs=[SMEM, SMEM] + [VMEM] * 12,
        out_specs=(VMEM,) * 4,
        compiler_params=pltpu.CompilerParams(vmem_limit_bytes=28 << 20),
        name="panel",
    )(place.reshape(1), jnp.maximum(tile[0:1], 0), inv0, l10, inv1, front, *received)
    root = [send(zero, [((z, y, c), (0, y, c)) for y in range(4) for c in range(2)]) for z in (3, 4, 5)]
    work = pl.pallas_call(
        update_kernel,
        out_shape=tiles(TILES)[0],
        in_specs=[SMEM] + [VMEM] * 3,
        out_specs=VMEM,
        compiler_params=pltpu.CompilerParams(vmem_limit_bytes=20 << 20),
        name="update",
    )(place.reshape(1), front, yh, yl)
    ancestor = lax.cond(over[0, 0] > 0.0, dense, sparse, work, root, tile, table[2], where, *tables)
    return (factor, ancestor.reshape(1, 1, ASLOT, T, T))


def solution(mesh):
    in_specs = (P("leaf", None, "front", None, None), P("leaf"), P("leaf", "front", None, None))
    out_specs = (P("leaf", None, "front", None, None), P("leaf", "front", None, None, None))
    return jax.shard_map(local, mesh=mesh, in_specs=in_specs, out_specs=out_specs, check_vma=False)
```

```python
import functools

import jax
import jax.numpy as jnp
from jax import lax
from jax.experimental import pallas as pl
from jax.experimental.pallas import tpu as pltpu
from jax.sharding import PartitionSpec as P

PT = 2
ASLOT = 16
TILES = 14
N1, N2 = 8, 5
FY1, FY2 = 5, 3
FZ, FZ4 = 5, 4
NY1, NY2 = 11, 7
BUF, ZN1, ZN2, YF1, YF2, YN1, YN2, ZF3, ZF4, ROOT = range(10)
B = 64
T = 256
F32 = jnp.float32
BF16 = jnp.bfloat16
HIGHEST = lax.Precision.HIGHEST
VMEM = pl.BlockSpec(memory_space=pltpu.VMEM)
SMEM = pl.BlockSpec(memory_space=pltpu.SMEM)
ANY = pl.BlockSpec(memory_space=pl.ANY)
NN = (((1,), (0,)), ((), ()))
NT = (((1,), (1,)), ((), ()))
TN = (((0,), (0,)), ((), ()))


def dot(a, b, dims):
    return lax.dot_general(a, b, dims, precision=HIGHEST, preferred_element_type=F32)


def dot1(a, b, dims):
    return lax.dot_general(a, b, dims, preferred_element_type=F32)


def split(x):
    high = x.astype(BF16)
    return high, (x - high.astype(F32)).astype(BF16)


def split3(x):
    high = x.astype(BF16)
    rest = x - high.astype(F32)
    mid = rest.astype(BF16)
    return high, mid, (rest - mid.astype(F32)).astype(BF16)


def dot3(a, b, dims):
    ah, al = a
    bh, bl = b
    return dot1(ah, bh, dims) + (dot1(ah, bl, dims) + dot1(al, bh, dims))


def factor64(groups, f_ref):
    sub = lax.broadcasted_iota(jnp.int32, (8, 128), 0)

    def body(it, gs):
        count = len(gs)
        cols = [[jnp.broadcast_to(g[:, t:t + 1], (8, 128)) for t in range(8)] for g in gs]
        rows = [jnp.broadcast_to(gs[0][t:t + 1, :], (8, 128)) for t in range(8)]
        s = [[jnp.broadcast_to(cols[0][t][u:u + 1, :], (8, 128)) if u >= t else None for t in range(8)] for u in range(8)]
        inv = [None] * 8
        for t in range(8):
            inv[t] = 1.0 / s[t][t]
            for u in range(t + 1, 8):
                low = s[u][t] * inv[t]
                for v in range(u, 8):
                    s[v][u] = s[v][u] - low * s[v][t]
                rows[u] = rows[u] - low * rows[t]
                for g in range(1, count):
                    cols[g][u] = cols[g][u] - low * cols[g][t]
        done = jnp.zeros((8, 128), F32)
        for t in range(8):
            done = jnp.where(sub == t, rows[t] * lax.rsqrt(s[t][t]), done)
        f_ref[pl.ds(pl.multiple_of(it * 8, 8), 8), :] = pltpu.roll(done, it * 8, 1)
        scaled = [rows[t] * inv[t] for t in range(8)]
        left = []
        for g in range(1, count):
            piece = gs[g]
            for t in range(8):
                piece = piece - cols[g][t] * scaled[t]
            left.append(pltpu.roll(piece, 120, 1))
        left.append(gs[0])
        return tuple(left)

    groups = tuple(groups)
    for first in range(0, 8, 2):
        groups = lax.fori_loop(first, first + 2, body, groups)[:6 - first]


def factor256(x_ref, f_ref):
    lane = lax.broadcasted_iota(jnp.int32, (B, 128), 1)
    row = lax.broadcasted_iota(jnp.int32, (B, 128), 0)
    ident = (lane - B == row).astype(F32)
    col = lax.broadcasted_iota(jnp.int32, (B, T), 1)
    wide_row = lax.broadcasted_iota(jnp.int32, (B, T), 0)
    for k in range(T // B):
        lo = k * B
        strip = x_ref[lo:lo + B, :]
        block = strip[:, (k // 2) * 128:(k // 2) * 128 + 128]
        if k % 2:
            block = pltpu.roll(block, B, 1)
        both = jnp.where(lane < B, block, ident)
        factor64([both[8 * g:8 * g + 8, :] for g in range(8)], f_ref)
        block_inv = f_ref[...][:, B:]
        inside = (col >= lo) & (col < lo + B)
        strip = jnp.where(inside, (col - lo == wide_row).astype(F32), strip)
        out = dot(block_inv, strip, NN)
        x_ref[lo:lo + B, :] = jnp.where(col < lo + B, out, 0.0)
        if lo + B < T:
            rest = T - lo - B
            rest_col = lax.broadcasted_iota(jnp.int32, (rest, T), 1)
            old = x_ref[lo + B:, :]
            old = jnp.where((rest_col >= lo) & (rest_col < lo + B), 0.0, old)
            x_ref[lo + B:, :] = old - dot(out[:, lo + B:], out, TN)


def first_kernel(w00_ref, inv0_ref, f_ref):
    inv0_ref[...] = w00_ref[...]
    factor256(inv0_ref, f_ref)


def second_kernel(piv_ref, inv0_ref, w10_ref, w11_ref, l10_ref, inv1_ref, f_ref):
    l10 = dot(w10_ref[...], inv0_ref[...], NT)
    l10_ref[...] = l10
    inv1_ref[...] = jnp.zeros((T, T), F32)

    @pl.when(piv_ref[0] >= 2)
    def _():
        inv1_ref[...] = w11_ref[...] - dot(l10, l10, NT)
        factor256(inv1_ref, f_ref)


def iota(shape, dim):
    return lax.broadcasted_iota(jnp.int32, shape, dim)


def fdot(a, b):
    return lax.dot_general(a, b, (((1,), (0,)), ((), ())), preferred_element_type=F32)


def route(codes, z, y, c, chip=False):
    shape, sq, rows = (32, 128), (128, 128), (32, 32)
    row, lane = iota(shape, 0), iota(shape, 1)
    zs, ys = row // 4, row % 4
    cs, zd, yd, cd = lane // 64, (lane // 8) % 8, (lane // 2) % 4, lane % 2
    dz, dy = (zd - zs + 8) % 8, (yd - ys + 4) % 4
    hops = jnp.minimum(dz, 8 - dz)
    far = hops > 2
    used = codes >= 0
    rooted = used & (lane % 64 == 0) & far
    live = used & ~rooted
    near = used & (~far | rooted)
    tile = jnp.where(used, codes // 16, 0)
    slot = jnp.where(used, codes % 16, 0)
    la, lb = iota(sq, 0), iota(sq, 1)
    before = la < lb
    same_zd = (la // 8) % 8 == (lb // 8) % 8
    same_yd = (la // 2) % 4 == (lb // 2) % 4
    ra, rb = iota(rows, 0), iota(rows, 1)
    same_ys = ra % 4 == rb % 4
    same_zs = ra // 4 == rb // 4

    def f(x):
        return x.astype(F32)

    def count(mask, lanes, peers):
        rank = fdot(f(mask), f(before & lanes))
        total = fdot(f(mask), f(lanes))
        if peers is not None:
            rank = rank + fdot(f(peers & (rb < ra)), total)
            total = fdot(f(peers), total)
        return rank, total

    def halves(n_up, n_both, n_down):
        up = jnp.clip(jnp.floor((n_both + n_down - n_up + 1.0) * 0.5), 0.0, n_both)
        return up, n_both - up

    every = la >= 0
    over = jnp.full(shape, -1.0, F32)
    r1, n1 = count(live & (dz == 1), every, None)
    r2, n2 = count(live & (dz == 2), every, None)
    r6, n6 = count(live & (dz == 6), every, None)
    r7, n7 = count(live & (dz == 7), every, None)
    zpos = jnp.where(dz == 1, n2 + r1, jnp.where(dz == 2, r2, jnp.where(dz == 6, r6, n6 + r7)))
    over = jnp.maximum(over, jnp.maximum(n1 + n2, n7 + n6) - 2 * N1)
    over = jnp.maximum(over, jnp.maximum(n2, n6) - 2 * N2)

    def ring(mask, lanes, peers, near, distant):
        a1, m1 = count(mask & (dy == 1), lanes, peers)
        a2, m2 = count(mask & (dy == 2), lanes, peers)
        a3, m3 = count(mask & (dy == 3), lanes, peers)
        up, down = halves(m1, m2, m3)
        minus = (dy == 3) | ((dy == 2) & (a2 >= up))
        pos = jnp.where(dy == 1, up + a1, jnp.where(dy == 3, down + a3, jnp.where(a2 < up, a2, a2 - up)))
        excess = jnp.maximum(jnp.maximum(up + m1, down + m3) - near, jnp.maximum(up, down) - distant)
        return minus.astype(jnp.int32), pos.astype(jnp.int32), excess

    fy_way, fy_pos, excess = ring(live & far, every, None, 2 * FY1, 2 * FY2)
    over = jnp.maximum(over, excess)
    r3, n3 = count(live & (dz == 3), same_yd, same_zs)
    r4, n4 = count(live & (dz == 4), same_yd, same_zs)
    r5, n5 = count(live & (dz == 5), same_yd, same_zs)
    up, down = halves(n3, n4, n5)
    fz_pos = jnp.where(dz == 3, up + r3, jnp.where(dz == 5, down + r5, jnp.where(r4 < up, r4, r4 - up)))
    over = jnp.maximum(over, jnp.maximum(up + n3, down + n5) - 2 * FZ)
    over = jnp.maximum(over, jnp.maximum(up, down) - 2 * FZ4)
    z_way = ((dz > 4) | ((dz == 4) & (r4 >= up))).astype(jnp.int32)
    ny_way, ny_pos, excess = ring(near, same_zd, same_ys, 2 * NY1, 2 * NY2)
    over = jnp.maximum(over, excess)
    zpos, fz_pos = zpos.astype(jnp.int32), fz_pos.astype(jnp.int32)

    def at(kind, way, pos):
        return ((kind * 2 + way) * 2 + (pos % 2 != c)) * 16 + jnp.minimum(pos // 2, 15)

    def listed(mask, way, pos, code):
        key = jnp.where(mask & (pos % 2 == c) & (pos < 32), way * 16 + pos // 2, -1)
        acc = jnp.zeros(shape, jnp.int32)
        for r in range(32):
            acc = acc + jnp.where(key[r:r + 1, :] == row, code[r:r + 1, :] + 1, 0)
        column = jnp.sum(acc, axis=1, keepdims=True)
        return jnp.sum(jnp.where(lane == row, column, 0), axis=0, keepdims=True) - 1

    held = (BUF * 4 + (cs != c)) * 16 + tile
    if chip:
        here = live & (row == z * 4 + y)
        queued = listed(here & ~far & (dz > 0), z_way, zpos, held)
        return queued, listed(here & far & (dy > 0), fy_way, fy_pos, held)
    after_y = jnp.where(dy == 0, held, at(jnp.where(dy == 2, YF2, YF1), fy_way, fy_pos))
    turn_far = listed(live & far & (zs == z) & (yd == y), z_way, fz_pos, after_y)
    after_z = jnp.where(dz == 0, held, at(jnp.where(hops == 1, ZN1, ZN2), z_way, zpos))
    after_z = jnp.where(rooted, (ROOT * 4 + (cs != c)) * 16 + zs - 3, after_z)
    turn_near = listed(near & (zd == z) & (ys == y) & (dy > 0), ny_way, ny_pos, after_z)
    end_near = jnp.where(dy == 0, after_z, at(jnp.where(dy == 2, YN2, YN1), ny_way, ny_pos))
    end_far = at(jnp.where(dz == 4, ZF4, ZF3), z_way, fz_pos)
    keeper = jnp.where(far & ~rooted, fz_pos % 2, jnp.where(dy > 0, ny_pos % 2, cd))
    mine = used & (zd == z) & (yd == y) & (keeper == c)
    end = jnp.where(mine, (jnp.where(live & far, end_far, end_near) * 2 + (cd != c)) * 16 + slot, -1)
    return turn_near, turn_far, end, jnp.max(over, keepdims=True)


def plan_kernel(chip, where_ref, codes_ref, *out_refs):
    for ref, value in zip(out_refs, route(codes_ref[...], where_ref[0], where_ref[1], where_ref[2], chip)):
        ref[...] = value


def plan(chip, where, codes):
    shapes = [(1, 128)] * 2 if chip else [(1, 128), (1, 128), (32, 128), (1, 1)]
    return pl.pallas_call(
        lambda *refs: plan_kernel(chip, *refs),
        out_shape=tuple(jax.ShapeDtypeStruct(s, F32 if s == (1, 1) else jnp.int32) for s in shapes),
        in_specs=[SMEM, VMEM],
        out_specs=(VMEM,) * len(shapes),
        compiler_params=pltpu.CompilerParams(vmem_limit_bytes=6 << 20),
        name="plan_chip" if chip else "plan",
    )(where, codes)


def panel_kernel(place_ref, first_ref, inv0_ref, l10_ref, inv1_ref, front_ref, *refs):
    right0, right2, far00, far01, far10, far11, left00, left3, factor_ref, zero_ref, yh_ref, yl_ref = refs
    pieces = [
        right0.at[0], right0.at[1], right2.at[0], right2.at[1], far00, far01, far10, far11,
        left00, left3.at[0], left3.at[1], left3.at[2],
    ]
    place = place_ref[0]
    a0 = split3(inv0_ref[...])
    low = split(l10_ref[...])
    inv1 = inv1_ref[...]
    for q in range(4):
        for r in range(2):
            if q == 0:
                p0 = front_ref[0, r, 0, :, 0:T]
                p1 = front_ref[0, r, 0, :, T:2 * T].astype(F32)
            else:
                p0 = pieces[(q - 1) * 4 + r * 2][...].astype(BF16)
                p1 = pieces[(q - 1) * 4 + r * 2 + 1][...]
            y0 = dot1(p0, a0[0], NT) + (dot1(p0, a0[1], NT) + dot1(p0, a0[2], NT))
            y0h, y0l = split(y0)
            p1 = p1 - dot3((y0h, y0l), low, NT)
            y1 = dot(p1, inv1, NT)
            if r == 0:
                owner = lax.rem(place + q, 4)
                y1 = jnp.where(owner > 0, y1, 0.0)
            y1h, y1l = split(y1)
            n = q * 2 + r
            yh_ref[n, :, 0:T] = y0h
            yl_ref[n, :, 0:T] = y0l
            yh_ref[n, :, T:2 * T] = y1h
            yl_ref[n, :, T:2 * T] = y1l
            if q == 0:
                factor_ref[0, r, 0, :, 0:T] = y0
                factor_ref[0, r, 0, :, T:2 * T] = y1
    row = first_ref[0] // 7
    column = first_ref[0] % 7 + 1
    n = lax.rem(column % 4 - place + 4, 4) * 2 + column // 4
    start = pl.multiple_of(column * T, T)
    tile = front_ref[0, row, 0, :, pl.ds(start, T)].astype(F32)
    zero_ref[...] = tile - dot3((yh_ref[row], yl_ref[row]), (yh_ref[n], yl_ref[n]), NT)


def update_kernel(place_ref, front_ref, yh_ref, yl_ref, out_ref):
    place = place_ref[0]
    for r in range(2):
        for n in range(8):
            column = lax.rem(place + n // 2, 4) + 4 * (n % 2)

            @pl.when(column > 0)
            def _():
                start = pl.multiple_of(column * T, T)
                tile = front_ref[0, r, 0, :, pl.ds(start, T)].astype(F32)
                own = (yh_ref[r], yl_ref[r])
                other = (yh_ref[n], yl_ref[n])
                out_ref[r * 7 + column - 1] = tile - dot3(own, other, NT)


def arrays(kind, own, other=()):
    out = []
    for sib, xs in ((0, own), (1, other)):
        for way, x in enumerate(xs):
            out.append(((kind * 2 + way) * 2 + sib,) + (x if isinstance(x, tuple) else (0, x)))
    return out


def copy_from(sources, code, target_ref, sem):
    for sid, first, ref in sources:
        @pl.when(code // 16 == sid)
        def _():
            pltpu.make_async_copy(ref.at[jnp.minimum(first + code % 16, ref.shape[0] - 1)], target_ref, sem).start()


def operands(sources):
    xs, numbered = [], []
    for sid, first, x in sources:
        where = [i for i, other in enumerate(xs) if other is x]
        if not where:
            xs.append(x)
        numbered.append((sid, first, where[0] if where else len(xs) - 1))
    return numbered, xs


def gather_kernel(numbered, size, table_ref, *refs):
    sources = [(sid, first, refs[i]) for sid, first, i in numbered]
    *outs, sem = refs[-3:]
    for way, out in enumerate(outs):
        def start(i, _):
            code = table_ref[0, way * 16 + i]

            @pl.when(code >= 0)
            def _():
                copy_from(sources, code, out.at[i], sem.at[way * size + i])
            return 0

        lax.fori_loop(0, size, start, 0)
    for way, out in enumerate(outs):
        def wait(i, _):
            @pl.when(table_ref[0, way * 16 + i] >= 0)
            def _():
                pltpu.make_async_copy(refs[0].at[0], out.at[i], sem.at[way * size + i]).wait()
            return 0

        lax.fori_loop(0, size, wait, 0)


def gather(table, sources, size, name, *first):
    numbered, xs = operands(sources)
    xs = xs + list(first)
    return pl.pallas_call(
        lambda *refs: gather_kernel(numbered, size, *refs),
        out_shape=tiles(size, size),
        in_specs=[SMEM] + [ANY] * len(xs),
        out_specs=(VMEM,) * 2,
        scratch_shapes=[pltpu.SemaphoreType.DMA((2 * size,))],
        compiler_params=pltpu.CompilerParams(vmem_limit_bytes=10 << 20),
        cost_estimate=pl.CostEstimate(flops=0, bytes_accessed=8 << 20, transcendentals=0),
        name=name,
    )(table, *xs)


DEPTH = 12


def sum_kernel(numbered, other, where_ref, table_ref, *refs):
    *ins, out_ref, list_ref, buf_ref, sem = refs
    z, y = where_ref[0], where_ref[1]
    sources = [(sid, first, ins[i]) for sid, first, i in numbered]

    def collect(i, n):
        code = table_ref[i // 4, (i // 2 % 2) * 64 + z * 8 + y * 2 + i % 2]

        take = (code >= 0) & ((code // 16) % 2 == other)

        @pl.when(take)
        def _():
            list_ref[n] = code
        return n + take.astype(jnp.int32)

    n = lax.fori_loop(0, 128, collect, jnp.int32(0))

    def start(i):
        slot = lax.rem(i, DEPTH)
        copy_from(sources, list_ref[i] // 32, buf_ref.at[slot], sem.at[slot])

    def prime(i, _):
        start(i)
        return 0

    def step(i, _):
        slot = lax.rem(i, DEPTH)
        pltpu.make_async_copy(ins[0].at[0], buf_ref.at[slot], sem.at[slot]).wait()
        out_ref[list_ref[i] % 16] += buf_ref[slot]

        @pl.when(i + DEPTH < n)
        def _():
            start(i + DEPTH)
        return 0

    lax.fori_loop(0, jnp.minimum(n, DEPTH), prime, 0)
    out_ref[...] = jnp.zeros_like(out_ref)
    lax.fori_loop(0, n, step, 0)


def add_up(where, table, sources, other):
    numbered, xs = operands(sources)
    return pl.pallas_call(
        lambda *refs: sum_kernel(numbered, other, *refs),
        out_shape=tiles(ASLOT)[0],
        in_specs=[SMEM, SMEM] + [ANY] * len(xs),
        out_specs=VMEM,
        scratch_shapes=[pltpu.SMEM((256,), jnp.int32), pltpu.VMEM((DEPTH, T, T), F32), pltpu.SemaphoreType.DMA((DEPTH,))],
        compiler_params=pltpu.CompilerParams(vmem_limit_bytes=16 << 20),
        cost_estimate=pl.CostEstimate(flops=0, bytes_accessed=30 << 20, transcendentals=0),
        name="sum_other" if other else "sum_own",
    )(where, table, *xs)


def slots_kernel(tile_ref, own_ref, out_ref, sem):
    def start(p, _):
        tile = tile_ref[p]

        @pl.when(tile >= 0)
        def _():
            pltpu.make_async_copy(own_ref.at[tile], out_ref.at[p], sem.at[p]).start()
        return 0

    def wait(p, _):
        @pl.when(tile_ref[p] >= 0)
        def _():
            pltpu.make_async_copy(own_ref.at[0], out_ref.at[p], sem.at[p]).wait()
        return 0

    lax.fori_loop(0, 64, start, 0)
    lax.fori_loop(0, 64, wait, 0)


def add_kernel(target_ref, arrived_ref, out_ref):
    step = pl.program_id(0)

    @pl.when(step == 0)
    def _():
        out_ref[...] = jnp.zeros_like(out_ref)

    for i in range(4):
        target = target_ref[step * 4 + i]

        @pl.when(target >= 0)
        def _():
            out_ref[target] += arrived_ref[i]


def tiles(*counts):
    return tuple(jax.ShapeDtypeStruct((n, T, T), F32) for n in counts)


def leaf_id(z, y, c):
    return ((z % 8) * 4 + y % 4) * 2 + c


PLACES = [(z, y, c) for z in range(8) for y in range(4) for c in range(2)]


def send(x, pairs):
    return lax.ppermute(x, "leaf", [(leaf_id(*a), leaf_id(*b)) for a, b in pairs])


def dense(work, tile, slot):
    outgoing = pl.pallas_call(
        slots_kernel,
        out_shape=tiles(64)[0],
        in_specs=[SMEM, ANY],
        out_specs=ANY,
        scratch_shapes=[pltpu.SemaphoreType.DMA((64,))],
        name="slots",
    )(tile, work)
    arrived = lax.all_to_all(outgoing, "leaf", split_axis=0, concat_axis=0, tiled=True)
    targets = lax.all_to_all(slot, "leaf", split_axis=0, concat_axis=0, tiled=True)
    return pl.pallas_call(
        add_kernel,
        out_shape=tiles(ASLOT)[0],
        grid=(16,),
        in_specs=[SMEM, pl.BlockSpec((4, T, T), lambda i: (i, 0, 0))],
        out_specs=pl.BlockSpec((ASLOT, T, T), lambda i: (0, 0, 0)),
        compiler_params=pltpu.CompilerParams(vmem_limit_bytes=32 << 20),
        name="add",
    )(targets, arrived)


def tie(x, *others):
    return lax.optimization_barrier((x,) + others)[0]


def sparse(work, root, code, where, queued, queued_far):
    swap = [((z, y, c), (z, y, 1 - c)) for z, y, c in PLACES]
    along_z = [[((z, y, c), (z + s, y, c)) for z, y, c in PLACES] for s in (1, -1)]
    along_y = [[((z, y, c), (z, y + s, c)) for z, y, c in PLACES] for s in (1, -1)]

    def sends(xs, ways):
        return [send(x, way) for x, way in zip(xs, ways)]

    def swaps(xs):
        return [send(x, swap) for x in xs]

    def after(xs, *others):
        return list(lax.optimization_barrier(tuple(xs) + others)[:len(xs)])

    other = send(after([work], *root)[0], swap)
    both = arrays(BUF, [work], [other])
    near_list = gather(queued, both, N1, "queue")
    n1 = sends(near_list, along_z)
    far_list = gather(tie(queued_far, *near_list), both, FY1, "queue_far")
    f1 = sends(far_list, along_y)
    f2 = sends([x[:FY2] for x in f1], along_y)
    everyone = jnp.broadcast_to(after([code], *f1)[0], (64, 64))
    codes = lax.all_to_all(everyone, "leaf", split_axis=0, concat_axis=0, tiled=True).reshape(32, 128)
    turn_near, turn_far, end, over = plan(False, where, codes)
    n2 = sends(after([x[:N2] for x in n1], *f1), along_z)
    mixed = send(after([jnp.concatenate([*f1, *f2])], *n1)[0], swap)
    parts = [(cut, mixed) for cut in (0, FY1, 2 * FY1, 2 * FY1 + FY2)]
    column = jnp.stack(root)
    column_other = send(after([column], *n1)[0], swap)
    far_list = gather(turn_far, both + arrays(YF1, f1, parts[0:2]) + arrays(YF2, f2, parts[2:4]), FZ, "turn_far", column_other)
    n1_other = swaps(after(n1, *far_list))
    z1 = sends(after(far_list, *n2, *n1_other), along_z)
    near_sources = both + arrays(ZN1, n1, n1_other) + arrays(ZN2, n2, swaps(n2)) + arrays(ROOT, [column], [column_other])
    near_list = gather(turn_near, near_sources, NY1, "turn_near")
    z2 = sends(after(z1, *near_list), along_z)
    y1 = sends(near_list, along_y)
    z3 = sends(z2, along_z)
    y2 = sends(after([x[:NY2] for x in y1], *z2), along_y)
    z4 = sends(after([x[:FZ4] for x in z3], *y1), along_z)
    sources = near_sources + arrays(YN1, y1) + arrays(YN2, y2) + arrays(ZF3, z3) + arrays(ZF4, z4)
    theirs = add_up(where, end, sources, 1)
    own = add_up(tie(where, theirs), end, sources, 0)
    return over, own, send(theirs, swap)


def local(front, pivot_tiles, send_table):
    place = lax.axis_index("front").astype(jnp.int32)
    leaf = lax.axis_index("leaf").astype(jnp.int32)
    where = jnp.stack([leaf // 8, (leaf // 2) % 4, leaf % 2])
    table = send_table[0, 0]
    used = table[0] >= 0
    tile = jnp.where(used, table[0] * 7 + table[1] - 1, -1)
    code = jnp.where(used, tile * 16 + table[2], -1)
    up = [(i, (i + 1) % 4) for i in range(4)]
    down = [(i, (i - 1) % 4) for i in range(4)]
    own = [[front[0, r, 0, :, k * T:k * T + T].astype(F32) for k in range(2)] for r in range(2)]
    def across(x, shift, *others):
        return lax.ppermute(tie(x, *others) if others else x, "front", [(i, (i + shift) % 4) for i in range(4)])

    left00 = across(own[0][0], 1)
    right0 = across(jnp.stack(own[0]), -1)
    far00 = across(left00, 1)
    far01 = across(right0[1], -1)
    left3 = across(jnp.stack([own[0][1], own[1][0], own[1][1]]), 1, far00, far01)
    right2 = across(jnp.stack(own[1]), -1, far00, far01)
    far10 = across(left3[1], 1)
    far11 = across(right2[1], -1)
    from_left = [[left00, left3[0]], [left3[1], left3[2]]]
    from_right = [[right0[0], right0[1]], [right2[0], right2[1]]]
    from_far = [[far00, far01], [far10, far11]]
    by_q = [own, from_right, from_far, from_left]

    def of_owner(owner, r, k, *after):
        q = lax.rem(owner - place + 4, 4)
        if after:
            q = tie(q, *after)
        out = by_q[0][r][k]
        for i in range(1, 4):
            out = jnp.where(q == i, by_q[i][r][k], out)
        return out

    inv0 = pl.pallas_call(
        first_kernel,
        out_shape=jax.ShapeDtypeStruct((T, T), F32),
        in_specs=[VMEM],
        out_specs=VMEM,
        scratch_shapes=[pltpu.VMEM((B, 128), F32)],
        compiler_params=pltpu.CompilerParams(vmem_limit_bytes=8 << 20),
        cost_estimate=pl.CostEstimate(flops=0, bytes_accessed=20 << 20, transcendentals=0),
        name="first",
    )(of_owner(0, 0, 0))
    w10 = of_owner(1, 0, 0, inv0)
    w11 = of_owner(1, 0, 1, inv0)
    l10, inv1 = pl.pallas_call(
        second_kernel,
        out_shape=(jax.ShapeDtypeStruct((T, T), F32),) * 2,
        in_specs=[SMEM, VMEM, VMEM, VMEM],
        out_specs=(VMEM, VMEM),
        scratch_shapes=[pltpu.VMEM((B, 128), F32)],
        compiler_params=pltpu.CompilerParams(vmem_limit_bytes=16 << 20),
        cost_estimate=pl.CostEstimate(flops=0, bytes_accessed=40 << 20, transcendentals=0),
        name="second",
    )(pivot_tiles, inv0, w10, w11)

    pair = send(code, [((z, y, c), (z, y, 1 - c)) for z, y, c in PLACES])
    pair = jnp.where(where[2] == 0, jnp.concatenate([code, pair]), jnp.concatenate([pair, code]))
    chip = jnp.where(iota((32, 128), 0) == where[0] * 4 + where[1], pair[None, :], -1)
    queued, queued_far = plan(True, where, chip)
    received = [right0, right2, far00, far01, far10, far11, left00, left3]
    factor, zero, yh, yl = pl.pallas_call(
        panel_kernel,
        out_shape=(jax.ShapeDtypeStruct((1, 2, 1, T, 2 * T), F32), jax.ShapeDtypeStruct((T, T), F32))
        + (jax.ShapeDtypeStruct((8, T, 2 * T), BF16),) * 2,
        in_specs=[SMEM, SMEM] + [VMEM] * 12,
        out_specs=(VMEM,) * 4,
        compiler_params=pltpu.CompilerParams(vmem_limit_bytes=18 << 20),
        name="panel",
    )(place.reshape(1), jnp.maximum(tile[0:1], 0), inv0, l10, inv1, front, *received)
    root = [send(zero, [((z, y, c), (0, y, c)) for y in range(4) for c in range(2)]) for z in (3, 4, 5)]
    work = pl.pallas_call(
        update_kernel,
        out_shape=tiles(TILES)[0],
        in_specs=[SMEM] + [VMEM] * 3,
        out_specs=VMEM,
        compiler_params=pltpu.CompilerParams(vmem_limit_bytes=14 << 20),
        name="update",
    )(place.reshape(1), front, yh, yl)
    over, own, theirs = sparse(work, root, code, where, queued, queued_far)
    _, ancestor = lax.while_loop(
        lambda state: state[0],
        lambda state: (False, dense(work, tile, table[2])),
        (over[0, 0] > 0.0, own + theirs),
    )
    return (factor, ancestor.reshape(1, 1, ASLOT, T, T))


def solution(mesh):
    in_specs = (P("leaf", None, "front", None, None), P("leaf"), P("leaf", "front", None, None))
    out_specs = (P("leaf", None, "front", None, None), P("leaf", "front", None, None, None))
    return jax.shard_map(local, mesh=mesh, in_specs=in_specs, out_specs=out_specs, check_vma=False)
```

```python
import functools

import jax
import jax.numpy as jnp
from jax import lax
from jax.experimental import pallas as pl
from jax.experimental.pallas import tpu as pltpu
from jax.sharding import PartitionSpec as P

PT = 2
ASLOT = 16
TILES = 14
N1, N2 = 8, 5
FY1, FY2 = 5, 3
FZ, FZ4 = 5, 4
NY1, NY2 = 11, 7
BUF, ZN1, ZN2, YF1, YF2, YN1, YN2, ZF3, ZF4, ROOT = range(10)
B = 64
T = 256
F32 = jnp.float32
BF16 = jnp.bfloat16
HIGHEST = lax.Precision.HIGHEST
VMEM = pl.BlockSpec(memory_space=pltpu.VMEM)
SMEM = pl.BlockSpec(memory_space=pltpu.SMEM)
ANY = pl.BlockSpec(memory_space=pl.ANY)
NN = (((1,), (0,)), ((), ()))
NT = (((1,), (1,)), ((), ()))
TN = (((0,), (0,)), ((), ()))


def dot(a, b, dims):
    return lax.dot_general(a, b, dims, precision=HIGHEST, preferred_element_type=F32)


def dot1(a, b, dims):
    return lax.dot_general(a, b, dims, preferred_element_type=F32)


def split(x):
    high = x.astype(BF16)
    return high, (x - high.astype(F32)).astype(BF16)


def split3(x):
    high = x.astype(BF16)
    rest = x - high.astype(F32)
    mid = rest.astype(BF16)
    return high, mid, (rest - mid.astype(F32)).astype(BF16)


def dot3(a, b, dims):
    ah, al = a
    bh, bl = b
    return dot1(ah, bh, dims) + (dot1(ah, bl, dims) + dot1(al, bh, dims))


def factor64(groups, f_ref):
    sub = lax.broadcasted_iota(jnp.int32, (8, 128), 0)

    def body(it, gs):
        count = len(gs)
        cols = [[jnp.broadcast_to(g[:, t:t + 1], (8, 128)) for t in range(8)] for g in gs]
        rows = [jnp.broadcast_to(gs[0][t:t + 1, :], (8, 128)) for t in range(8)]
        s = [[jnp.broadcast_to(cols[0][t][u:u + 1, :], (8, 128)) if u >= t else None for t in range(8)] for u in range(8)]
        inv = [None] * 8
        for t in range(8):
            inv[t] = 1.0 / s[t][t]
            for u in range(t + 1, 8):
                low = s[u][t] * inv[t]
                for v in range(u, 8):
                    s[v][u] = s[v][u] - low * s[v][t]
                rows[u] = rows[u] - low * rows[t]
                for g in range(1, count):
                    cols[g][u] = cols[g][u] - low * cols[g][t]
        done = jnp.zeros((8, 128), F32)
        for t in range(8):
            done = jnp.where(sub == t, rows[t] * lax.rsqrt(s[t][t]), done)
        f_ref[pl.ds(pl.multiple_of(it * 8, 8), 8), :] = pltpu.roll(done, it * 8, 1)
        scaled = [rows[t] * inv[t] for t in range(8)]
        left = []
        for g in range(1, count):
            piece = gs[g]
            for t in range(8):
                piece = piece - cols[g][t] * scaled[t]
            left.append(pltpu.roll(piece, 120, 1))
        left.append(gs[0])
        return tuple(left)

    groups = tuple(groups)
    for first in range(0, 8, 2):
        groups = lax.fori_loop(first, first + 2, body, groups)[:6 - first]


def factor256(x_ref, f_ref):
    lane = lax.broadcasted_iota(jnp.int32, (B, 128), 1)
    row = lax.broadcasted_iota(jnp.int32, (B, 128), 0)
    ident = (lane - B == row).astype(F32)
    col = lax.broadcasted_iota(jnp.int32, (B, T), 1)
    wide_row = lax.broadcasted_iota(jnp.int32, (B, T), 0)
    for k in range(T // B):
        lo = k * B
        strip = x_ref[lo:lo + B, :]
        block = strip[:, (k // 2) * 128:(k // 2) * 128 + 128]
        if k % 2:
            block = pltpu.roll(block, B, 1)
        both = jnp.where(lane < B, block, ident)
        factor64([both[8 * g:8 * g + 8, :] for g in range(8)], f_ref)
        block_inv = f_ref[...][:, B:]
        inside = (col >= lo) & (col < lo + B)
        strip = jnp.where(inside, (col - lo == wide_row).astype(F32), strip)
        out = dot(block_inv, strip, NN)
        x_ref[lo:lo + B, :] = jnp.where(col < lo + B, out, 0.0)
        if lo + B < T:
            rest = T - lo - B
            rest_col = lax.broadcasted_iota(jnp.int32, (rest, T), 1)
            old = x_ref[lo + B:, :]
            old = jnp.where((rest_col >= lo) & (rest_col < lo + B), 0.0, old)
            x_ref[lo + B:, :] = old - dot(out[:, lo + B:], out, TN)


def first_kernel(w00_ref, inv0_ref, f_ref):
    inv0_ref[...] = w00_ref[...]
    factor256(inv0_ref, f_ref)


def second_kernel(piv_ref, inv0_ref, w10_ref, w11_ref, l10_ref, inv1_ref, f_ref):
    l10 = dot(w10_ref[...], inv0_ref[...], NT)
    l10_ref[...] = l10
    inv1_ref[...] = jnp.zeros((T, T), F32)

    @pl.when(piv_ref[0] >= 2)
    def _():
        inv1_ref[...] = w11_ref[...] - dot(l10, l10, NT)
        factor256(inv1_ref, f_ref)


def iota(shape, dim):
    return lax.broadcasted_iota(jnp.int32, shape, dim)


def fdot(a, b):
    return lax.dot_general(a, b, (((1,), (0,)), ((), ())), preferred_element_type=F32)


def route(codes, z, y, c, chip=False):
    shape, sq, rows = (32, 128), (128, 128), (32, 32)
    row, lane = iota(shape, 0), iota(shape, 1)
    zs, ys = row // 4, row % 4
    cs, zd, yd, cd = lane // 64, (lane // 8) % 8, (lane // 2) % 4, lane % 2
    dz, dy = (zd - zs + 8) % 8, (yd - ys + 4) % 4
    hops = jnp.minimum(dz, 8 - dz)
    far = hops > 2
    used = codes >= 0
    rooted = used & (lane % 64 == 0) & far
    live = used & ~rooted
    near = used & (~far | rooted)
    tile = jnp.where(used, codes // 16, 0)
    slot = jnp.where(used, codes % 16, 0)
    la, lb = iota(sq, 0), iota(sq, 1)
    before = la < lb
    same_zd = (la // 8) % 8 == (lb // 8) % 8
    same_yd = (la // 2) % 4 == (lb // 2) % 4
    ra, rb = iota(rows, 0), iota(rows, 1)
    same_ys = ra % 4 == rb % 4
    same_zs = ra // 4 == rb // 4

    def f(x):
        return x.astype(F32)

    def count(mask, lanes, peers):
        rank = fdot(f(mask), f(before & lanes))
        total = fdot(f(mask), f(lanes))
        if peers is not None:
            rank = rank + fdot(f(peers & (rb < ra)), total)
            total = fdot(f(peers), total)
        return rank, total

    def halves(n_up, n_both, n_down):
        up = jnp.clip(jnp.floor((n_both + n_down - n_up + 1.0) * 0.5), 0.0, n_both)
        return up, n_both - up

    every = la >= 0
    over = jnp.full(shape, -1.0, F32)
    r1, n1 = count(live & (dz == 1), every, None)
    r2, n2 = count(live & (dz == 2), every, None)
    r6, n6 = count(live & (dz == 6), every, None)
    r7, n7 = count(live & (dz == 7), every, None)
    zpos = jnp.where(dz == 1, n2 + r1, jnp.where(dz == 2, r2, jnp.where(dz == 6, r6, n6 + r7)))
    over = jnp.maximum(over, jnp.maximum(n1 + n2, n7 + n6) - 2 * N1)
    over = jnp.maximum(over, jnp.maximum(n2, n6) - 2 * N2)

    def ring(mask, lanes, peers, near, distant):
        a1, m1 = count(mask & (dy == 1), lanes, peers)
        a2, m2 = count(mask & (dy == 2), lanes, peers)
        a3, m3 = count(mask & (dy == 3), lanes, peers)
        up, down = halves(m1, m2, m3)
        minus = (dy == 3) | ((dy == 2) & (a2 >= up))
        pos = jnp.where(dy == 1, up + a1, jnp.where(dy == 3, down + a3, jnp.where(a2 < up, a2, a2 - up)))
        excess = jnp.maximum(jnp.maximum(up + m1, down + m3) - near, jnp.maximum(up, down) - distant)
        return minus.astype(jnp.int32), pos.astype(jnp.int32), excess

    fy_way, fy_pos, excess = ring(live & far, every, None, 2 * FY1, 2 * FY2)
    over = jnp.maximum(over, excess)
    r3, n3 = count(live & (dz == 3), same_yd, same_zs)
    r4, n4 = count(live & (dz == 4), same_yd, same_zs)
    r5, n5 = count(live & (dz == 5), same_yd, same_zs)
    up, down = halves(n3, n4, n5)
    fz_pos = jnp.where(dz == 3, up + r3, jnp.where(dz == 5, down + r5, jnp.where(r4 < up, r4, r4 - up)))
    over = jnp.maximum(over, jnp.maximum(up + n3, down + n5) - 2 * FZ)
    over = jnp.maximum(over, jnp.maximum(up, down) - 2 * FZ4)
    z_way = ((dz > 4) | ((dz == 4) & (r4 >= up))).astype(jnp.int32)
    ny_way, ny_pos, excess = ring(near, same_zd, same_ys, 2 * NY1, 2 * NY2)
    over = jnp.maximum(over, excess)
    zpos, fz_pos = zpos.astype(jnp.int32), fz_pos.astype(jnp.int32)

    def at(kind, way, pos):
        return ((kind * 2 + way) * 2 + (pos % 2 != c)) * 16 + jnp.minimum(pos // 2, 15)

    def listed(mask, way, pos, code):
        key = jnp.where(mask & (pos % 2 == c) & (pos < 32), way * 16 + pos // 2, -1)
        acc = jnp.zeros(shape, jnp.int32)
        for r in range(32):
            acc = acc + jnp.where(key[r:r + 1, :] == row, code[r:r + 1, :] + 1, 0)
        column = jnp.sum(acc, axis=1, keepdims=True)
        return jnp.sum(jnp.where(lane == row, column, 0), axis=0, keepdims=True) - 1

    held = (BUF * 4 + (cs != c)) * 16 + tile
    if chip:
        here = live & (row == z * 4 + y)
        queued = listed(here & ~far & (dz > 0), z_way, zpos, held)
        return queued, listed(here & far & (dy > 0), fy_way, fy_pos, held)
    after_y = jnp.where(dy == 0, held, at(jnp.where(dy == 2, YF2, YF1), fy_way, fy_pos))
    turn_far = listed(live & far & (zs == z) & (yd == y), z_way, fz_pos, after_y)
    after_z = jnp.where(dz == 0, held, at(jnp.where(hops == 1, ZN1, ZN2), z_way, zpos))
    after_z = jnp.where(rooted, (ROOT * 4 + (cs != c)) * 16 + zs - 3, after_z)
    turn_near = listed(near & (zd == z) & (ys == y) & (dy > 0), ny_way, ny_pos, after_z)
    end_near = jnp.where(dy == 0, after_z, at(jnp.where(dy == 2, YN2, YN1), ny_way, ny_pos))
    end_far = at(jnp.where(dz == 4, ZF4, ZF3), z_way, fz_pos)
    keeper = jnp.where(far & ~rooted, fz_pos % 2, jnp.where(dy > 0, ny_pos % 2, cd))
    mine = used & (zd == z) & (yd == y) & (keeper == c)
    end = jnp.where(mine, (jnp.where(live & far, end_far, end_near) * 2 + (cd != c)) * 16 + slot, -1)
    return turn_near, turn_far, end, jnp.max(over, keepdims=True)


def plan_kernel(chip, where_ref, codes_ref, *out_refs):
    for ref, value in zip(out_refs, route(codes_ref[...], where_ref[0], where_ref[1], where_ref[2], chip)):
        ref[...] = value


def plan(chip, where, codes):
    shapes = [(1, 128)] * 2 if chip else [(1, 128), (1, 128), (32, 128), (1, 1)]
    return pl.pallas_call(
        lambda *refs: plan_kernel(chip, *refs),
        out_shape=tuple(jax.ShapeDtypeStruct(s, F32 if s == (1, 1) else jnp.int32) for s in shapes),
        in_specs=[SMEM, VMEM],
        out_specs=(VMEM,) * len(shapes),
        compiler_params=pltpu.CompilerParams(vmem_limit_bytes=6 << 20),
        name="plan_chip" if chip else "plan",
    )(where, codes)


def panel_kernel(place_ref, first_ref, inv0_ref, l10_ref, inv1_ref, front_ref, *refs):
    right0, right2, far00, far01, far10, far11, left00, left3, factor_ref, zero_ref, yh_ref, yl_ref = refs
    pieces = [
        right0.at[0], right0.at[1], right2.at[0], right2.at[1], far00, far01, far10, far11,
        left00, left3.at[0], left3.at[1], left3.at[2],
    ]
    place = place_ref[0]
    a0 = split3(inv0_ref[...])
    low = split(l10_ref[...])
    inv1 = inv1_ref[...]
    for q in range(4):
        for r in range(2):
            if q == 0:
                p0 = front_ref[0, r, 0, :, 0:T]
                p1 = front_ref[0, r, 0, :, T:2 * T].astype(F32)
            else:
                p0 = pieces[(q - 1) * 4 + r * 2][...].astype(BF16)
                p1 = pieces[(q - 1) * 4 + r * 2 + 1][...]
            y0 = dot1(p0, a0[0], NT) + (dot1(p0, a0[1], NT) + dot1(p0, a0[2], NT))
            y0h, y0l = split(y0)
            p1 = p1 - dot3((y0h, y0l), low, NT)
            y1 = dot(p1, inv1, NT)
            if r == 0:
                owner = lax.rem(place + q, 4)
                y1 = jnp.where(owner > 0, y1, 0.0)
            y1h, y1l = split(y1)
            n = q * 2 + r
            yh_ref[n, :, 0:T] = y0h
            yl_ref[n, :, 0:T] = y0l
            yh_ref[n, :, T:2 * T] = y1h
            yl_ref[n, :, T:2 * T] = y1l
            if q == 0:
                factor_ref[0, r, 0, :, 0:T] = y0
                factor_ref[0, r, 0, :, T:2 * T] = y1
    row = first_ref[0] // 7
    column = first_ref[0] % 7 + 1
    n = lax.rem(column % 4 - place + 4, 4) * 2 + column // 4
    start = pl.multiple_of(column * T, T)
    tile = front_ref[0, row, 0, :, pl.ds(start, T)].astype(F32)
    zero_ref[...] = tile - dot3((yh_ref[row], yl_ref[row]), (yh_ref[n], yl_ref[n]), NT)


def update_kernel(place_ref, front_ref, yh_ref, yl_ref, out_ref):
    place = place_ref[0]
    for r in range(2):
        for n in range(8):
            column = lax.rem(place + n // 2, 4) + 4 * (n % 2)

            @pl.when(column > 0)
            def _():
                start = pl.multiple_of(column * T, T)
                tile = front_ref[0, r, 0, :, pl.ds(start, T)].astype(F32)
                own = (yh_ref[r], yl_ref[r])
                other = (yh_ref[n], yl_ref[n])
                out_ref[r * 7 + column - 1] = tile - dot3(own, other, NT)


def arrays(kind, own, other=()):
    out = []
    for sib, xs in ((0, own), (1, other)):
        for way, x in enumerate(xs):
            out.append(((kind * 2 + way) * 2 + sib,) + (x if isinstance(x, tuple) else (0, x)))
    return out


def copy_from(sources, code, target_ref, sem):
    for sid, first, ref in sources:
        @pl.when(code // 16 == sid)
        def _():
            pltpu.make_async_copy(ref.at[jnp.minimum(first + code % 16, ref.shape[0] - 1)], target_ref, sem).start()


def operands(sources):
    xs, numbered = [], []
    for sid, first, x in sources:
        where = [i for i, other in enumerate(xs) if other is x]
        if not where:
            xs.append(x)
        numbered.append((sid, first, where[0] if where else len(xs) - 1))
    return numbered, xs


def gather_kernel(numbered, size, table_ref, *refs):
    sources = [(sid, first, refs[i]) for sid, first, i in numbered]
    *outs, sem = refs[-3:]
    for way, out in enumerate(outs):
        def start(i, _):
            code = table_ref[0, way * 16 + i]

            @pl.when(code >= 0)
            def _():
                copy_from(sources, code, out.at[i], sem.at[way * size + i])
            return 0

        lax.fori_loop(0, size, start, 0)
    for way, out in enumerate(outs):
        def wait(i, _):
            @pl.when(table_ref[0, way * 16 + i] >= 0)
            def _():
                pltpu.make_async_copy(refs[0].at[0], out.at[i], sem.at[way * size + i]).wait()
            return 0

        lax.fori_loop(0, size, wait, 0)


def gather(table, sources, size, name, *first):
    numbered, xs = operands(sources)
    xs = xs + list(first)
    return pl.pallas_call(
        lambda *refs: gather_kernel(numbered, size, *refs),
        out_shape=tiles(size, size),
        in_specs=[SMEM] + [ANY] * len(xs),
        out_specs=(VMEM,) * 2,
        scratch_shapes=[pltpu.SemaphoreType.DMA((2 * size,))],
        compiler_params=pltpu.CompilerParams(vmem_limit_bytes=10 << 20),
        cost_estimate=pl.CostEstimate(flops=0, bytes_accessed=8 << 20, transcendentals=0),
        name=name,
    )(table, *xs)


DEPTH = 12


def sum_kernel(numbered, other, where_ref, table_ref, *refs):
    *ins, out_ref, list_ref, buf_ref, sem = refs
    z, y = where_ref[0], where_ref[1]
    sources = [(sid, first, ins[i]) for sid, first, i in numbered]

    def collect(i, n):
        code = table_ref[i // 4, (i // 2 % 2) * 64 + z * 8 + y * 2 + i % 2]

        take = (code >= 0) & ((code // 16) % 2 == other)

        @pl.when(take)
        def _():
            list_ref[n] = code
        return n + take.astype(jnp.int32)

    n = lax.fori_loop(0, 128, collect, jnp.int32(0))

    def start(i):
        slot = lax.rem(i, DEPTH)
        copy_from(sources, list_ref[i] // 32, buf_ref.at[slot], sem.at[slot])

    def prime(i, _):
        start(i)
        return 0

    def step(i, _):
        slot = lax.rem(i, DEPTH)
        pltpu.make_async_copy(ins[0].at[0], buf_ref.at[slot], sem.at[slot]).wait()
        out_ref[list_ref[i] % 16] += buf_ref[slot]

        @pl.when(i + DEPTH < n)
        def _():
            start(i + DEPTH)
        return 0

    lax.fori_loop(0, jnp.minimum(n, DEPTH), prime, 0)
    out_ref[...] = jnp.zeros_like(out_ref)
    lax.fori_loop(0, n, step, 0)


def add_up(where, table, sources, other):
    numbered, xs = operands(sources)
    return pl.pallas_call(
        lambda *refs: sum_kernel(numbered, other, *refs),
        out_shape=tiles(ASLOT)[0],
        in_specs=[SMEM, SMEM] + [ANY] * len(xs),
        out_specs=VMEM,
        scratch_shapes=[pltpu.SMEM((256,), jnp.int32), pltpu.VMEM((DEPTH, T, T), F32), pltpu.SemaphoreType.DMA((DEPTH,))],
        compiler_params=pltpu.CompilerParams(vmem_limit_bytes=16 << 20),
        cost_estimate=pl.CostEstimate(flops=0, bytes_accessed=30 << 20, transcendentals=0),
        name="sum_other" if other else "sum_own",
    )(where, table, *xs)


def slots_kernel(tile_ref, own_ref, out_ref, sem):
    def start(p, _):
        tile = tile_ref[p]

        @pl.when(tile >= 0)
        def _():
            pltpu.make_async_copy(own_ref.at[tile], out_ref.at[p], sem.at[p]).start()
        return 0

    def wait(p, _):
        @pl.when(tile_ref[p] >= 0)
        def _():
            pltpu.make_async_copy(own_ref.at[0], out_ref.at[p], sem.at[p]).wait()
        return 0

    lax.fori_loop(0, 64, start, 0)
    lax.fori_loop(0, 64, wait, 0)


def add_kernel(target_ref, arrived_ref, out_ref):
    step = pl.program_id(0)

    @pl.when(step == 0)
    def _():
        out_ref[...] = jnp.zeros_like(out_ref)

    for i in range(4):
        target = target_ref[step * 4 + i]

        @pl.when(target >= 0)
        def _():
            out_ref[target] += arrived_ref[i]


def tiles(*counts):
    return tuple(jax.ShapeDtypeStruct((n, T, T), F32) for n in counts)


def leaf_id(z, y, c):
    return ((z % 8) * 4 + y % 4) * 2 + c


PLACES = [(z, y, c) for z in range(8) for y in range(4) for c in range(2)]


def send(x, pairs):
    return lax.ppermute(x, "leaf", [(leaf_id(*a), leaf_id(*b)) for a, b in pairs])


def dense(work, tile, slot):
    outgoing = pl.pallas_call(
        slots_kernel,
        out_shape=tiles(64)[0],
        in_specs=[SMEM, ANY],
        out_specs=ANY,
        scratch_shapes=[pltpu.SemaphoreType.DMA((64,))],
        name="slots",
    )(tile, work)
    arrived = lax.all_to_all(outgoing, "leaf", split_axis=0, concat_axis=0, tiled=True)
    targets = lax.all_to_all(slot, "leaf", split_axis=0, concat_axis=0, tiled=True)
    return pl.pallas_call(
        add_kernel,
        out_shape=tiles(ASLOT)[0],
        grid=(16,),
        in_specs=[SMEM, pl.BlockSpec((4, T, T), lambda i: (i, 0, 0))],
        out_specs=pl.BlockSpec((ASLOT, T, T), lambda i: (0, 0, 0)),
        compiler_params=pltpu.CompilerParams(vmem_limit_bytes=32 << 20),
        name="add",
    )(targets, arrived)


def tie(x, *others):
    return lax.optimization_barrier((x,) + others)[0]


def sparse(work, root, code, where, queued, queued_far):
    swap = [((z, y, c), (z, y, 1 - c)) for z, y, c in PLACES]
    along_z = [[((z, y, c), (z + s, y, c)) for z, y, c in PLACES] for s in (1, -1)]
    along_y = [[((z, y, c), (z, y + s, c)) for z, y, c in PLACES] for s in (1, -1)]

    def sends(xs, ways):
        return [send(x, way) for x, way in zip(xs, ways)]

    def swaps(xs):
        return [send(x, swap) for x in xs]

    def after(xs, *others):
        return list(lax.optimization_barrier(tuple(xs) + others)[:len(xs)])

    other = send(after([work], *root)[0], swap)
    both = arrays(BUF, [work], [other])
    near_list = gather(queued, both, N1, "queue")
    n1 = sends(near_list, along_z)
    far_list = gather(tie(queued_far, *near_list), both, FY1, "queue_far")
    f1 = sends(far_list, along_y)
    everyone = jnp.broadcast_to(after([code], *near_list, *far_list)[0], (64, 64))
    codes = lax.all_to_all(everyone, "leaf", split_axis=0, concat_axis=0, tiled=True).reshape(32, 128)
    f2 = sends(after([x[:FY2] for x in f1], codes), along_y)
    turn_near, turn_far, end, over = plan(False, where, codes)
    n2 = sends(after([x[:N2] for x in n1], *f1), along_z)
    mixed = send(after([jnp.concatenate([*f1, *f2])], *n1)[0], swap)
    parts = [(cut, mixed) for cut in (0, FY1, 2 * FY1, 2 * FY1 + FY2)]
    column = jnp.stack(root)
    column_other = send(after([column], *n1)[0], swap)
    far_list = gather(turn_far, both + arrays(YF1, f1, parts[0:2]) + arrays(YF2, f2, parts[2:4]), FZ, "turn_far", column_other)
    n1_other = swaps(after(n1, *far_list))
    z1 = sends(after(far_list, *n2, *n1_other), along_z)
    near_sources = both + arrays(ZN1, n1, n1_other) + arrays(ZN2, n2, swaps(n2)) + arrays(ROOT, [column], [column_other])
    near_list = gather(turn_near, near_sources, NY1, "turn_near")
    z2 = sends(after(z1, *near_list), along_z)
    y1 = sends(near_list, along_y)
    z3 = sends(z2, along_z)
    y2 = sends(after([x[:NY2] for x in y1], *z2), along_y)
    z4 = sends(after([x[:FZ4] for x in z3], *y1), along_z)
    sources = near_sources + arrays(YN1, y1) + arrays(YN2, y2) + arrays(ZF3, z3) + arrays(ZF4, z4)
    theirs = add_up(where, end, sources, 1)
    own = add_up(tie(where, theirs), end, sources, 0)
    return over, own, send(theirs, swap)


def local(front, pivot_tiles, send_table):
    place = lax.axis_index("front").astype(jnp.int32)
    leaf = lax.axis_index("leaf").astype(jnp.int32)
    where = jnp.stack([leaf // 8, (leaf // 2) % 4, leaf % 2])
    table = send_table[0, 0]
    used = table[0] >= 0
    tile = jnp.where(used, table[0] * 7 + table[1] - 1, -1)
    code = jnp.where(used, tile * 16 + table[2], -1)
    up = [(i, (i + 1) % 4) for i in range(4)]
    down = [(i, (i - 1) % 4) for i in range(4)]
    own = [[front[0, r, 0, :, k * T:k * T + T].astype(F32) for k in range(2)] for r in range(2)]
    def across(x, shift, *others):
        return lax.ppermute(tie(x, *others) if others else x, "front", [(i, (i + shift) % 4) for i in range(4)])

    left00 = across(own[0][0], 1)
    right0 = across(jnp.stack(own[0]), -1)
    far00 = across(left00, 1)
    far01 = across(right0[1], -1)
    left3 = across(jnp.stack([own[0][1], own[1][0], own[1][1]]), 1, far00, far01)
    right2 = across(jnp.stack(own[1]), -1, far00, far01)
    far10 = across(left3[1], 1)
    far11 = across(right2[1], -1)
    from_left = [[left00, left3[0]], [left3[1], left3[2]]]
    from_right = [[right0[0], right0[1]], [right2[0], right2[1]]]
    from_far = [[far00, far01], [far10, far11]]
    by_q = [own, from_right, from_far, from_left]

    def of_owner(owner, r, k, *after):
        q = lax.rem(owner - place + 4, 4)
        if after:
            q = tie(q, *after)
        out = by_q[0][r][k]
        for i in range(1, 4):
            out = jnp.where(q == i, by_q[i][r][k], out)
        return out

    inv0 = pl.pallas_call(
        first_kernel,
        out_shape=jax.ShapeDtypeStruct((T, T), F32),
        in_specs=[VMEM],
        out_specs=VMEM,
        scratch_shapes=[pltpu.VMEM((B, 128), F32)],
        compiler_params=pltpu.CompilerParams(vmem_limit_bytes=8 << 20),
        cost_estimate=pl.CostEstimate(flops=0, bytes_accessed=20 << 20, transcendentals=0),
        name="first",
    )(of_owner(0, 0, 0))
    w10 = of_owner(1, 0, 0, inv0)
    w11 = of_owner(1, 0, 1, inv0)
    l10, inv1 = pl.pallas_call(
        second_kernel,
        out_shape=(jax.ShapeDtypeStruct((T, T), F32),) * 2,
        in_specs=[SMEM, VMEM, VMEM, VMEM],
        out_specs=(VMEM, VMEM),
        scratch_shapes=[pltpu.VMEM((B, 128), F32)],
        compiler_params=pltpu.CompilerParams(vmem_limit_bytes=16 << 20),
        cost_estimate=pl.CostEstimate(flops=0, bytes_accessed=40 << 20, transcendentals=0),
        name="second",
    )(pivot_tiles, inv0, w10, w11)

    pair = send(code, [((z, y, c), (z, y, 1 - c)) for z, y, c in PLACES])
    pair = jnp.where(where[2] == 0, jnp.concatenate([code, pair]), jnp.concatenate([pair, code]))
    chip = jnp.where(iota((32, 128), 0) == where[0] * 4 + where[1], pair[None, :], -1)
    queued, queued_far = plan(True, where, chip)
    received = [right0, right2, far00, far01, far10, far11, left00, left3]
    factor, zero, yh, yl = pl.pallas_call(
        panel_kernel,
        out_shape=(jax.ShapeDtypeStruct((1, 2, 1, T, 2 * T), F32), jax.ShapeDtypeStruct((T, T), F32))
        + (jax.ShapeDtypeStruct((8, T, 2 * T), BF16),) * 2,
        in_specs=[SMEM, SMEM] + [VMEM] * 12,
        out_specs=(VMEM,) * 4,
        compiler_params=pltpu.CompilerParams(vmem_limit_bytes=18 << 20),
        name="panel",
    )(place.reshape(1), jnp.maximum(tile[0:1], 0), inv0, l10, inv1, front, *received)
    root = [send(zero, [((z, y, c), (0, y, c)) for y in range(4) for c in range(2)]) for z in (3, 4, 5)]
    work = pl.pallas_call(
        update_kernel,
        out_shape=tiles(TILES)[0],
        in_specs=[SMEM] + [VMEM] * 3,
        out_specs=VMEM,
        compiler_params=pltpu.CompilerParams(vmem_limit_bytes=14 << 20),
        name="update",
    )(place.reshape(1), front, yh, yl)
    over, own, theirs = sparse(work, root, code, where, queued, queued_far)
    _, ancestor = lax.while_loop(
        lambda state: state[0],
        lambda state: (False, dense(work, tile, table[2])),
        (over[0, 0] > 0.0, own + theirs),
    )
    return (factor, ancestor.reshape(1, 1, ASLOT, T, T))


def solution(mesh):
    in_specs = (P("leaf", None, "front", None, None), P("leaf"), P("leaf", "front", None, None))
    out_specs = (P("leaf", None, "front", None, None), P("leaf", "front", None, None, None))
    return jax.shard_map(local, mesh=mesh, in_specs=in_specs, out_specs=out_specs, check_vma=False)
```

```python
import functools

import jax
import jax.numpy as jnp
from jax import lax
from jax.experimental import pallas as pl
from jax.experimental.pallas import tpu as pltpu
from jax.sharding import PartitionSpec as P

PT = 2
ASLOT = 16
TILES = 14
N1, N2 = 8, 5
FY1, FY2 = 5, 3
FZ, FZ4 = 5, 4
NY1, NY2 = 11, 7
BUF, ZN1, ZN2, YF1, YF2, YN1, YN2, ZF3, ZF4, ROOT = range(10)
B = 64
T = 256
F32 = jnp.float32
BF16 = jnp.bfloat16
HIGHEST = lax.Precision.HIGHEST
VMEM = pl.BlockSpec(memory_space=pltpu.VMEM)
SMEM = pl.BlockSpec(memory_space=pltpu.SMEM)
ANY = pl.BlockSpec(memory_space=pl.ANY)
NN = (((1,), (0,)), ((), ()))
NT = (((1,), (1,)), ((), ()))
TN = (((0,), (0,)), ((), ()))


def dot(a, b, dims):
    return lax.dot_general(a, b, dims, precision=HIGHEST, preferred_element_type=F32)


def dot1(a, b, dims):
    return lax.dot_general(a, b, dims, preferred_element_type=F32)


def split(x):
    high = x.astype(BF16)
    return high, (x - high.astype(F32)).astype(BF16)


def split3(x):
    high = x.astype(BF16)
    rest = x - high.astype(F32)
    mid = rest.astype(BF16)
    return high, mid, (rest - mid.astype(F32)).astype(BF16)


def dot3(a, b, dims):
    ah, al = a
    bh, bl = b
    return dot1(ah, bh, dims) + (dot1(ah, bl, dims) + dot1(al, bh, dims))


def factor64(groups, f_ref):
    sub = lax.broadcasted_iota(jnp.int32, (8, 128), 0)

    def body(it, gs):
        count = len(gs)
        cols = [[jnp.broadcast_to(g[:, t:t + 1], (8, 128)) for t in range(8)] for g in gs]
        rows = [jnp.broadcast_to(gs[0][t:t + 1, :], (8, 128)) for t in range(8)]
        s = [[jnp.broadcast_to(cols[0][t][u:u + 1, :], (8, 128)) if u >= t else None for t in range(8)] for u in range(8)]
        inv = [None] * 8
        for t in range(8):
            inv[t] = 1.0 / s[t][t]
            for u in range(t + 1, 8):
                low = s[u][t] * inv[t]
                for v in range(u, 8):
                    s[v][u] = s[v][u] - low * s[v][t]
                rows[u] = rows[u] - low * rows[t]
                for g in range(1, count):
                    cols[g][u] = cols[g][u] - low * cols[g][t]
        done = jnp.zeros((8, 128), F32)
        for t in range(8):
            done = jnp.where(sub == t, rows[t] * lax.rsqrt(s[t][t]), done)
        f_ref[pl.ds(pl.multiple_of(it * 8, 8), 8), :] = pltpu.roll(done, it * 8, 1)
        scaled = [rows[t] * inv[t] for t in range(8)]
        left = []
        for g in range(1, count):
            piece = gs[g]
            for t in range(8):
                piece = piece - cols[g][t] * scaled[t]
            left.append(pltpu.roll(piece, 120, 1))
        left.append(gs[0])
        return tuple(left)

    groups = tuple(groups)
    for first in range(0, 8, 2):
        groups = lax.fori_loop(first, first + 2, body, groups)[:6 - first]


def factor256(x_ref, f_ref):
    lane = lax.broadcasted_iota(jnp.int32, (B, 128), 1)
    row = lax.broadcasted_iota(jnp.int32, (B, 128), 0)
    ident = (lane - B == row).astype(F32)
    col = lax.broadcasted_iota(jnp.int32, (B, T), 1)
    wide_row = lax.broadcasted_iota(jnp.int32, (B, T), 0)
    for k in range(T // B):
        lo = k * B
        strip = x_ref[lo:lo + B, :]
        block = strip[:, (k // 2) * 128:(k // 2) * 128 + 128]
        if k % 2:
            block = pltpu.roll(block, B, 1)
        both = jnp.where(lane < B, block, ident)
        factor64([both[8 * g:8 * g + 8, :] for g in range(8)], f_ref)
        block_inv = f_ref[...][:, B:]
        inside = (col >= lo) & (col < lo + B)
        strip = jnp.where(inside, (col - lo == wide_row).astype(F32), strip)
        out = dot(block_inv, strip, NN)
        x_ref[lo:lo + B, :] = jnp.where(col < lo + B, out, 0.0)
        if lo + B < T:
            rest = T - lo - B
            rest_col = lax.broadcasted_iota(jnp.int32, (rest, T), 1)
            old = x_ref[lo + B:, :]
            old = jnp.where((rest_col >= lo) & (rest_col < lo + B), 0.0, old)
            x_ref[lo + B:, :] = old - dot(out[:, lo + B:], out, TN)


def first_kernel(w00_ref, inv0_ref, f_ref):
    inv0_ref[...] = w00_ref[...]
    factor256(inv0_ref, f_ref)


def second_kernel(piv_ref, inv0_ref, w10_ref, w11_ref, l10_ref, inv1_ref, f_ref):
    l10 = dot(w10_ref[...], inv0_ref[...], NT)
    l10_ref[...] = l10
    inv1_ref[...] = jnp.zeros((T, T), F32)

    @pl.when(piv_ref[0] >= 2)
    def _():
        inv1_ref[...] = w11_ref[...] - dot(l10, l10, NT)
        factor256(inv1_ref, f_ref)


def iota(shape, dim):
    return lax.broadcasted_iota(jnp.int32, shape, dim)


def fdot(a, b):
    return lax.dot_general(a, b, (((1,), (0,)), ((), ())), preferred_element_type=F32)


def route(codes, z, y, c, chip=False):
    shape, sq, rows = (32, 128), (128, 128), (32, 32)
    row, lane = iota(shape, 0), iota(shape, 1)
    zs, ys = row // 4, row % 4
    cs, zd, yd, cd = lane // 64, (lane // 8) % 8, (lane // 2) % 4, lane % 2
    dz, dy = (zd - zs + 8) % 8, (yd - ys + 4) % 4
    hops = jnp.minimum(dz, 8 - dz)
    far = hops > 2
    used = codes >= 0
    rooted = used & (lane % 64 == 0) & far
    live = used & ~rooted
    near = used & (~far | rooted)
    tile = jnp.where(used, codes // 16, 0)
    slot = jnp.where(used, codes % 16, 0)
    la, lb = iota(sq, 0), iota(sq, 1)
    before = la < lb
    same_zd = (la // 8) % 8 == (lb // 8) % 8
    same_yd = (la // 2) % 4 == (lb // 2) % 4
    ra, rb = iota(rows, 0), iota(rows, 1)
    same_ys = ra % 4 == rb % 4
    same_zs = ra // 4 == rb // 4

    def f(x):
        return x.astype(F32)

    def count(mask, lanes, peers):
        rank = fdot(f(mask), f(before & lanes))
        total = fdot(f(mask), f(lanes))
        if peers is not None:
            rank = rank + fdot(f(peers & (rb < ra)), total)
            total = fdot(f(peers), total)
        return rank, total

    def halves(n_up, n_both, n_down):
        up = jnp.clip(jnp.floor((n_both + n_down - n_up + 1.0) * 0.5), 0.0, n_both)
        return up, n_both - up

    every = la >= 0
    over = jnp.full(shape, -1.0, F32)
    r1, n1 = count(live & (dz == 1), every, None)
    r2, n2 = count(live & (dz == 2), every, None)
    r6, n6 = count(live & (dz == 6), every, None)
    r7, n7 = count(live & (dz == 7), every, None)
    zpos = jnp.where(dz == 1, n2 + r1, jnp.where(dz == 2, r2, jnp.where(dz == 6, r6, n6 + r7)))
    over = jnp.maximum(over, jnp.maximum(n1 + n2, n7 + n6) - 2 * N1)
    over = jnp.maximum(over, jnp.maximum(n2, n6) - 2 * N2)

    def ring(mask, lanes, peers, near, distant):
        a1, m1 = count(mask & (dy == 1), lanes, peers)
        a2, m2 = count(mask & (dy == 2), lanes, peers)
        a3, m3 = count(mask & (dy == 3), lanes, peers)
        up, down = halves(m1, m2, m3)
        minus = (dy == 3) | ((dy == 2) & (a2 >= up))
        pos = jnp.where(dy == 1, up + a1, jnp.where(dy == 3, down + a3, jnp.where(a2 < up, a2, a2 - up)))
        excess = jnp.maximum(jnp.maximum(up + m1, down + m3) - near, jnp.maximum(up, down) - distant)
        return minus.astype(jnp.int32), pos.astype(jnp.int32), excess

    fy_way, fy_pos, excess = ring(live & far, every, None, 2 * FY1, 2 * FY2)
    over = jnp.maximum(over, excess)
    r3, n3 = count(live & (dz == 3), same_yd, same_zs)
    r4, n4 = count(live & (dz == 4), same_yd, same_zs)
    r5, n5 = count(live & (dz == 5), same_yd, same_zs)
    up, down = halves(n3, n4, n5)
    fz_pos = jnp.where(dz == 3, up + r3, jnp.where(dz == 5, down + r5, jnp.where(r4 < up, r4, r4 - up)))
    over = jnp.maximum(over, jnp.maximum(up + n3, down + n5) - 2 * FZ)
    over = jnp.maximum(over, jnp.maximum(up, down) - 2 * FZ4)
    z_way = ((dz > 4) | ((dz == 4) & (r4 >= up))).astype(jnp.int32)
    ny_way, ny_pos, excess = ring(near, same_zd, same_ys, 2 * NY1, 2 * NY2)
    over = jnp.maximum(over, excess)
    zpos, fz_pos = zpos.astype(jnp.int32), fz_pos.astype(jnp.int32)

    def at(kind, way, pos):
        return ((kind * 2 + way) * 2 + (pos % 2 != c)) * 16 + jnp.minimum(pos // 2, 15)

    def listed(mask, way, pos, code):
        key = jnp.where(mask & (pos % 2 == c) & (pos < 32), way * 16 + pos // 2, -1)
        acc = jnp.zeros(shape, jnp.int32)
        for r in range(32):
            acc = acc + jnp.where(key[r:r + 1, :] == row, code[r:r + 1, :] + 1, 0)
        column = jnp.sum(acc, axis=1, keepdims=True)
        return jnp.sum(jnp.where(lane == row, column, 0), axis=0, keepdims=True) - 1

    held = (BUF * 4 + (cs != c)) * 16 + tile
    if chip:
        here = live & (row == z * 4 + y)
        queued = listed(here & ~far & (dz > 0), z_way, zpos, held)
        return queued, listed(here & far & (dy > 0), fy_way, fy_pos, held)
    after_y = jnp.where(dy == 0, held, at(jnp.where(dy == 2, YF2, YF1), fy_way, fy_pos))
    turn_far = listed(live & far & (zs == z) & (yd == y), z_way, fz_pos, after_y)
    after_z = jnp.where(dz == 0, held, at(jnp.where(hops == 1, ZN1, ZN2), z_way, zpos))
    after_z = jnp.where(rooted, (ROOT * 4 + (cs != c)) * 16 + zs - 3, after_z)
    turn_near = listed(near & (zd == z) & (ys == y) & (dy > 0), ny_way, ny_pos, after_z)
    end_near = jnp.where(dy == 0, after_z, at(jnp.where(dy == 2, YN2, YN1), ny_way, ny_pos))
    end_far = at(jnp.where(dz == 4, ZF4, ZF3), z_way, fz_pos)
    keeper = jnp.where(far & ~rooted, fz_pos % 2, jnp.where(dy > 0, ny_pos % 2, cd))
    mine = used & (zd == z) & (yd == y) & (keeper == c)
    end = jnp.where(mine, (jnp.where(live & far, end_far, end_near) * 2 + (cd != c)) * 16 + slot, -1)
    return turn_near, turn_far, end, jnp.max(over, keepdims=True)


def plan_kernel(chip, where_ref, codes_ref, *out_refs):
    for ref, value in zip(out_refs, route(codes_ref[...], where_ref[0], where_ref[1], where_ref[2], chip)):
        ref[...] = value


def plan(chip, where, codes):
    shapes = [(1, 128)] * 2 if chip else [(1, 128), (1, 128), (32, 128), (1, 1)]
    return pl.pallas_call(
        lambda *refs: plan_kernel(chip, *refs),
        out_shape=tuple(jax.ShapeDtypeStruct(s, F32 if s == (1, 1) else jnp.int32) for s in shapes),
        in_specs=[SMEM, VMEM],
        out_specs=(VMEM,) * len(shapes),
        compiler_params=pltpu.CompilerParams(vmem_limit_bytes=6 << 20),
        name="plan_chip" if chip else "plan",
    )(where, codes)


def panel_kernel(place_ref, first_ref, inv0_ref, l10_ref, inv1_ref, front_ref, *refs):
    right0, right2, far00, far01, far10, far11, left00, left3, factor_ref, zero_ref, yh_ref, yl_ref = refs
    pieces = [
        right0.at[0], right0.at[1], right2.at[0], right2.at[1], far00, far01, far10, far11,
        left00, left3.at[0], left3.at[1], left3.at[2],
    ]
    place = place_ref[0]
    a0 = split3(inv0_ref[...])
    low = split(l10_ref[...])
    inv1 = inv1_ref[...]
    for q in range(4):
        for r in range(2):
            if q == 0:
                p0 = front_ref[0, r, 0, :, 0:T]
                p1 = front_ref[0, r, 0, :, T:2 * T].astype(F32)
            else:
                p0 = pieces[(q - 1) * 4 + r * 2][...].astype(BF16)
                p1 = pieces[(q - 1) * 4 + r * 2 + 1][...]
            y0 = dot1(p0, a0[0], NT) + (dot1(p0, a0[1], NT) + dot1(p0, a0[2], NT))
            y0h, y0l = split(y0)
            p1 = p1 - dot3((y0h, y0l), low, NT)
            y1 = dot(p1, inv1, NT)
            if r == 0:
                owner = lax.rem(place + q, 4)
                y1 = jnp.where(owner > 0, y1, 0.0)
            y1h, y1l = split(y1)
            n = q * 2 + r
            yh_ref[n, :, 0:T] = y0h
            yl_ref[n, :, 0:T] = y0l
            yh_ref[n, :, T:2 * T] = y1h
            yl_ref[n, :, T:2 * T] = y1l
            if q == 0:
                factor_ref[0, r, 0, :, 0:T] = y0
                factor_ref[0, r, 0, :, T:2 * T] = y1
    row = first_ref[0] // 7
    column = first_ref[0] % 7 + 1
    n = lax.rem(column % 4 - place + 4, 4) * 2 + column // 4
    start = pl.multiple_of(column * T, T)
    tile = front_ref[0, row, 0, :, pl.ds(start, T)].astype(F32)
    zero_ref[...] = tile - dot3((yh_ref[row], yl_ref[row]), (yh_ref[n], yl_ref[n]), NT)


def update_kernel(place_ref, front_ref, yh_ref, yl_ref, out_ref):
    place = place_ref[0]
    for r in range(2):
        for n in range(8):
            column = lax.rem(place + n // 2, 4) + 4 * (n % 2)

            @pl.when(column > 0)
            def _():
                start = pl.multiple_of(column * T, T)
                tile = front_ref[0, r, 0, :, pl.ds(start, T)].astype(F32)
                own = (yh_ref[r], yl_ref[r])
                other = (yh_ref[n], yl_ref[n])
                out_ref[r * 7 + column - 1] = tile - dot3(own, other, NT)


def arrays(kind, own, other=()):
    out = []
    for sib, xs in ((0, own), (1, other)):
        for way, x in enumerate(xs):
            out.append(((kind * 2 + way) * 2 + sib,) + (x if isinstance(x, tuple) else (0, x)))
    return out


def copy_from(sources, code, target_ref, sem):
    for sid, first, ref in sources:
        @pl.when(code // 16 == sid)
        def _():
            pltpu.make_async_copy(ref.at[jnp.minimum(first + code % 16, ref.shape[0] - 1)], target_ref, sem).start()


def operands(sources):
    xs, numbered = [], []
    for sid, first, x in sources:
        where = [i for i, other in enumerate(xs) if other is x]
        if not where:
            xs.append(x)
        numbered.append((sid, first, where[0] if where else len(xs) - 1))
    return numbered, xs


def gather_kernel(numbered, size, table_ref, *refs):
    sources = [(sid, first, refs[i]) for sid, first, i in numbered]
    *outs, sem = refs[-3:]
    for way, out in enumerate(outs):
        def start(i, _):
            code = table_ref[0, way * 16 + i]

            @pl.when(code >= 0)
            def _():
                copy_from(sources, code, out.at[i], sem.at[way * size + i])
            return 0

        lax.fori_loop(0, size, start, 0)
    for way, out in enumerate(outs):
        def wait(i, _):
            @pl.when(table_ref[0, way * 16 + i] >= 0)
            def _():
                pltpu.make_async_copy(refs[0].at[0], out.at[i], sem.at[way * size + i]).wait()
            return 0

        lax.fori_loop(0, size, wait, 0)


def gather(table, sources, size, name, *first):
    numbered, xs = operands(sources)
    xs = xs + list(first)
    return pl.pallas_call(
        lambda *refs: gather_kernel(numbered, size, *refs),
        out_shape=tiles(size, size),
        in_specs=[SMEM] + [ANY] * len(xs),
        out_specs=(VMEM,) * 2,
        scratch_shapes=[pltpu.SemaphoreType.DMA((2 * size,))],
        compiler_params=pltpu.CompilerParams(vmem_limit_bytes=10 << 20),
        cost_estimate=pl.CostEstimate(flops=0, bytes_accessed=8 << 20, transcendentals=0),
        name=name,
    )(table, *xs)


DEPTH = 12


def sum_kernel(numbered, other, where_ref, table_ref, *refs):
    *ins, out_ref, list_ref, buf_ref, sem = refs
    z, y = where_ref[0], where_ref[1]
    sources = [(sid, first, ins[i]) for sid, first, i in numbered]

    def collect(i, n):
        code = table_ref[i // 4, (i // 2 % 2) * 64 + z * 8 + y * 2 + i % 2]

        take = (code >= 0) & ((code // 16) % 2 == other)

        @pl.when(take)
        def _():
            list_ref[n] = code
        return n + take.astype(jnp.int32)

    n = lax.fori_loop(0, 128, collect, jnp.int32(0))

    def start(i):
        slot = lax.rem(i, DEPTH)
        copy_from(sources, list_ref[i] // 32, buf_ref.at[slot], sem.at[slot])

    def prime(i, _):
        start(i)
        return 0

    def step(i, _):
        slot = lax.rem(i, DEPTH)
        pltpu.make_async_copy(ins[0].at[0], buf_ref.at[slot], sem.at[slot]).wait()
        out_ref[list_ref[i] % 16] += buf_ref[slot]

        @pl.when(i + DEPTH < n)
        def _():
            start(i + DEPTH)
        return 0

    lax.fori_loop(0, jnp.minimum(n, DEPTH), prime, 0)
    out_ref[...] = jnp.zeros_like(out_ref)
    lax.fori_loop(0, n, step, 0)


def add_up(where, table, sources, other):
    numbered, xs = operands(sources)
    return pl.pallas_call(
        lambda *refs: sum_kernel(numbered, other, *refs),
        out_shape=tiles(ASLOT)[0],
        in_specs=[SMEM, SMEM] + [ANY] * len(xs),
        out_specs=VMEM,
        scratch_shapes=[pltpu.SMEM((256,), jnp.int32), pltpu.VMEM((DEPTH, T, T), F32), pltpu.SemaphoreType.DMA((DEPTH,))],
        compiler_params=pltpu.CompilerParams(vmem_limit_bytes=16 << 20),
        cost_estimate=pl.CostEstimate(flops=0, bytes_accessed=30 << 20, transcendentals=0),
        name="sum_other" if other else "sum_own",
    )(where, table, *xs)


def slots_kernel(tile_ref, own_ref, out_ref, sem):
    def start(p, _):
        tile = tile_ref[p]

        @pl.when(tile >= 0)
        def _():
            pltpu.make_async_copy(own_ref.at[tile], out_ref.at[p], sem.at[p]).start()
        return 0

    def wait(p, _):
        @pl.when(tile_ref[p] >= 0)
        def _():
            pltpu.make_async_copy(own_ref.at[0], out_ref.at[p], sem.at[p]).wait()
        return 0

    lax.fori_loop(0, 64, start, 0)
    lax.fori_loop(0, 64, wait, 0)


def add_kernel(target_ref, arrived_ref, out_ref):
    step = pl.program_id(0)

    @pl.when(step == 0)
    def _():
        out_ref[...] = jnp.zeros_like(out_ref)

    for i in range(4):
        target = target_ref[step * 4 + i]

        @pl.when(target >= 0)
        def _():
            out_ref[target] += arrived_ref[i]


def tiles(*counts):
    return tuple(jax.ShapeDtypeStruct((n, T, T), F32) for n in counts)


def leaf_id(z, y, c):
    return ((z % 8) * 4 + y % 4) * 2 + c


PLACES = [(z, y, c) for z in range(8) for y in range(4) for c in range(2)]


def send(x, pairs):
    return lax.ppermute(x, "leaf", [(leaf_id(*a), leaf_id(*b)) for a, b in pairs])


def dense(work, tile, slot):
    outgoing = pl.pallas_call(
        slots_kernel,
        out_shape=tiles(64)[0],
        in_specs=[SMEM, ANY],
        out_specs=ANY,
        scratch_shapes=[pltpu.SemaphoreType.DMA((64,))],
        name="slots",
    )(tile, work)
    arrived = lax.all_to_all(outgoing, "leaf", split_axis=0, concat_axis=0, tiled=True)
    targets = lax.all_to_all(slot, "leaf", split_axis=0, concat_axis=0, tiled=True)
    return pl.pallas_call(
        add_kernel,
        out_shape=tiles(ASLOT)[0],
        grid=(16,),
        in_specs=[SMEM, pl.BlockSpec((4, T, T), lambda i: (i, 0, 0))],
        out_specs=pl.BlockSpec((ASLOT, T, T), lambda i: (0, 0, 0)),
        compiler_params=pltpu.CompilerParams(vmem_limit_bytes=32 << 20),
        name="add",
    )(targets, arrived)


def tie(x, *others):
    return lax.optimization_barrier((x,) + others)[0]


def sparse(work, root, code, where, queued, queued_far):
    swap = [((z, y, c), (z, y, 1 - c)) for z, y, c in PLACES]
    along_z = [[((z, y, c), (z + s, y, c)) for z, y, c in PLACES] for s in (1, -1)]
    along_y = [[((z, y, c), (z, y + s, c)) for z, y, c in PLACES] for s in (1, -1)]

    def sends(xs, ways):
        return [send(x, way) for x, way in zip(xs, ways)]

    def swaps(xs):
        return [send(x, swap) for x in xs]

    def after(xs, *others):
        return list(lax.optimization_barrier(tuple(xs) + others)[:len(xs)])

    other = send(work, swap)
    everyone = jnp.broadcast_to(after([code], work)[0], (64, 64))
    codes = lax.all_to_all(everyone, "leaf", split_axis=0, concat_axis=0, tiled=True).reshape(32, 128)
    queued = after([queued], codes, *root)[0]
    both = arrays(BUF, [work], [other])
    near_list = gather(queued, both, N1, "queue")
    n1 = sends(near_list, along_z)
    far_list = gather(tie(queued_far, *near_list), both, FY1, "queue_far")
    f1 = sends(far_list, along_y)
    f2 = sends([x[:FY2] for x in f1], along_y)
    turn_near, turn_far, end, over = plan(False, where, codes)
    n2 = sends(after([x[:N2] for x in n1], *f1), along_z)
    mixed = send(after([jnp.concatenate([*f1, *f2])], *n1)[0], swap)
    parts = [(cut, mixed) for cut in (0, FY1, 2 * FY1, 2 * FY1 + FY2)]
    column = jnp.stack(root)
    column_other = send(after([column], *n1)[0], swap)
    far_list = gather(turn_far, both + arrays(YF1, f1, parts[0:2]) + arrays(YF2, f2, parts[2:4]), FZ, "turn_far", column_other)
    n1_other = swaps(after(n1, *far_list))
    z1 = sends(after(far_list, *n2, *n1_other), along_z)
    near_sources = both + arrays(ZN1, n1, n1_other) + arrays(ZN2, n2, swaps(n2)) + arrays(ROOT, [column], [column_other])
    near_list = gather(turn_near, near_sources, NY1, "turn_near")
    z2 = sends(after(z1, *near_list), along_z)
    y1 = sends(near_list, along_y)
    z3 = sends(z2, along_z)
    y2 = sends(after([x[:NY2] for x in y1], *z2), along_y)
    z4 = sends(after([x[:FZ4] for x in z3], *y1), along_z)
    sources = near_sources + arrays(YN1, y1) + arrays(YN2, y2) + arrays(ZF3, z3) + arrays(ZF4, z4)
    theirs = add_up(where, end, sources, 1)
    own = add_up(tie(where, theirs), end, sources, 0)
    return over, own, send(theirs, swap)


def local(front, pivot_tiles, send_table):
    place = lax.axis_index("front").astype(jnp.int32)
    leaf = lax.axis_index("leaf").astype(jnp.int32)
    where = jnp.stack([leaf // 8, (leaf // 2) % 4, leaf % 2])
    table = send_table[0, 0]
    used = table[0] >= 0
    tile = jnp.where(used, table[0] * 7 + table[1] - 1, -1)
    code = jnp.where(used, tile * 16 + table[2], -1)
    up = [(i, (i + 1) % 4) for i in range(4)]
    down = [(i, (i - 1) % 4) for i in range(4)]
    own = [[front[0, r, 0, :, k * T:k * T + T].astype(F32) for k in range(2)] for r in range(2)]
    def across(x, shift, *others):
        return lax.ppermute(tie(x, *others) if others else x, "front", [(i, (i + shift) % 4) for i in range(4)])

    left00 = across(own[0][0], 1)
    right0 = across(jnp.stack(own[0]), -1)
    far00 = across(left00, 1)
    far01 = across(right0[1], -1)
    left3 = across(jnp.stack([own[0][1], own[1][0], own[1][1]]), 1, far00, far01)
    right2 = across(jnp.stack(own[1]), -1, far00, far01)
    far10 = across(left3[1], 1)
    far11 = across(right2[1], -1)
    from_left = [[left00, left3[0]], [left3[1], left3[2]]]
    from_right = [[right0[0], right0[1]], [right2[0], right2[1]]]
    from_far = [[far00, far01], [far10, far11]]
    by_q = [own, from_right, from_far, from_left]

    def of_owner(owner, r, k, *after):
        q = lax.rem(owner - place + 4, 4)
        if after:
            q = tie(q, *after)
        out = by_q[0][r][k]
        for i in range(1, 4):
            out = jnp.where(q == i, by_q[i][r][k], out)
        return out

    inv0 = pl.pallas_call(
        first_kernel,
        out_shape=jax.ShapeDtypeStruct((T, T), F32),
        in_specs=[VMEM],
        out_specs=VMEM,
        scratch_shapes=[pltpu.VMEM((B, 128), F32)],
        compiler_params=pltpu.CompilerParams(vmem_limit_bytes=8 << 20),
        cost_estimate=pl.CostEstimate(flops=0, bytes_accessed=20 << 20, transcendentals=0),
        name="first",
    )(of_owner(0, 0, 0))
    w10 = of_owner(1, 0, 0, inv0)
    w11 = of_owner(1, 0, 1, inv0)
    l10, inv1 = pl.pallas_call(
        second_kernel,
        out_shape=(jax.ShapeDtypeStruct((T, T), F32),) * 2,
        in_specs=[SMEM, VMEM, VMEM, VMEM],
        out_specs=(VMEM, VMEM),
        scratch_shapes=[pltpu.VMEM((B, 128), F32)],
        compiler_params=pltpu.CompilerParams(vmem_limit_bytes=16 << 20),
        cost_estimate=pl.CostEstimate(flops=0, bytes_accessed=40 << 20, transcendentals=0),
        name="second",
    )(pivot_tiles, inv0, w10, w11)

    pair = send(code, [((z, y, c), (z, y, 1 - c)) for z, y, c in PLACES])
    pair = jnp.where(where[2] == 0, jnp.concatenate([code, pair]), jnp.concatenate([pair, code]))
    chip = jnp.where(iota((32, 128), 0) == where[0] * 4 + where[1], pair[None, :], -1)
    queued, queued_far = plan(True, where, chip)
    received = [right0, right2, far00, far01, far10, far11, left00, left3]
    factor, zero, yh, yl = pl.pallas_call(
        panel_kernel,
        out_shape=(jax.ShapeDtypeStruct((1, 2, 1, T, 2 * T), F32), jax.ShapeDtypeStruct((T, T), F32))
        + (jax.ShapeDtypeStruct((8, T, 2 * T), BF16),) * 2,
        in_specs=[SMEM, SMEM] + [VMEM] * 12,
        out_specs=(VMEM,) * 4,
        compiler_params=pltpu.CompilerParams(vmem_limit_bytes=18 << 20),
        name="panel",
    )(place.reshape(1), jnp.maximum(tile[0:1], 0), inv0, l10, inv1, front, *received)
    root = [send(zero, [((z, y, c), (0, y, c)) for y in range(4) for c in range(2)]) for z in (3, 4, 5)]
    work = pl.pallas_call(
        update_kernel,
        out_shape=tiles(TILES)[0],
        in_specs=[SMEM] + [VMEM] * 3,
        out_specs=VMEM,
        compiler_params=pltpu.CompilerParams(vmem_limit_bytes=14 << 20),
        name="update",
    )(place.reshape(1), front, yh, yl)
    over, own, theirs = sparse(work, root, code, where, queued, queued_far)
    _, ancestor = lax.while_loop(
        lambda state: state[0],
        lambda state: (False, dense(work, tile, table[2])),
        (over[0, 0] > 0.0, own + theirs),
    )
    return (factor, ancestor.reshape(1, 1, ASLOT, T, T))


def solution(mesh):
    in_specs = (P("leaf", None, "front", None, None), P("leaf"), P("leaf", "front", None, None))
    out_specs = (P("leaf", None, "front", None, None), P("leaf", "front", None, None, None))
    return jax.shard_map(local, mesh=mesh, in_specs=in_specs, out_specs=out_specs, check_vma=False)
```
